128 devices in a mesh: kv: 4 (over x_lo, core), grp: 8 (over x_hi, z), prompt: 4 (over y).
Axes of the slice: x: 4 (x_hi: 2, x_lo: 2; x = x_hi * 2 + x_lo), y: 4, z: 4, core: 2. Of those that a mesh axis runs over, the one named last changes fastest.
Arguments:
- queries: bfloat16 [4, 8, 256, 8192], P('prompt', 'grp', None, 'kv'), may hold values from -6 to 6
- resp_keys: bfloat16 [4, 8, 256, 1024], P('prompt', 'grp', None, 'kv'), may hold values from -6 to 6
- resp_values: bfloat16 [4, 8, 256, 1024], P('prompt', 'grp', None, 'kv'), may hold values from -6 to 6
- prompt_keys: bfloat16 [4, 2048, 1024], P('prompt', ('kv', 'grp')), may hold values from -6 to 6
- prompt_values: bfloat16 [4, 2048, 1024], P('prompt', ('kv', 'grp')), may hold values from -6 to 6
- grad_out: bfloat16 [4, 8, 256, 8192], P('prompt', 'grp', None, 'kv'), may hold values from -6 to 6
- resp_len: int32 [4, 8], P('prompt', 'grp'), may hold values from 32 to 255, as said below
- prompt_len: int32 [4], P('prompt'), may hold values from 512 to 2048, as said below
Outputs:
- attended: bfloat16 [4, 8, 256, 8192], P('prompt', 'grp', None, 'kv')
- grad_queries: bfloat16 [4, 8, 256, 8192], P('prompt', 'grp', None, 'kv')
- grad_resp_keys: bfloat16 [4, 8, 256, 1024], P('prompt', 'grp', None, 'kv')
- grad_resp_values: bfloat16 [4, 8, 256, 1024], P('prompt', 'grp', None, 'kv')
- grad_prompt_keys: float32 [4, 2048, 1024], P('prompt', ('kv', 'grp'))
- grad_prompt_values: float32 [4, 2048, 1024], P('prompt', ('kv', 'grp'))
The draws below stay inside these ranges and needn't reach their ends.
Inputs may be any that keep to these rules, and one draw needn't show every extreme that they name: `resp_len`: some response has exactly 255 valid tokens in every draw. `prompt_len`: some prompt has exactly 2048 valid tokens in every draw.
All inputs are finite; a program needn't handle non-finite values.
Results may differ from the reference program's by a relative error of at most 0.034.
Values may be sent and summed in bfloat16 or wider, within the bound.
A program may use at most 128 MiB of HBM per device.

```python
import jax
import jax.numpy as jnp
from jax import lax

HD = 128
KVH = 8
QH = 64
QPG = 8
SLICE = 256
PLEN = 2048
RESP = 8
PROMPTS = 4
ALL_SLOTS = 8192


def draw_queries(key, part):
    key = jax.random.fold_in(key, 1)
    values = jnp.clip(jax.random.normal(key, (PROMPTS, RESP, SLICE, QH, HD), jnp.float32), -6.0, 6.0)
    return values.reshape(PROMPTS, RESP, SLICE, QH * HD).astype(jnp.bfloat16)


def draw_prompt_keys(key, part):
    key = jax.random.fold_in(key, 2)
    values = jnp.clip(jax.random.normal(key, (PROMPTS, PLEN, KVH, HD), jnp.float32), -6.0, 6.0)
    return values.reshape(PROMPTS, PLEN, KVH * HD).astype(jnp.bfloat16)


def draw_resp_len(key, part):
    key = jax.random.fold_in(key, 3)
    lengths = jax.random.randint(jax.random.fold_in(key, 1), (PROMPTS * RESP,), SLICE // 8, SLICE)
    chosen = jax.random.randint(jax.random.fold_in(key, 2), (), 0, PROMPTS * RESP)
    lengths = jnp.where(jnp.arange(PROMPTS * RESP) == chosen, SLICE - 1, lengths)
    return lengths.reshape(PROMPTS, RESP).astype(jnp.int32)


def draw_prompt_len(key, part):
    key = jax.random.fold_in(key, 4)
    lengths = jax.random.randint(jax.random.fold_in(key, 1), (PROMPTS,), PLEN // 4, PLEN + 1)
    chosen = jax.random.randint(jax.random.fold_in(key, 2), (), 0, PROMPTS)
    lengths = jnp.where(jnp.arange(PROMPTS) == chosen, PLEN, lengths)
    return lengths.astype(jnp.int32)


def block_levels(own_key, dims, split, least, high):
    loudness = 1.0
    for axis_at, blocks in split:
        heights = jax.random.uniform(jax.random.fold_in(jax.random.fold_in(own_key, 6), axis_at), (blocks,), jnp.float32, least / len(split), high / len(split))
        loudness = loudness * jnp.repeat(jnp.exp(heights), dims[axis_at] // blocks).reshape((-1,) + (1,) * (len(dims) - 1 - axis_at))
    return loudness


def scatter_about(key, shape, scale, most, pieces=(), dtype=jnp.bfloat16):
    drawn = scale * jax.random.normal(key, shape, jnp.float32)
    if pieces:
        drawn = drawn * block_levels(key, shape, pieces, -0.22, 0.18)
    return jnp.clip(drawn, -most, most).astype(dtype)


def setup_inputs(seed: int = 0) -> dict:
    seeds = jax.random.split(jax.random.key(seed), 9)
    return {
        "queries": draw_queries(jax.random.fold_in(seeds[8], 71), 0),
        "resp_keys": scatter_about(seeds[1], (PROMPTS, RESP, SLICE, KVH * HD), 1.0, 6.0, ((0, 4), (1, 8), (3, 4))),
        "resp_values": scatter_about(seeds[2], (PROMPTS, RESP, SLICE, KVH * HD), 1.0, 6.0, ((0, 4), (1, 8), (3, 4))),
        "prompt_keys": draw_prompt_keys(jax.random.fold_in(seeds[8], 71), 0),
        "prompt_values": scatter_about(seeds[4], (PROMPTS, PLEN, KVH * HD), 1.0, 6.0, ((0, 4), (1, 32))),
        "grad_out": scatter_about(seeds[5], (PROMPTS, RESP, SLICE, QH * HD), 1.0, 6.0, ((0, 4), (1, 8), (3, 4))),
        "resp_len": draw_resp_len(jax.random.fold_in(seeds[8], 71), 0),
        "prompt_len": draw_prompt_len(jax.random.fold_in(seeds[8], 71), 0),
    }


def round_half(values):
    return lax.optimization_barrier(values.astype(jnp.bfloat16)).astype(jnp.float32)


def one_response(query_rows, key_rows, value_rows, cotangent_rows, resp_length, prompt_key_rows, prompt_value_rows, prompt_length, weight):
    scale = HD ** -0.5
    key_count = PLEN + SLICE
    query_all = query_rows.astype(jnp.float32).reshape(SLICE, KVH, QPG, HD)
    key_all = jnp.concatenate([prompt_key_rows, key_rows], 0).astype(jnp.float32).reshape(key_count, KVH, HD)
    value_all = jnp.concatenate([prompt_value_rows, value_rows], 0).astype(jnp.float32).reshape(key_count, KVH, HD)
    positions = jnp.arange(key_count)[None, :]
    query_pos = jnp.arange(SLICE)[:, None]
    offsets = positions - PLEN
    visible = jnp.where(positions < PLEN, positions < prompt_length, (offsets <= query_pos) & (offsets < resp_length))
    scores = jnp.einsum('ikgd,jkd->kgij', query_all, key_all) * scale
    masked = jnp.where(visible, scores, -jnp.inf)
    highest = jnp.max(masked, -1, keepdims=True)
    log_total = highest + jnp.log(jnp.sum(jnp.exp(masked - highest), -1, keepdims=True))
    probs = round_half(jnp.exp(jnp.where(visible, scores - log_total, -jnp.inf)))
    attended = jnp.einsum('kgij,jkd->ikgd', probs, value_all).astype(jnp.bfloat16)
    live_rows = (jnp.arange(SLICE) < resp_length).astype(jnp.float32)
    scaled = round_half(cotangent_rows.astype(jnp.float32).reshape(SLICE, KVH, QPG, HD) * live_rows[:, None, None, None] * weight)
    delta = jnp.sum(scaled * attended.astype(jnp.float32), -1).transpose(1, 2, 0)[..., None]
    grad_probs = jnp.einsum('ikgd,jkd->kgij', scaled, value_all)
    grad_scores = round_half(probs * (grad_probs - delta) * scale)
    grad_query = jnp.einsum('kgij,jkd->ikgd', grad_scores, key_all).astype(jnp.bfloat16).reshape(SLICE, QH * HD)
    grad_key = jnp.einsum('kgij,ikgd->jkd', grad_scores, query_all).reshape(key_count, KVH * HD)
    grad_value = jnp.einsum('kgij,ikgd->jkd', probs, scaled).reshape(key_count, KVH * HD)
    return (attended.reshape(SLICE, QH * HD), grad_query, grad_key[PLEN:].astype(jnp.bfloat16),
            grad_value[PLEN:].astype(jnp.bfloat16), grad_key[:PLEN], grad_value[:PLEN])


def reference(queries, resp_keys, resp_values, prompt_keys, prompt_values, grad_out, resp_len, prompt_len):
    weight = jnp.float32(ALL_SLOTS) / jnp.sum(resp_len).astype(jnp.float32)

    def per_prompt(items):
        query_block, key_block, value_block, cotangent_block, length_block, prompt_key_rows, prompt_value_rows, prompt_length = items

        def per_response(carry, inner):
            query_rows, key_rows, value_rows, cotangent_rows, resp_length = inner
            results = one_response(query_rows, key_rows, value_rows, cotangent_rows, resp_length,
                                   prompt_key_rows, prompt_value_rows, prompt_length, weight)
            return (carry[0] + results[4], carry[1] + results[5]), results[:4]

        zero_grads = jnp.zeros((PLEN, KVH * HD), jnp.float32)
        (key_sum, value_sum), stacked = lax.scan(per_response, (zero_grads, zero_grads),
                                                 (query_block, key_block, value_block, cotangent_block, length_block))
        return stacked[0], stacked[1], stacked[2], stacked[3], key_sum, value_sum

    results = lax.map(per_prompt, (queries, resp_keys, resp_values, grad_out, resp_len, prompt_keys, prompt_values, prompt_len))
    return (results[0], results[1], results[2], results[3], results[4], results[5])
```

```python
import functools

import jax
import jax.numpy as jnp
from jax import lax
from jax.experimental import pallas as pl
from jax.experimental.pallas import tpu as pltpu
from jax.sharding import PartitionSpec as P

F32 = jnp.float32
BF = jnp.bfloat16
MESH = pl.DeviceIdType.MESH
HD = 128
QPG = 8
SCALE = HD ** (-0.5)
LOG2E = 1.4426950408889634
NT = (((1,), (1,)), ((), ()))
NN = (((1,), (0,)), ((), ()))
SET = 256
PC = 512
HEADS = 16
SLOTS = 256
SETS = ((0, 0), (0, 3), (0, 1), (1, 0), (1, 1), (1, 3), (0, 2), (1, 2))


def dot(a, b, dims):
    return lax.dot_general(a, b, dims, preferred_element_type=F32)


def cat(parts, axis):
    return parts[0] if len(parts) == 1 else jnp.concatenate(parts, axis)


def kernel(
    rl_ref, pl_ref, q_ref, do_ref, rk_ref, rv_ref, pk_ref, pv_ref,
    o_ref, dq_ref, drk_ref, drv_ref, dpk_ref, dpv_ref,
    sets, p_ref, o_acc, dq_acc, mc, lse, ka, va, k_t, v_t, qq, dd, s_a, s_b,
    dk_acc, dv_acc, out_buf, half_in, full_in, x_in, fin, w_own, w_in,
    a2a_s, a2a_r, gs, gr, hs, hr, fs, fr, xs, xr, ks, kr, ws, wr,
):
    kv = lax.axis_index("kv")
    grp = lax.axis_index("grp")
    prm = lax.axis_index("prompt")
    xh = grp // 4
    z = grp % 4
    zat = lambda d: {"grp": xh * 4 + (z + d) % 4}
    zp, zm, xp = zat(1), zat(3), {"grp": (1 - xh) * 4 + z}
    kvat = lambda d: (kv + d) % 4
    yat = lambda d: {"prompt": (prm + d) % 4}

    peers = [{"kv": kvat(d)} for d in (1, 2, 3)] + [zat(d) for d in (1, 2, 3)]
    peers += [yat(d) for d in (1, 2, 3)] + [xp]
    barrier = pltpu.get_barrier_semaphore()
    for peer in peers:
        pl.semaphore_signal(barrier, inc=1, device_id=peer, device_id_type=MESH)
    pl.semaphore_wait(barrier, len(peers))

    def cp(src, dst, ssem, rsem, dev):
        return pltpu.make_async_remote_copy(
            src_ref=src, dst_ref=dst, send_sem=ssem, recv_sem=rsem, device_id=dev, device_id_type=MESH
        )

    spread = []
    for d in (1, 2, 3):
        cols = pl.ds(pl.multiple_of(kvat(d) * 256, 256), 256)
        rows = pl.ds(pl.multiple_of(kv * 64, 64), 64)
        for t, ref in ((0, pk_ref), (1, pv_ref)):
            i = (d - 1) * 2 + t
            spread.append(cp(ref.at[:, cols], sets.at[0, t, rows, :], a2a_s.at[i], a2a_r.at[i], {"kv": kvat(d)}))
    lo, hi = pl.ds(0, 128), pl.ds(128, 128)
    to_x = cp(sets.at[0], sets.at[3], gs.at[0], gr.at[0], xp)
    to_p = cp(sets.at[0], sets.at[1], gs.at[1], gr.at[1], zp)
    to_m = cp(sets.at[0], sets.at[2], gs.at[2], gr.at[2], zm)
    on_p = cp(sets.at[1, :, lo], sets.at[6, :, lo], gs.at[3], gr.at[3], zp)
    on_m = cp(sets.at[2, :, hi], sets.at[6, :, hi], gs.at[4], gr.at[4], zm)
    xto_p = cp(sets.at[3], sets.at[5], gs.at[5], gr.at[5], zp)
    xto_m = cp(sets.at[3], sets.at[4], gs.at[6], gr.at[6], zm)
    xon_p = cp(sets.at[5, :, lo], sets.at[7, :, lo], gs.at[7], gr.at[7], zp)
    xon_m = cp(sets.at[4, :, hi], sets.at[7, :, hi], gs.at[8], gr.at[8], zm)
    gather = [to_x, to_p, to_m, on_p, on_m, xto_p, xto_m, xon_p, xon_m]
    w_x = cp(w_own.at[0], w_in.at[0], ws.at[0], wr.at[0], xp)
    w_z = [cp(w_own.at[1], w_in.at[d], ws.at[d], wr.at[d], zat(d)) for d in (1, 2, 3)]
    w_y = [cp(w_own.at[2], w_in.at[3 + d], ws.at[3 + d], wr.at[3 + d], yat(d)) for d in (1, 2, 3)]
    half = {}
    full = {}
    for dx, s in ((0, 6), (1, 7)):
        half[dx, 0] = cp(out_buf.at[s, :, lo], half_in.at[dx, 0], hs.at[dx * 2], hr.at[dx * 2], zp)
        half[dx, 1] = cp(out_buf.at[s, :, hi], half_in.at[dx, 1], hs.at[dx * 2 + 1], hr.at[dx * 2 + 1], zm)
    for dx, d, s in ((0, 0, 2), (0, 1, 1), (1, 0, 4), (1, 1, 5)):
        i = dx * 2 + d
        full[dx, d] = cp(out_buf.at[s], full_in.at[dx, d], fs.at[i], fr.at[i], zm if d else zp)
    sum_x = cp(out_buf.at[3], x_in, xs, xr, xp)
    owners = []
    for d in (1, 2, 3):
        rows = pl.ds(pl.multiple_of(kvat(d) * 64, 64), 64)
        owners.append(cp(out_buf.at[0, :, rows, :], fin.at[d], ks.at[d], kr.at[d], {"kv": kvat(d)}))

    for c in spread:
        c.start()
    w_own[0] = jnp.full((8, 128), rl_ref[0, 0].astype(F32))
    w_x.start()

    rows = pl.ds(pl.multiple_of(kv * 64, 64), 64)
    cols = pl.ds(pl.multiple_of(kv * 256, 256), 256)
    sets[0, 0, rows, :] = pk_ref[:, cols]
    sets[0, 1, rows, :] = pv_ref[:, cols]

    live = lax.broadcasted_iota(jnp.int32, (SLOTS, HD), 0) < rl_ref[0, 0]

    def stage_queries(h, _):
        col = pl.ds(pl.multiple_of(h * HD, HD), HD)
        q = q_ref[:, col]
        qq[h, :, 0:HD] = q
        qq[h, :, HD:] = q
        dd[h, :, 0:HD] = jnp.where(live, do_ref[:, col].astype(F32), 0.0).astype(BF)
        return 0

    lax.fori_loop(0, HEADS, stage_queries, 0)
    ones = jnp.where(lax.broadcasted_iota(jnp.int32, (2304, HD), 1) < 2, 1.0, 0.0).astype(BF)
    for kh in range(2):
        va[kh, :, HD:] = ones

    def put_keys(kh, at, k, k_masked, v, valid):
        scaled = k * (SCALE * LOG2E)
        high = scaled.astype(BF)
        ka[kh, pl.ds(at, SET), 0:HD] = high
        ka[kh, pl.ds(at, SET), HD:] = (scaled - high.astype(F32)).astype(BF)
        va[kh, pl.ds(at, SET), 0:HD] = v.astype(BF)
        k_t[kh, :, pl.ds(at, SET)] = k_masked.T.astype(BF)
        v_t[kh, 0:HD, pl.ds(at, SET)] = v.T.astype(BF)
        v_t[kh, HD:, pl.ds(at, SET)] = valid

    for kh in range(2):
        k = rk_ref[:, kh * HD:(kh + 1) * HD].astype(F32)
        v = rv_ref[:, kh * HD:(kh + 1) * HD].astype(F32)
        put_keys(kh, 2048, k, k, v, jnp.ones((16, SET), BF))

    plen = pl_ref[0]

    def key_index(s, shape, axis):
        dx, dz = SETS[s]
        owner = (xh if dx == 0 else 1 - xh) * 4 + (z + dz) % 4
        r = lax.broadcasted_iota(jnp.int32, shape, axis)
        return ((r // 64) * 8 + owner) * 64 + r % 64

    def put_set(s):
        dead = key_index(s, (SET, HD), 0) >= plen
        valid = jnp.where(key_index(s, (16, SET), 1) < plen, 1.0, 0.0).astype(BF)
        for kh in range(2):
            k = sets[s, 0, :, kh * HD:(kh + 1) * HD].astype(F32)
            v = sets[s, 1, :, kh * HD:(kh + 1) * HD].astype(F32)
            put_keys(kh, s * SET, jnp.where(dead, k[0:1, :], k), jnp.where(dead, 0.0, k),
                     jnp.where(dead, 0.0, v), valid)

    def fwd_resp(h, _):
        kh = h // QPG
        s = dot(ka[kh, 2048:2304, :], qq[h], NT)
        t = lax.broadcasted_iota(jnp.int32, (SET, SLOTS), 0)
        i = lax.broadcasted_iota(jnp.int32, (SET, SLOTS), 1)
        s = jnp.where((t <= i) & (t < rl_ref[0, 0]), s, -1e30)
        m = jnp.max(s, 0, keepdims=True)
        p = jnp.exp2(s - m).astype(BF)
        mc[0, h] = m
        p_ref[h, 2048:2304, :] = p
        o_acc[h] = dot(v_t[kh, :, 2048:2304], p, NN)
        return 0

    for c in spread:
        c.wait_recv()
    for c in (to_x, to_p, to_m):
        c.start()
    lax.fori_loop(0, HEADS, fwd_resp, 0)
    w_x.wait_recv()
    w_own[1] = w_own[0] + w_in[0]
    for c in w_z:
        c.start()
    put_set(0)

    def score(c, at, h, s_ref):
        kh = h // QPG
        top = None
        for r in range(0, PC, 256):
            s = dot(ka[kh, pl.ds(at + r, 256), :], qq[h], NT)
            s_ref[r:r + 256, :] = s
            b = jnp.max(s.reshape(32, 8, SLOTS), 0)
            top = b if top is None else jnp.maximum(top, b)
        mc[c + 1, h] = jnp.maximum(mc[c, h], jnp.max(top, 0, keepdims=True))

    def attend(c, at, h, s_ref):
        kh = h // QPG
        m = mc[c + 1, h]
        old = o_acc[h] * jnp.exp2(mc[c, h] - m)
        parts = []
        for r in range(0, PC, 256):
            p = jnp.exp2(s_ref[r:r + 256, :] - m).astype(BF)
            p_ref[h, pl.ds(at + r, 256), :] = p
            parts.append(p)
        o_acc[h] = old + dot(v_t[kh, :, pl.ds(at, PC)], cat(parts, 0), NN)

    def fwd_chunk(c, _):
        @pl.when(c == 0)
        def _():
            to_p.wait_recv()
            on_p.start()
            to_m.wait_recv()
            on_m.start()
            put_set(1)

        @pl.when(c == 1)
        def _():
            to_x.wait_recv()
            xto_p.start()
            xto_m.start()
            put_set(2)
            put_set(3)
            for w in w_z:
                w.wait_recv()
            w_own[2] = w_own[1] + (w_in[1] + w_in[2] + w_in[3])
            for w in w_y:
                w.start()

        @pl.when(c == 2)
        def _():
            xto_p.wait_recv()
            xon_p.start()
            xto_m.wait_recv()
            xon_m.start()
            put_set(4)
            put_set(5)

        @pl.when(c == 3)
        def _():
            on_p.wait_recv()
            on_m.wait_recv()
            put_set(6)
            xon_p.wait_recv()
            xon_m.wait_recv()
            put_set(7)

        at = pl.multiple_of(c * PC, PC)
        score(c, at, 0, s_a)

        def heads(i, _):
            score(c, at, 2 * i + 1, s_b)
            attend(c, at, 2 * i, s_a)
            score(c, at, jnp.minimum(2 * i + 2, HEADS - 1), s_a)
            attend(c, at, 2 * i + 1, s_b)
            return 0

        lax.fori_loop(0, HEADS // 2, heads, 0)
        return 0

    lax.fori_loop(0, 4, fwd_chunk, 0)

    lane = lax.broadcasted_iota(jnp.int32, (SLOTS, HD), 1)

    def finish_fwd(h, _):
        col = pl.ds(pl.multiple_of(h * HD, HD), HD)
        o = o_acc[h]
        total = o[HD:HD + 1, :]
        out = (o[0:HD, :] * (1.0 / total)).T.astype(BF)
        o_ref[:, col] = out
        delta = -jnp.sum(out.astype(F32) * dd[h, :, 0:HD].astype(F32), 1, keepdims=True)
        high = delta.astype(BF).astype(F32)
        dd[h, :, HD:] = jnp.where(lane == 0, high, jnp.where(lane == 1, delta - high, 0.0)).astype(BF)
        lse[h] = mc[4, h] + jnp.log2(total)
        dq_acc[h] = jnp.zeros((HD, SLOTS), F32)
        return 0

    lax.fori_loop(0, HEADS, finish_fwd, 0)
    for w in w_y:
        w.wait_recv()
    count = w_own[2] + (w_in[4] + w_in[5] + w_in[6])
    weight = (8192.0 / count)[0:1, :]

    UB = 4

    def bwd_part(c, at, rows, kh):
        sub = min(256, rows)
        cols = slice(kh * HD, (kh + 1) * HD)
        dk_acc[0:rows, cols] = jnp.zeros((rows, HD), F32)
        dv_acc[0:rows, cols] = jnp.zeros((rows, HD), F32)

        def heads(i, _):
            ps, ss, dos, qs = [], [], [], []
            for u in range(UB):
                h = kh * QPG + i * UB + u
                corr = jnp.exp2(mc[c, h] - lse[h])
                pp, sp = [], []
                for r in range(0, rows, sub):
                    dp = dot(va[kh, pl.ds(at + r, sub), :], dd[h], NT)
                    p = p_ref[h, pl.ds(at + r, sub), :].astype(F32) * corr
                    pp.append(p.astype(BF))
                    sp.append((p * dp).astype(BF))
                ds = cat(sp, 0)
                dq_acc[h] += dot(k_t[kh, :, pl.ds(at, rows)], ds, NN)
                ps.append(cat(pp, 0))
                ss.append(ds)
                dos.append(dd[h, :, 0:HD])
                qs.append(qq[h, :, 0:HD])
            dv_acc[0:rows, cols] += dot(cat(ps, 1), cat(dos, 0), NN)
            dk_acc[0:rows, cols] += dot(cat(ss, 1), cat(qs, 0), NN)
            return 0

        lax.fori_loop(0, QPG // UB, heads, 0)

    def acc_of(s):
        r = (s % 2) * SET
        return dk_acc[r:r + SET, :], dv_acc[r:r + SET, :]

    def bwd_chunk(i, _):
        c = 3 - i
        at = pl.multiple_of(c * PC, PC)
        for kh in range(2):
            bwd_part(c + 1, at, PC, kh)

        @pl.when(c == 3)
        def _():
            for dx, s in ((1, 7), (0, 6)):
                for t, a in enumerate(acc_of(s)):
                    out_buf[s, t] = a.astype(BF)
                half[dx, 0].start()
                half[dx, 1].start()

        @pl.when(c == 2)
        def _():
            for d, s in ((0, 4), (1, 5)):
                half[1, d].wait_recv()
                for t, a in enumerate(acc_of(s)):
                    part = half_in[1, d, t].astype(F32)
                    out_buf[s, t, d * 128:d * 128 + 128, :] = (a[d * 128:d * 128 + 128] + part).astype(BF)
                    e = 1 - d
                    out_buf[s, t, e * 128:e * 128 + 128, :] = a[e * 128:e * 128 + 128].astype(BF)
                full[1, d].start()

        @pl.when(c == 1)
        def _():
            half[0, 0].wait_recv()
            for t, a in enumerate(acc_of(2)):
                out_buf[2, t, 0:128, :] = (a[0:128] + half_in[0, 0, t].astype(F32)).astype(BF)
                out_buf[2, t, 128:256, :] = a[128:256].astype(BF)
            full[0, 0].start()
            full[1, 0].wait_recv()
            full[1, 1].wait_recv()
            for t, a in enumerate(acc_of(3)):
                out_buf[3, t] = (a + full_in[1, 0, t].astype(F32) + full_in[1, 1, t].astype(F32)).astype(BF)
            sum_x.start()

        @pl.when(c == 0)
        def _():
            half[0, 1].wait_recv()
            for t, a in enumerate(acc_of(1)):
                out_buf[1, t, 0:128, :] = a[0:128].astype(BF)
                out_buf[1, t, 128:256, :] = (a[128:256] + half_in[0, 1, t].astype(F32)).astype(BF)
            full[0, 1].start()
            full[0, 0].wait_recv()
            full[0, 1].wait_recv()
            sum_x.wait_recv()
            for t, a in enumerate(acc_of(0)):
                more = full_in[0, 0, t].astype(F32) + full_in[0, 1, t].astype(F32) + x_in[t].astype(F32)
                out_buf[0, t] = (a + more).astype(BF)
            for o in owners:
                o.start()

        return 0

    lax.fori_loop(0, 4, bwd_chunk, 0)
    for kh in range(2):
        bwd_part(0, 2048, SET, kh)
    w2 = cat([weight, weight], 1)
    drk_ref[...] = (dk_acc[0:SET, :] * (w2 * SCALE)).astype(BF)
    drv_ref[...] = (dv_acc[0:SET, :] * w2).astype(BF)

    def finish_bwd(h, _):
        col = pl.ds(pl.multiple_of(h * HD, HD), HD)
        dq_ref[:, col] = (dq_acc[h].T * (weight * SCALE)).astype(BF)
        return 0

    lax.fori_loop(0, HEADS, finish_bwd, 0)

    mine = lax.broadcasted_iota(jnp.int32, (64, 256), 0) + (kv * 8 + grp) * 64 < plen
    for d in range(4):
        src = kvat(4 - d)
        cols = pl.ds(pl.multiple_of(src * 256, 256), 256)
        if d == 0:
            rows = pl.ds(pl.multiple_of(kv * 64, 64), 64)
            got_k, got_v = out_buf[0, 0, rows, :], out_buf[0, 1, rows, :]
        else:
            owners[d - 1].wait_recv()
            got_k, got_v = fin[d, 0], fin[d, 1]
        dpk_ref[:, cols] = jnp.where(mine, got_k.astype(F32) * (w2 * SCALE), 0.0)
        dpv_ref[:, cols] = jnp.where(mine, got_v.astype(F32) * w2, 0.0)

    for c in spread + gather + [w_x] + w_z + w_y + list(half.values()) + list(full.values()) + [sum_x] + owners:
        c.wait_send()


def on_device(
    queries, resp_keys, resp_values, prompt_keys, prompt_values, grad_out, resp_len, prompt_len
):
    vm = pl.BlockSpec(memory_space=pltpu.VMEM)
    sm = pl.BlockSpec(memory_space=pltpu.SMEM)
    shape = jax.ShapeDtypeStruct
    dma = pltpu.SemaphoreType.DMA
    outs = pl.pallas_call(
        kernel,
        out_shape=[
            shape((256, 2048), BF), shape((256, 2048), BF), shape((256, 256), BF), shape((256, 256), BF),
            shape((64, 1024), F32), shape((64, 1024), F32),
        ],
        in_specs=[sm, sm] + [vm] * 6,
        out_specs=[vm] * 6,
        scratch_shapes=[
            pltpu.VMEM((8, 2, SET, 256), BF),
            pltpu.VMEM((HEADS, 2304, SLOTS), BF),
            pltpu.VMEM((HEADS, HD + 16, SLOTS), F32),
            pltpu.VMEM((HEADS, HD, SLOTS), F32),
            pltpu.VMEM((5, HEADS, 1, SLOTS), F32),
            pltpu.VMEM((HEADS, 1, SLOTS), F32),
            pltpu.VMEM((2, 2304, 256), BF),
            pltpu.VMEM((2, 2304, 256), BF),
            pltpu.VMEM((2, HD, 2304), BF),
            pltpu.VMEM((2, HD + 16, 2304), BF),
            pltpu.VMEM((HEADS, SLOTS, 256), BF),
            pltpu.VMEM((HEADS, SLOTS, 256), BF),
            pltpu.VMEM((PC, SLOTS), F32),
            pltpu.VMEM((PC, SLOTS), F32),
            pltpu.VMEM((PC, 256), F32),
            pltpu.VMEM((PC, 256), F32),
            pltpu.VMEM((8, 2, SET, 256), BF),
            pltpu.VMEM((2, 2, 2, 128, 256), BF),
            pltpu.VMEM((2, 2, 2, SET, 256), BF),
            pltpu.VMEM((2, SET, 256), BF),
            pltpu.VMEM((4, 2, 64, 256), BF),
            pltpu.VMEM((3, 8, 128), F32),
            pltpu.VMEM((7, 8, 128), F32),
            dma((6,)), dma((6,)), dma((9,)), dma((9,)), dma((4,)), dma((4,)), dma((4,)), dma((4,)),
            dma(()), dma(()), dma((4,)), dma((4,)), dma((7,)), dma((7,)),
        ],
        compiler_params=pltpu.CompilerParams(
            collective_id=0, has_side_effects=True, vmem_limit_bytes=60 * 2**20
        ),
        name="attention",
    )(
        resp_len, prompt_len, queries.reshape(256, 2048), grad_out.reshape(256, 2048),
        resp_keys.reshape(256, 256), resp_values.reshape(256, 256),
        prompt_keys.reshape(64, 1024), prompt_values.reshape(64, 1024),
    )
    attended, grad_q, grad_rk, grad_rv, grad_pk, grad_pv = outs
    return (
        attended.reshape(queries.shape),
        grad_q.reshape(queries.shape),
        grad_rk.reshape(resp_keys.shape),
        grad_rv.reshape(resp_values.shape),
        grad_pk.reshape(1, 64, 1024),
        grad_pv.reshape(1, 64, 1024),
    )


def solution(mesh):
    wide = P("prompt", "grp", None, "kv")
    rows = P("prompt", ("kv", "grp"), None)
    return jax.shard_map(
        on_device,
        mesh=mesh,
        in_specs=(wide, wide, wide, rows, rows, wide, P("prompt", "grp"), P("prompt")),
        out_specs=(wide, wide, wide, wide, rows, rows),
        check_vma=False,
    )
```

```python
import functools

import jax
import jax.numpy as jnp
from jax import lax
from jax.experimental import pallas as pl
from jax.experimental.pallas import tpu as pltpu
from jax.sharding import PartitionSpec as P

F32 = jnp.float32
BF = jnp.bfloat16
MESH = pl.DeviceIdType.MESH
HD = 128
QPG = 8
SCALE = HD ** (-0.5)
LOG2E = 1.4426950408889634
NT = (((1,), (1,)), ((), ()))
NN = (((1,), (0,)), ((), ()))
SET = 256
PC = 512
HEADS = 16
SLOTS = 256
RESP_AT = 2048
SETS = ((0, 0), (0, 3), (0, 1), (1, 0), (1, 1), (1, 3), (0, 2), (1, 2))


def dot(a, b, dims):
    return lax.dot_general(a, b, dims, preferred_element_type=F32)


def cat(parts, axis):
    return parts[0] if len(parts) == 1 else jnp.concatenate(parts, axis)


def kernel(
    rl_ref, pl_ref, q_ref, do_ref, rk_ref, rv_ref, pk_ref, pv_ref,
    o_ref, dq_ref, drk_ref, drv_ref, dpk_ref, dpv_ref,
    sets, p_ref, o_acc, dq_acc, mc, lse, delta, k_n, k_t, v_t, q_t, d_t, s_buf, ds_buf, dc_buf,
    dk_acc, dv_acc, out_buf, own, half_in, full_in, x_in, fin, w_own, w_in,
    a2a_s, a2a_r, gs, gr, hs, hr, fs, fr, xs, xr, ks, kr, ws, wr,
):
    kv = lax.axis_index("kv")
    grp = lax.axis_index("grp")
    prm = lax.axis_index("prompt")
    xh = grp // 4
    z = grp % 4
    zat = lambda d: {"grp": xh * 4 + (z + d) % 4}
    zp, zm, xp = zat(1), zat(3), {"grp": (1 - xh) * 4 + z}
    kvat = lambda d: (kv + d) % 4
    yat = lambda d: {"prompt": (prm + d) % 4}

    peers = [{"kv": kvat(d)} for d in (1, 2, 3)] + [zat(d) for d in (1, 2, 3)]
    peers += [yat(d) for d in (1, 2, 3)] + [xp]
    barrier = pltpu.get_barrier_semaphore()
    for peer in peers:
        pl.semaphore_signal(barrier, inc=1, device_id=peer, device_id_type=MESH)
    pl.semaphore_wait(barrier, len(peers))

    def cp(src, dst, ssem, rsem, dev):
        return pltpu.make_async_remote_copy(
            src_ref=src, dst_ref=dst, send_sem=ssem, recv_sem=rsem, device_id=dev, device_id_type=MESH
        )

    spread = []
    for d in (1, 2, 3):
        cols = pl.ds(pl.multiple_of(kvat(d) * 256, 256), 256)
        rows = pl.ds(pl.multiple_of(kv * 64, 64), 64)
        for t, ref in ((0, pk_ref), (1, pv_ref)):
            i = (d - 1) * 2 + t
            spread.append(cp(ref.at[:, cols], sets.at[0, t, rows, :], a2a_s.at[i], a2a_r.at[i], {"kv": kvat(d)}))
    lo, hi = pl.ds(0, 128), pl.ds(128, 128)
    to_x = cp(sets.at[0], sets.at[3], gs.at[0], gr.at[0], xp)
    to_p = cp(sets.at[0], sets.at[1], gs.at[1], gr.at[1], zp)
    to_m = cp(sets.at[0], sets.at[2], gs.at[2], gr.at[2], zm)
    on_p = cp(sets.at[1, :, lo], sets.at[6, :, lo], gs.at[3], gr.at[3], zp)
    on_m = cp(sets.at[2, :, hi], sets.at[6, :, hi], gs.at[4], gr.at[4], zm)
    xto_p = cp(sets.at[3], sets.at[5], gs.at[5], gr.at[5], zp)
    xto_m = cp(sets.at[3], sets.at[4], gs.at[6], gr.at[6], zm)
    xon_p = cp(sets.at[5, :, lo], sets.at[7, :, lo], gs.at[7], gr.at[7], zp)
    xon_m = cp(sets.at[4, :, hi], sets.at[7, :, hi], gs.at[8], gr.at[8], zm)
    gather = [to_x, to_p, to_m, on_p, on_m, xto_p, xto_m, xon_p, xon_m]
    w_x = cp(w_own.at[0], w_in.at[0], ws.at[0], wr.at[0], xp)
    w_z = [cp(w_own.at[1], w_in.at[d], ws.at[d], wr.at[d], zat(d)) for d in (1, 2, 3)]
    w_y = [cp(w_own.at[2], w_in.at[3 + d], ws.at[3 + d], wr.at[3 + d], yat(d)) for d in (1, 2, 3)]
    half = {}
    full = {}
    for dx, s in ((0, 6), (1, 7)):
        half[dx, 0] = cp(out_buf.at[s, :, :, lo], half_in.at[dx, 0], hs.at[dx * 2], hr.at[dx * 2], zp)
        half[dx, 1] = cp(out_buf.at[s, :, :, hi], half_in.at[dx, 1], hs.at[dx * 2 + 1], hr.at[dx * 2 + 1], zm)
    for dx, d, s in ((0, 0, 2), (0, 1, 1), (1, 0, 4), (1, 1, 5)):
        i = dx * 2 + d
        full[dx, d] = cp(out_buf.at[s], full_in.at[dx, d], fs.at[i], fr.at[i], zm if d else zp)
    sum_x = cp(out_buf.at[3], x_in, xs, xr, xp)
    owners = []
    for d in (1, 2, 3):
        rows = pl.ds(pl.multiple_of(kvat(d) * 64, 64), 64)
        owners.append(cp(own.at[:, rows, :], fin.at[d], ks.at[d], kr.at[d], {"kv": kvat(d)}))

    for c in spread:
        c.start()
    w_own[0] = jnp.full((8, 128), rl_ref[0, 0].astype(F32))
    w_x.start()

    rows = pl.ds(pl.multiple_of(kv * 64, 64), 64)
    cols = pl.ds(pl.multiple_of(kv * 256, 256), 256)
    sets[0, 0, rows, :] = pk_ref[:, cols]
    sets[0, 1, rows, :] = pv_ref[:, cols]

    live = jnp.where(lax.broadcasted_iota(jnp.int32, (HD, SLOTS), 1) < rl_ref[0, 0], 1.0, 0.0).astype(BF)

    def stage_queries(i, _):
        for u in range(4):
            h = i * 4 + u
            col = pl.ds(pl.multiple_of(h * HD, HD), HD)
            q_t[h] = q_ref[:, col].T
            d_t[h] = do_ref[:, col].T * live
            dq_acc[h] = jnp.zeros((HD, SLOTS), F32)
        return 0

    lax.fori_loop(0, HEADS // 4, stage_queries, 0)
    for kh in range(2):
        head = slice(kh * HD, (kh + 1) * HD)
        k_t[kh, :, RESP_AT:] = rk_ref[:, head].T
        v_t[kh, 0:HD, RESP_AT:] = rv_ref[:, head].T
        v_t[kh, HD:, RESP_AT:] = jnp.ones((16, SET), BF)

    plen = pl_ref[0]

    def valid_keys(s, shape, axis):
        dx, dz = SETS[s]
        owner = (xh if dx == 0 else 1 - xh) * 4 + (z + dz) % 4
        r = lax.broadcasted_iota(jnp.int32, shape, axis)
        index = ((r // 64) * 8 + owner) * 64 + r % 64
        return jnp.where(index < plen, 1.0, 0.0).astype(BF)

    def put_set(s):
        by_row = valid_keys(s, (SET, HD), 0)
        by_col = valid_keys(s, (HD, SET), 1)
        at = slice(s * SET, (s + 1) * SET)
        for kh in range(2):
            head = slice(kh * HD, (kh + 1) * HD)
            k = sets[s, 0, :, head]
            k_n[at, head] = k * by_row + k[0:1, :] * (1 - by_row)
            k_t[kh, :, at] = k.T * by_col
            v_t[kh, 0:HD, at] = sets[s, 1, :, head].T * by_col
            v_t[kh, HD:, at] = by_col[0:16, :]

    def scores(j, h, rows, keys, mask, s_ref):
        top = None
        for r in range(0, rows, 256):
            s = dot(keys(r, h // QPG), q_t[h], NN) * (SCALE * LOG2E)
            if mask is not None:
                s = jnp.where(mask, s, -1e30)
            s_ref[r:r + 256, :] = s
            b = jnp.max(s.reshape(32, 8, SLOTS), 0)
            top = b if top is None else jnp.maximum(top, b)
        m = jnp.max(top, 0, keepdims=True)
        mc[j, h] = m if mask is not None else jnp.maximum(mc[j - 1, h], m)

    def attend(j, h, rows, at, s_ref, first):
        m = mc[j, h]
        parts = []
        for r in range(0, rows, 256):
            p = jnp.exp2(s_ref[r:r + 256, :] - m).astype(BF)
            p_ref[h, pl.ds(at + r, 256), :] = p
            parts.append(p)
        new = dot(v_t[h // QPG, :, pl.ds(at, rows)], cat(parts, 0), NN)
        o_acc[h] = new if first else o_acc[h] * jnp.exp2(mc[j - 1, h] - m) + new

    def forward(j, rows, at, keys, mask):
        first = mask is not None
        for h in range(HEADS + 1):
            if h < HEADS:
                scores(j, h, rows, keys, mask, s_buf.at[h % 2])
            if h > 0:
                attend(j, h - 1, rows, at, s_buf.at[(h - 1) % 2], first)

    for c in spread:
        c.wait_recv()
    for c in (to_x, to_p, to_m):
        c.start()
    t = lax.broadcasted_iota(jnp.int32, (SET, SLOTS), 0)
    i = lax.broadcasted_iota(jnp.int32, (SET, SLOTS), 1)
    forward(0, SET, RESP_AT, lambda r, kh: rk_ref[:, kh * HD:(kh + 1) * HD], (t <= i) & (t < rl_ref[0, 0]))
    w_x.wait_recv()
    w_own[1] = w_own[0] + w_in[0]
    for c in w_z:
        c.start()
    put_set(0)

    def fwd_chunk(c, _):
        @pl.when(c == 0)
        def _():
            to_p.wait_recv()
            on_p.start()
            to_m.wait_recv()
            on_m.start()
            put_set(1)

        @pl.when(c == 1)
        def _():
            to_x.wait_recv()
            xto_p.start()
            xto_m.start()
            put_set(2)
            put_set(3)
            for w in w_z:
                w.wait_recv()
            w_own[2] = w_own[1] + (w_in[1] + w_in[2] + w_in[3])
            for w in w_y:
                w.start()

        @pl.when(c == 2)
        def _():
            xto_p.wait_recv()
            xon_p.start()
            xto_m.wait_recv()
            xon_m.start()
            put_set(4)
            put_set(5)

        @pl.when(c == 3)
        def _():
            on_p.wait_recv()
            on_m.wait_recv()
            put_set(6)
            xon_p.wait_recv()
            xon_m.wait_recv()
            put_set(7)

        at = pl.multiple_of(c * PC, PC)
        forward(c + 1, PC, at, lambda r, kh: k_n[pl.ds(at + r, 256), kh * HD:(kh + 1) * HD], None)
        return 0

    lax.fori_loop(0, 4, fwd_chunk, 0)

    def finish_fwd(i, _):
        for u in range(4):
            h = i * 4 + u
            col = pl.ds(pl.multiple_of(h * HD, HD), HD)
            o = o_acc[h]
            total = o[HD:HD + 1, :]
            out = (o[0:HD, :] * (1.0 / total)).astype(BF)
            o_ref[:, col] = out.T
            delta[h] = jnp.sum(out.astype(F32) * d_t[h].astype(F32), 0, keepdims=True)
            lse[h] = mc[4, h] + jnp.log2(total)
        return 0

    lax.fori_loop(0, HEADS // 4, finish_fwd, 0)
    for w in w_y:
        w.wait_recv()
    count = w_own[2] + (w_in[4] + w_in[5] + w_in[6])
    weight = (8192.0 / count)[0:1, :]

    def weigh(j, h, rows, at, values, ds_ref, dc_ref):
        corr = jnp.exp2(mc[j, h] - lse[h])
        dc = (d_t[h].astype(F32) * corr).astype(BF)
        dc_ref[...] = dc
        cd = corr * delta[h]
        for r in range(0, rows, 256):
            dp = dot(values(r, h // QPG), dc, NN) - cd
            ds_ref[r:r + 256, :] = p_ref[h, pl.ds(at + r, 256), :] * dp.astype(BF)

    def spread_back(h, rows, at, ds_ref, dc_ref):
        kh = h // QPG
        dq_acc[h] += dot(k_t[kh, :, pl.ds(at, rows)], ds_ref[0:rows, :], NN)
        for r in range(0, rows, 256):
            dv = dot(dc_ref[...], p_ref[h, pl.ds(at + r, 256), :], NT)
            dk = dot(q_t[h], ds_ref[r:r + 256, :], NT)
            if h % QPG == 0:
                dv_acc[kh, :, r:r + 256] = dv
                dk_acc[kh, :, r:r + 256] = dk
            else:
                dv_acc[kh, :, r:r + 256] += dv
                dk_acc[kh, :, r:r + 256] += dk

    def backward(j, rows, at, values):
        for h in range(HEADS + 1):
            if h < HEADS:
                weigh(j, h, rows, at, values, ds_buf.at[h % 2], dc_buf.at[h % 2])
            if h > 0:
                spread_back(h - 1, rows, at, ds_buf.at[(h - 1) % 2], dc_buf.at[(h - 1) % 2])

    def acc_of(s):
        r = slice((s % 2) * SET, (s % 2 + 1) * SET)
        return [cat([a[0, :, r], a[1, :, r]], 0) for a in (dk_acc, dv_acc)]

    def bwd_chunk(i, _):
        c = 3 - i
        at = pl.multiple_of(c * PC, PC)
        backward(c + 1, PC, at, lambda r, kh: sets[2 * c + r // SET, 1, :, kh * HD:(kh + 1) * HD])

        @pl.when(c == 3)
        def _():
            for dx, s in ((1, 7), (0, 6)):
                for t, a in enumerate(acc_of(s)):
                    out_buf[s, t] = a.astype(BF)
                half[dx, 0].start()
                half[dx, 1].start()

        @pl.when(c == 2)
        def _():
            for d, s in ((0, 4), (1, 5)):
                half[1, d].wait_recv()
                for t, a in enumerate(acc_of(s)):
                    put_half(s, t, d, a, half_in[1, d, t])
                full[1, d].start()

        @pl.when(c == 1)
        def _():
            half[0, 0].wait_recv()
            for t, a in enumerate(acc_of(2)):
                put_half(2, t, 0, a, half_in[0, 0, t])
            full[0, 0].start()
            full[1, 0].wait_recv()
            full[1, 1].wait_recv()
            for t, a in enumerate(acc_of(3)):
                out_buf[3, t] = (a + full_in[1, 0, t].astype(F32) + full_in[1, 1, t].astype(F32)).astype(BF)
            sum_x.start()

        @pl.when(c == 0)
        def _():
            half[0, 1].wait_recv()
            for t, a in enumerate(acc_of(1)):
                put_half(1, t, 1, a, half_in[0, 1, t])
            full[0, 1].start()
            full[0, 0].wait_recv()
            full[0, 1].wait_recv()
            sum_x.wait_recv()
            for t, a in enumerate(acc_of(0)):
                more = full_in[0, 0, t].astype(F32) + full_in[0, 1, t].astype(F32) + x_in[t].astype(F32)
                own[t] = (a + more).astype(BF).T
            for o in owners:
                o.start()

        return 0

    def put_half(s, t, d, a, part):
        near, far = slice(d * 128, d * 128 + 128), slice(128 - d * 128, 256 - d * 128)
        out_buf[s, t, :, near] = (a[:, near] + part.astype(F32)).astype(BF)
        out_buf[s, t, :, far] = a[:, far].astype(BF)

    lax.fori_loop(0, 4, bwd_chunk, 0)
    backward(0, SET, RESP_AT, lambda r, kh: rv_ref[:, kh * HD:(kh + 1) * HD])
    w2 = cat([weight, weight], 1)
    acc_k, acc_v = acc_of(0)
    drk_ref[...] = (acc_k * (w2 * SCALE)).T.astype(BF)
    drv_ref[...] = (acc_v * w2).T.astype(BF)

    def finish_bwd(i, _):
        for u in range(4):
            h = i * 4 + u
            col = pl.ds(pl.multiple_of(h * HD, HD), HD)
            dq_ref[:, col] = (dq_acc[h] * (w2 * SCALE)).astype(BF).T
        return 0

    lax.fori_loop(0, HEADS // 4, finish_bwd, 0)

    mine = lax.broadcasted_iota(jnp.int32, (64, 256), 0) + (kv * 8 + grp) * 64 < plen
    for d in range(4):
        src = kvat(4 - d)
        cols = pl.ds(pl.multiple_of(src * 256, 256), 256)
        if d == 0:
            rows = pl.ds(pl.multiple_of(kv * 64, 64), 64)
            got_k, got_v = own[0, rows, :], own[1, rows, :]
        else:
            owners[d - 1].wait_recv()
            got_k, got_v = fin[d, 0], fin[d, 1]
        dpk_ref[:, cols] = jnp.where(mine, got_k.astype(F32) * (w2 * SCALE), 0.0)
        dpv_ref[:, cols] = jnp.where(mine, got_v.astype(F32) * w2, 0.0)

    for c in spread + gather + [w_x] + w_z + w_y + list(half.values()) + list(full.values()) + [sum_x] + owners:
        c.wait_send()


def on_device(
    queries, resp_keys, resp_values, prompt_keys, prompt_values, grad_out, resp_len, prompt_len
):
    vm = pl.BlockSpec(memory_space=pltpu.VMEM)
    sm = pl.BlockSpec(memory_space=pltpu.SMEM)
    shape = jax.ShapeDtypeStruct
    dma = pltpu.SemaphoreType.DMA
    outs = pl.pallas_call(
        kernel,
        out_shape=[
            shape((256, 2048), BF), shape((256, 2048), BF), shape((256, 256), BF), shape((256, 256), BF),
            shape((64, 1024), F32), shape((64, 1024), F32),
        ],
        in_specs=[sm, sm] + [vm] * 6,
        out_specs=[vm] * 6,
        scratch_shapes=[
            pltpu.VMEM((8, 2, SET, 256), BF),
            pltpu.VMEM((HEADS, 2304, SLOTS), BF),
            pltpu.VMEM((HEADS, HD + 16, SLOTS), F32),
            pltpu.VMEM((HEADS, HD, SLOTS), F32),
            pltpu.VMEM((5, HEADS, 1, SLOTS), F32),
            pltpu.VMEM((HEADS, 1, SLOTS), F32),
            pltpu.VMEM((HEADS, 1, SLOTS), F32),
            pltpu.VMEM((RESP_AT, 256), BF),
            pltpu.VMEM((2, HD, 2304), BF),
            pltpu.VMEM((2, HD + 16, 2304), BF),
            pltpu.VMEM((HEADS, HD, SLOTS), BF),
            pltpu.VMEM((HEADS, HD, SLOTS), BF),
            pltpu.VMEM((2, PC, SLOTS), F32),
            pltpu.VMEM((2, PC, SLOTS), BF),
            pltpu.VMEM((2, HD, SLOTS), BF),
            pltpu.VMEM((2, HD, PC), F32),
            pltpu.VMEM((2, HD, PC), F32),
            pltpu.VMEM((8, 2, 256, SET), BF),
            pltpu.VMEM((2, SET, 256), BF),
            pltpu.VMEM((2, 2, 2, 256, 128), BF),
            pltpu.VMEM((2, 2, 2, 256, SET), BF),
            pltpu.VMEM((2, 256, SET), BF),
            pltpu.VMEM((4, 2, 64, 256), BF),
            pltpu.VMEM((3, 8, 128), F32),
            pltpu.VMEM((7, 8, 128), F32),
            dma((6,)), dma((6,)), dma((9,)), dma((9,)), dma((4,)), dma((4,)), dma((4,)), dma((4,)),
            dma(()), dma(()), dma((4,)), dma((4,)), dma((7,)), dma((7,)),
        ],
        compiler_params=pltpu.CompilerParams(
            collective_id=0, has_side_effects=True, vmem_limit_bytes=60 * 2**20
        ),
        name="attention",
    )(
        resp_len, prompt_len, queries.reshape(256, 2048), grad_out.reshape(256, 2048),
        resp_keys.reshape(256, 256), resp_values.reshape(256, 256),
        prompt_keys.reshape(64, 1024), prompt_values.reshape(64, 1024),
    )
    attended, grad_q, grad_rk, grad_rv, grad_pk, grad_pv = outs
    return (
        attended.reshape(queries.shape),
        grad_q.reshape(queries.shape),
        grad_rk.reshape(resp_keys.shape),
        grad_rv.reshape(resp_values.shape),
        grad_pk.reshape(1, 64, 1024),
        grad_pv.reshape(1, 64, 1024),
    )


def solution(mesh):
    wide = P("prompt", "grp", None, "kv")
    rows = P("prompt", ("kv", "grp"), None)
    return jax.shard_map(
        on_device,
        mesh=mesh,
        in_specs=(wide, wide, wide, rows, rows, wide, P("prompt", "grp"), P("prompt")),
        out_specs=(wide, wide, wide, wide, rows, rows),
        check_vma=False,
    )
```

```python
import jax
import jax.numpy as jnp
from jax import lax
from jax.experimental import pallas as pl
from jax.experimental.pallas import tpu as pltpu
from jax.sharding import PartitionSpec as P

F32 = jnp.float32
BF = jnp.bfloat16
MESH = pl.DeviceIdType.MESH
HD = 128
QPG = 8
SCALE = HD ** (-0.5)
LOG2E = 1.4426950408889634
NT = (((1,), (1,)), ((), ()))
NN = (((1,), (0,)), ((), ()))
SET = 256
PC = 512
HEADS = 16
SLOTS = 256
RESP_AT = 2048
KEYS = 2304
SETS = ((0, 0), (0, 3), (0, 1), (1, 0), (1, 1), (1, 3), (0, 2), (1, 2))


def dot(a, b, dims):
    return lax.dot_general(a, b, dims, preferred_element_type=F32)


def cat(parts, axis):
    return parts[0] if len(parts) == 1 else jnp.concatenate(parts, axis)


def kernel(
    rl_ref, pl_ref, q_hbm, do_hbm, rk_hbm, rv_hbm, pk_hbm, pv_hbm,
    o_hbm, dq_hbm, drk_ref, drv_ref, dpk_ref, dpv_ref,
    sets, p_ref, ds_ref, o_acc, o_out, mc, lse, delta, k_n, k_t, v_t, r_kv, q_t, d_t,
    s_a, s_b, ds_a, ds_b, dc_a, dc_b, dk_acc, dv_acc,
    out_buf, own, half_in, plane_in, z_in, x_in, far_in, fin, w_own, w_in,
    ls, a2a_s, a2a_r, gs, gr, hs, hr, ks, kr, ws, wr,
):
    kv = lax.axis_index("kv")
    grp = lax.axis_index("grp")
    prm = lax.axis_index("prompt")
    xh = grp // 4
    z = grp % 4
    zat = lambda d: {"grp": xh * 4 + (z + d) % 4}
    zp, zm, xp = zat(1), zat(3), {"grp": (1 - xh) * 4 + z}
    kvat = lambda d: (kv + d) % 4
    yat = lambda d: {"prompt": (prm + d) % 4}
    my_rows = pl.ds(pl.multiple_of(kv * 64, 64), 64)
    head_cols = lambda who, t: pl.ds(pl.multiple_of(who * 256 + t * HD, HD), HD)

    pair = lambda i: pl.ds(i * 256, 256)
    local = []
    for i in range(8):
        local.append(pltpu.make_async_copy(q_hbm.at[:, pair(i)], ds_ref.at[i, 0:256, :], ls.at[i]))
        local.append(pltpu.make_async_copy(do_hbm.at[:, pair(i)], ds_ref.at[i, 256:512, :], ls.at[8 + i]))
    local.append(pltpu.make_async_copy(rk_hbm, r_kv.at[0], ls.at[16]))
    local.append(pltpu.make_async_copy(rv_hbm, r_kv.at[1], ls.at[17]))
    for t in range(2):
        for i, ref in ((0, pk_hbm), (1, pv_hbm)):
            local.append(
                pltpu.make_async_copy(
                    ref.at[:, head_cols(kv, t)], sets.at[t, 0, i, my_rows, :], ls.at[18 + t * 2 + i]
                )
            )
    for c in local:
        c.start()

    peers = [{"kv": kvat(d)} for d in (1, 2, 3)] + [zat(d) for d in (1, 2, 3)]
    peers += [yat(d) for d in (1, 2, 3)] + [xp]
    barrier = pltpu.get_barrier_semaphore()
    for peer in peers:
        pl.semaphore_signal(barrier, inc=1, device_id=peer, device_id_type=MESH)
    pl.semaphore_wait(barrier, len(peers))

    def cp(src, dst, ssem, rsem, dev):
        return pltpu.make_async_remote_copy(
            src_ref=src, dst_ref=dst, send_sem=ssem, recv_sem=rsem, device_id=dev, device_id_type=MESH
        )

    def spread(t):
        made = []
        for d in (1, 2, 3):
            for i, ref in ((0, pk_hbm), (1, pv_hbm)):
                n = (d - 1) * 2 + i
                made.append(
                    cp(ref.at[:, head_cols(kvat(d), t)], sets.at[t, 0, i, my_rows, :],
                       a2a_s.at[t, n], a2a_r.at[t, n], {"kv": kvat(d)})
                )
        return made

    lo, hi = pl.ds(0, 128), pl.ds(128, 128)

    def moved(t, n, src, dst, dev, rows=None):
        a, b = sets.at[t, src], sets.at[t, dst]
        if rows is not None:
            a, b = a.at[:, rows], b.at[:, rows]
        return cp(a, b, gs.at[t, n], gr.at[t, n], dev)

    to_x = lambda t: moved(t, 0, 0, 3, xp)
    to_p = lambda t: moved(t, 1, 0, 1, zp)
    to_m = lambda t: moved(t, 2, 0, 2, zm)
    on_p = lambda t: moved(t, 3, 1, 6, zp, lo)
    on_m = lambda t: moved(t, 4, 2, 6, zm, hi)
    xto_p = lambda t: moved(t, 5, 3, 5, zp)
    xto_m = lambda t: moved(t, 6, 3, 4, zm)
    far = lambda t: moved(t, 7, 6, 7, xp)
    gather = [to_x, to_p, to_m, on_p, on_m, xto_p, xto_m, far]
    w_x = cp(w_own.at[0], w_in.at[0], ws.at[0], wr.at[0], xp)
    w_z = [cp(w_own.at[1], w_in.at[d], ws.at[d], wr.at[d], zat(d)) for d in (1, 2, 3)]
    w_y = [cp(w_own.at[2], w_in.at[3 + d], ws.at[3 + d], wr.at[3 + d], yat(d)) for d in (1, 2, 3)]
    def summed(t, n, src, dst, dev):
        return cp(src, dst, hs.at[t, n], hr.at[t, n], dev)

    far_sum = lambda t: summed(t, 0, out_buf.at[t, 7], far_in.at[t], xp)
    half_p = lambda t: summed(t, 1, out_buf.at[t, 6, :, :, lo], half_in.at[t, 0], zp)
    half_m = lambda t: summed(t, 2, out_buf.at[t, 6, :, :, hi], half_in.at[t, 1], zm)
    plane_p = lambda t: summed(t, 3, out_buf.at[t, 4], plane_in.at[t, 0], zp)
    plane_m = lambda t: summed(t, 4, out_buf.at[t, 5], plane_in.at[t, 1], zm)
    z_p = lambda t: summed(t, 5, out_buf.at[t, 2], z_in.at[t, 0], zp)
    z_m = lambda t: summed(t, 6, out_buf.at[t, 1], z_in.at[t, 1], zm)
    x_sum = lambda t: summed(t, 7, out_buf.at[t, 3], x_in.at[t], xp)
    sums = [far_sum, half_p, half_m, plane_p, plane_m, z_p, z_m, x_sum]

    def to_owner(t, d):
        rows = pl.ds(pl.multiple_of(kvat(d) * 64, 64), 64)
        return cp(own.at[t, :, rows, :], fin.at[t, d], ks.at[t, d], kr.at[t, d], {"kv": kvat(d)})

    for t in range(2):
        for c in spread(t):
            c.start()
    w_own[0] = jnp.full((8, 128), rl_ref[0, 0].astype(F32))
    w_x.start()
    for c in local:
        c.wait()

    live = jnp.where(lax.broadcasted_iota(jnp.int32, (HD, SLOTS), 1) < rl_ref[0, 0], 1.0, 0.0).astype(BF)

    def stage_queries(i, _):
        for u in range(2):
            for v in range(2):
                h = i * 4 + u * 2 + v
                half = slice(v * HD, (v + 1) * HD)
                q_t[h] = ds_ref[i * 2 + u, 0:256, half].T
                d_t[h] = ds_ref[i * 2 + u, 256:512, half].T * live
        return 0

    lax.fori_loop(0, HEADS // 4, stage_queries, 0)
    for t in range(2):
        head = slice(t * HD, (t + 1) * HD)
        k_t[t, :, RESP_AT:] = r_kv[0, :, head].T
        v_t[t, 0:HD, RESP_AT:] = r_kv[1, :, head].T
        v_t[t, HD:, RESP_AT:] = jnp.ones((16, SET), BF)

    plen = pl_ref[0]

    def valid_keys(s, shape, axis):
        dx, dz = SETS[s]
        owner = (xh if dx == 0 else 1 - xh) * 4 + (z + dz) % 4
        r = lax.broadcasted_iota(jnp.int32, shape, axis)
        return jnp.where((r // 64) * 512 + r % 64 < plen - owner * 64, 1.0, 0.0).astype(BF)

    def put_set(t, s):
        by_row = valid_keys(s, (SET, HD), 0)
        by_col = valid_keys(s, (16, SET), 1)
        at = slice(s * SET, (s + 1) * SET)
        k = sets[t, s, 0]
        k_n[t, at, :] = k * by_row + k[0:1, :] * (1 - by_row)
        k_t[t, :, at] = k.T * by_col[0:1, :]
        v_t[t, 0:HD, at] = sets[t, s, 1].T * by_col[0:1, :]
        v_t[t, HD:, at] = by_col

    s_bufs, ds_bufs, dc_bufs = (s_a, s_b), (ds_a, ds_b), (dc_a, dc_b)

    def scores(t, j, u, rows, keys, mask):
        h = t * QPG + u
        s_ref = s_bufs[u % 2]
        top = None
        for r in range(0, rows, 256):
            s = dot(keys(r), q_t[h], NN) * (SCALE * LOG2E)
            if mask is not None:
                s = jnp.where(mask, s, -1e30)
            s_ref[r:r + 256, :] = s
            b = jnp.max(s.reshape(32, 8, SLOTS), 0)
            top = b if top is None else jnp.maximum(top, b)
        m = jnp.max(top, 0, keepdims=True)
        mc[j, h] = m if mask is not None else jnp.maximum(mc[j - 1, h], m)

    def attend(t, j, u, rows, at, first):
        h = t * QPG + u
        s_ref = s_bufs[u % 2]
        m = mc[j, h]
        parts = []
        for r in range(0, rows, 256):
            p = jnp.exp2(s_ref[r:r + 256, :] - m).astype(BF)
            p_ref[h, pl.ds(at + r, 256), :] = p
            parts.append(p)
        new = dot(v_t[t, :, pl.ds(at, rows)], cat(parts, 0), NN)
        o_acc[h] = new if first else o_acc[h] * jnp.exp2(mc[j - 1, h] - m) + new

    def forward(t, j, rows, at, keys, mask):
        for u in range(QPG + 1):
            if u < QPG:
                scores(t, j, u, rows, keys, mask)
            if u > 0:
                attend(t, j, u - 1, rows, at, mask is not None)

    def weigh(t, j, u, rows, at, values):
        h = t * QPG + u
        corr = jnp.exp2(mc[j, h] - lse[h])
        dc = (d_t[h].astype(F32) * corr).astype(BF)
        dc_bufs[u % 2][...] = dc
        cd = corr * delta[h]
        for r in range(0, rows, 256):
            dp = dot(values(r), dc, NN) - cd
            ds = p_ref[h, pl.ds(at + r, 256), :] * dp.astype(BF)
            ds_bufs[u % 2][r:r + 256, :] = ds
            ds_ref[h, pl.ds(at + r, 256), :] = ds

    def key_sums(t, u, rows, at):
        h = t * QPG + u
        for r in range(0, rows, 256):
            dv = dot(dc_bufs[u % 2][...], p_ref[h, pl.ds(at + r, 256), :], NT)
            dk = dot(q_t[h], ds_bufs[u % 2][r:r + 256, :], NT)
            if u == 0:
                dv_acc[:, r:r + 256] = dv
                dk_acc[:, r:r + 256] = dk
            else:
                dv_acc[:, r:r + 256] += dv
                dk_acc[:, r:r + 256] += dk

    def backward(t, j, rows, at, values):
        for u in range(QPG + 1):
            if u < QPG:
                weigh(t, j, u, rows, at, values)
            if u > 0:
                key_sums(t, u - 1, rows, at)

    def query_sums(t):
        for u in range(QPG):
            h = t * QPG + u
            dq = dot(k_t[t], ds_ref[h], NN) * (w2 * SCALE)
            p_ref[t * 4 + u // 2, 0:256, (u % 2) * HD:(u % 2 + 1) * HD] = dq.astype(BF).T

    for c in spread(0):
        c.wait_recv()
    for c in (to_x, to_p, to_m):
        c(0).start()
    row_at = lax.broadcasted_iota(jnp.int32, (SET, SLOTS), 0)
    slot_at = lax.broadcasted_iota(jnp.int32, (SET, SLOTS), 1)
    causal = (row_at <= slot_at) & (row_at < rl_ref[0, 0])

    for t in range(2):
        head = slice(t * HD, (t + 1) * HD)
        forward(t, 0, SET, RESP_AT, lambda r: r_kv[0, :, head], causal)
    w_x.wait_recv()
    w_own[1] = w_own[0] + w_in[0]
    for c in w_z:
        c.start()

    def owner_sum(t):
        z_p(t).wait_recv()
        z_m(t).wait_recv()
        x_sum(t).wait_recv()
        for i in range(2):
            total = out_buf[t, 0, i].astype(F32) + z_in[t, 0, i].astype(F32)
            total = total + (z_in[t, 1, i].astype(F32) + x_in[t, i].astype(F32))
            own[t, i] = total.astype(BF).T
        for d in (1, 2, 3):
            to_owner(t, d).start()

    def fwd_chunk(t, c):
        first = t == 0

        @pl.when(c == 0)
        def _():
            @pl.when(first)
            def _():
                to_p(0).wait_recv()
                on_p(0).start()
                to_m(0).wait_recv()
                on_m(0).start()
                to_x(0).wait_recv()
                xto_p(0).start()
                xto_m(0).start()

            put_set(t, 0)
            put_set(t, 1)

        @pl.when(c == 1)
        def _():
            @pl.when(first)
            def _():
                for w in w_z:
                    w.wait_recv()
                w_own[2] = w_own[1] + (w_in[1] + w_in[2] + w_in[3])
                for w in w_y:
                    w.start()

            @pl.when(jnp.logical_not(first))
            def _():
                owner_sum(0)

            put_set(t, 2)
            put_set(t, 3)

        @pl.when(c == 2)
        def _():
            @pl.when(first)
            def _():
                on_p(0).wait_recv()
                on_m(0).wait_recv()
                far(0).start()
                for o in spread(1):
                    o.wait_recv()
                for o in (to_x, to_p, to_m):
                    o(1).start()

            xto_p(t).wait_recv()
            xto_m(t).wait_recv()
            put_set(t, 4)
            put_set(t, 5)

        @pl.when(c == 3)
        def _():
            far(t).wait_recv()
            put_set(t, 6)
            put_set(t, 7)

        at = pl.multiple_of(c * PC, PC)
        forward(t, c + 1, PC, at, lambda r: k_n[t, pl.ds(at + r, 256), :], None)

    def finish_fwd(t):
        for u in range(QPG):
            h = t * QPG + u
            o = o_acc[h]
            total = o[HD:HD + 1, :]
            out = (o[0:HD, :] * (1.0 / total)).astype(BF)
            o_out[t * 4 + u // 2, :, (u % 2) * HD:(u % 2 + 1) * HD] = out.T
            delta[h] = jnp.sum(out.astype(F32) * d_t[h].astype(F32), 0, keepdims=True)
            lse[h] = mc[4, h] + jnp.log2(total)

    def bwd_chunk(t, c):
        first = t == 0

        @pl.when((c == 3) & first)
        def _():
            to_p(1).wait_recv()
            on_p(1).start()
            to_m(1).wait_recv()
            on_m(1).start()
            to_x(1).wait_recv()
            xto_p(1).start()
            xto_m(1).start()

        @pl.when((c == 1) & first)
        def _():
            on_p(1).wait_recv()
            on_m(1).wait_recv()
            far(1).start()

        at = pl.multiple_of(c * PC, PC)
        backward(t, c + 1, PC, at, lambda r: sets[t, 2 * c + r // SET, 1])
        for i in range(2):
            out_buf[t, 2 * c + i, 0] = dk_acc[:, i * SET:(i + 1) * SET].astype(BF)
            out_buf[t, 2 * c + i, 1] = dv_acc[:, i * SET:(i + 1) * SET].astype(BF)

        @pl.when(c == 3)
        def _():
            far_sum(t).start()

        @pl.when(c == 2)
        def _():
            plane_p(t).start()
            plane_m(t).start()
            far_sum(t).wait_recv()
            out_buf[t, 6] = (out_buf[t, 6].astype(F32) + far_in[t].astype(F32)).astype(BF)
            half_p(t).start()
            half_m(t).start()

        @pl.when(c == 0)
        def _():
            plane_p(t).wait_recv()
            plane_m(t).wait_recv()
            total = plane_in[t, 0].astype(F32) + plane_in[t, 1].astype(F32)
            out_buf[t, 3] = (out_buf[t, 3].astype(F32) + total).astype(BF)
            x_sum(t).start()
            half_p(t).wait_recv()
            out_buf[t, 2, :, :, 0:128] = (
                out_buf[t, 2, :, :, 0:128].astype(F32) + half_in[t, 0].astype(F32)
            ).astype(BF)
            z_p(t).start()
            half_m(t).wait_recv()
            out_buf[t, 1, :, :, 128:256] = (
                out_buf[t, 1, :, :, 128:256].astype(F32) + half_in[t, 1].astype(F32)
            ).astype(BF)
            z_m(t).start()

    def o_copy(i):
        return pltpu.make_async_copy(o_out.at[i], o_hbm.at[:, pair(i)], ls.at[i])

    def both(t, _):
        lax.fori_loop(0, 4, lambda c, _: (fwd_chunk(t, c), 0)[1], 0)
        finish_fwd(t)
        lax.fori_loop(0, 4, lambda i, _: (bwd_chunk(t, 3 - i), 0)[1], 0)
        return 0

    lax.fori_loop(0, 2, both, 0)
    for i in range(8):
        o_copy(i).start()
    for w in w_y:
        w.wait_recv()
    count = w_own[2] + (w_in[4] + w_in[5] + w_in[6])
    weight = (8192.0 / count)[0:1, :]
    w2 = cat([weight, weight], 1)

    for t in range(2):
        head = slice(t * HD, (t + 1) * HD)
        backward(t, 0, SET, RESP_AT, lambda r: r_kv[1, :, head])
        drk_ref[:, head] = (dk_acc[:, 0:SET] * (w2 * SCALE)).T.astype(BF)
        drv_ref[:, head] = (dv_acc[:, 0:SET] * w2).T.astype(BF)

    def dq_copy(i):
        return pltpu.make_async_copy(p_ref.at[i, 0:256, :], dq_hbm.at[:, pair(i)], ls.at[8 + i])

    query_sums(0)
    for i in range(4):
        dq_copy(i).start()
    owner_sum(1)
    query_sums(1)
    for i in range(4, 8):
        dq_copy(i).start()

    mine = lax.broadcasted_iota(jnp.int32, (64, HD), 0) + (kv * 8 + grp) * 64 < plen
    for t in range(2):
        for d in range(4):
            cols = head_cols(kvat(4 - d), t)
            if d == 0:
                got_k, got_v = own[t, 0, my_rows, :], own[t, 1, my_rows, :]
            else:
                to_owner(t, d).wait_recv()
                got_k, got_v = fin[t, d, 0], fin[t, d, 1]
            dpk_ref[:, cols] = jnp.where(mine, got_k.astype(F32) * (weight * SCALE), 0.0)
            dpv_ref[:, cols] = jnp.where(mine, got_v.astype(F32) * weight, 0.0)

    for t in range(2):
        for c in spread(t) + [g(t) for g in gather] + [s(t) for s in sums] + [to_owner(t, d) for d in (1, 2, 3)]:
            c.wait_send()
    for c in [w_x] + w_z + w_y:
        c.wait_send()
    for i in range(8):
        o_copy(i).wait()
        dq_copy(i).wait()


def hand_over(*refs):
    n = len(refs) // 2
    sems = refs[-1]
    copies = [pltpu.make_async_copy(refs[i], refs[n + i], sems.at[i]) for i in range(n)]
    for c in copies:
        c.start()
    for c in copies:
        c.wait()


def on_device(
    queries, resp_keys, resp_values, prompt_keys, prompt_values, grad_out, resp_len, prompt_len
):
    vm = pl.BlockSpec(memory_space=pltpu.VMEM)
    sm = pl.BlockSpec(memory_space=pltpu.SMEM)
    hbm = pl.BlockSpec(memory_space=pl.ANY)
    shape = jax.ShapeDtypeStruct
    dma = pltpu.SemaphoreType.DMA
    shapes = [
        shape((256, 2048), BF), shape((256, 2048), BF), shape((256, 256), BF), shape((256, 256), BF),
        shape((64, 1024), F32), shape((64, 1024), F32),
    ]
    outs = pl.pallas_call(
        kernel,
        out_shape=shapes,
        in_specs=[sm, sm] + [hbm] * 6,
        out_specs=[hbm, hbm] + [vm] * 4,
        scratch_shapes=[
            pltpu.VMEM((2, 8, 2, SET, HD), BF),
            pltpu.VMEM((HEADS, KEYS, SLOTS), BF),
            pltpu.VMEM((HEADS, KEYS, SLOTS), BF),
            pltpu.VMEM((HEADS, HD + 16, SLOTS), F32),
            pltpu.VMEM((8, SLOTS, 256), BF),
            pltpu.VMEM((5, HEADS, 1, SLOTS), F32),
            pltpu.VMEM((HEADS, 1, SLOTS), F32),
            pltpu.VMEM((HEADS, 1, SLOTS), F32),
            pltpu.VMEM((2, RESP_AT, HD), BF),
            pltpu.VMEM((2, HD, KEYS), BF),
            pltpu.VMEM((2, HD + 16, KEYS), BF),
            pltpu.VMEM((2, SET, 256), BF),
            pltpu.VMEM((HEADS, HD, SLOTS), BF),
            pltpu.VMEM((HEADS, HD, SLOTS), BF),
            pltpu.VMEM((PC, SLOTS), F32),
            pltpu.VMEM((PC, SLOTS), F32),
            pltpu.VMEM((PC, SLOTS), BF),
            pltpu.VMEM((PC, SLOTS), BF),
            pltpu.VMEM((HD, SLOTS), BF),
            pltpu.VMEM((HD, SLOTS), BF),
            pltpu.VMEM((HD, PC), F32),
            pltpu.VMEM((HD, PC), F32),
            pltpu.VMEM((2, 8, 2, HD, SET), BF),
            pltpu.VMEM((2, 2, SET, HD), BF),
            pltpu.VMEM((2, 2, 2, HD, 128), BF),
            pltpu.VMEM((2, 2, 2, HD, SET), BF),
            pltpu.VMEM((2, 2, 2, HD, SET), BF),
            pltpu.VMEM((2, 2, HD, SET), BF),
            pltpu.VMEM((2, 2, HD, SET), BF),
            pltpu.VMEM((2, 4, 2, 64, HD), BF),
            pltpu.VMEM((3, 8, 128), F32),
            pltpu.VMEM((7, 8, 128), F32),
            dma((22,)), dma((2, 6)), dma((2, 6)), dma((2, 8)), dma((2, 8)), dma((2, 8)), dma((2, 8)),
            dma((2, 4)), dma((2, 4)), dma((7,)), dma((7,)),
        ],
        compiler_params=pltpu.CompilerParams(
            collective_id=0, has_side_effects=True, vmem_limit_bytes=62 * 2**20
        ),
        name="attention",
    )(
        resp_len, prompt_len, queries.reshape(256, 2048), grad_out.reshape(256, 2048),
        resp_keys.reshape(256, 256), resp_values.reshape(256, 256),
        prompt_keys.reshape(64, 1024), prompt_values.reshape(64, 1024),
    )
    attended, grad_q, grad_rk, grad_rv, grad_pk, grad_pv = pl.pallas_call(
        hand_over,
        out_shape=shapes,
        in_specs=[hbm] * 6,
        out_specs=[hbm] * 6,
        scratch_shapes=[dma((6,))],
        name="hand_over",
    )(*outs)
    return (
        attended.reshape(queries.shape),
        grad_q.reshape(queries.shape),
        grad_rk.reshape(resp_keys.shape),
        grad_rv.reshape(resp_values.shape),
        grad_pk.reshape(1, 64, 1024),
        grad_pv.reshape(1, 64, 1024),
    )


def solution(mesh):
    wide = P("prompt", "grp", None, "kv")
    rows = P("prompt", ("kv", "grp"), None)
    return jax.shard_map(
        on_device,
        mesh=mesh,
        in_specs=(wide, wide, wide, rows, rows, wide, P("prompt", "grp"), P("prompt")),
        out_specs=(wide, wide, wide, wide, rows, rows),
        check_vma=False,
    )
```

```python
import jax
import jax.numpy as jnp
from jax import lax
from jax.experimental import pallas as pl
from jax.experimental.pallas import tpu as pltpu
from jax.sharding import PartitionSpec as P

F32 = jnp.float32
BF = jnp.bfloat16
MESH = pl.DeviceIdType.MESH
HD = 128
QPG = 8
SCALE = HD ** (-0.5)
LOG2E = 1.4426950408889634
NT = (((1,), (1,)), ((), ()))
NN = (((1,), (0,)), ((), ()))
SET = 256
PC = 512
HEADS = 16
SLOTS = 256
RESP_AT = 2048
KEYS = 2304
OWN_AT = 1792
LAST_AT = 1536
SETS = ((0, 0), (0, 3), (0, 1), (1, 0), (0, 2), (1, 1), (1, 3), (1, 2))


def dot(a, b, dims):
    return lax.dot_general(a, b, dims, preferred_element_type=F32)


def cat(parts, axis):
    return parts[0] if len(parts) == 1 else jnp.concatenate(parts, axis)


def kernel(
    rl_ref, pl_ref, q_hbm, do_hbm, rk_hbm, rv_hbm, pk_hbm, pv_hbm,
    o_hbm, dq_hbm, drk_ref, drv_ref, dpk_ref, dpv_ref,
    sets, p_ref, ds_ref, o_acc, o_out, mc, lse, delta, k_n, k_t, v_t, r_kv, q_t, d_t,
    s_a, s_b, ds_a, ds_b, dc_a, dc_b, dk_acc, dv_acc,
    out_buf, own, half_in, plane_in, z_in, x_in, far_in, fin, w_own, w_in,
    ls, a2a_s, a2a_r, gs, gr, hs, hr, ks, kr, ws, wr,
):
    kv = lax.axis_index("kv")
    grp = lax.axis_index("grp")
    prm = lax.axis_index("prompt")
    xh = grp // 4
    z = grp % 4
    zat = lambda d: {"grp": xh * 4 + (z + d) % 4}
    zp, zm, xp = zat(1), zat(3), {"grp": (1 - xh) * 4 + z}
    kvat = lambda d: (kv + d) % 4
    yat = lambda d: {"prompt": (prm + d) % 4}
    my_rows = pl.ds(pl.multiple_of(kv * 64, 64), 64)
    head_cols = lambda who, t: pl.ds(pl.multiple_of(who * 256 + t * HD, HD), HD)

    pair = lambda i: pl.ds(i * 256, 256)
    local = []
    for i in range(8):
        local.append(pltpu.make_async_copy(q_hbm.at[:, pair(i)], ds_ref.at[i, 0:256, :], ls.at[i]))
        local.append(pltpu.make_async_copy(do_hbm.at[:, pair(i)], ds_ref.at[i, 256:512, :], ls.at[8 + i]))
    for t in range(2):
        for i, ref in ((0, pk_hbm), (1, pv_hbm)):
            n = 16 + t * 2 + i
            local.append(pltpu.make_async_copy(ref.at[:, head_cols(kv, t)], sets.at[t, 0, i, my_rows, :], ls.at[n]))
        for i, ref in ((0, rk_hbm), (1, rv_hbm)):
            n = 20 + t * 2 + i
            local.append(pltpu.make_async_copy(ref.at[:, t * HD:(t + 1) * HD], r_kv.at[i, t], ls.at[n]))
    for c in local:
        c.start()

    peers = [{"kv": kvat(d)} for d in (1, 2, 3)] + [zat(d) for d in (1, 2, 3)]
    peers += [yat(d) for d in (1, 2, 3)] + [xp]
    barrier = pltpu.get_barrier_semaphore()
    for peer in peers:
        pl.semaphore_signal(barrier, inc=1, device_id=peer, device_id_type=MESH)
    pl.semaphore_wait(barrier, len(peers))

    def cp(src, dst, ssem, rsem, dev):
        return pltpu.make_async_remote_copy(
            src_ref=src, dst_ref=dst, send_sem=ssem, recv_sem=rsem, device_id=dev, device_id_type=MESH
        )

    def spread(t):
        made = []
        for d in (1, 2, 3):
            for i, ref in ((0, pk_hbm), (1, pv_hbm)):
                n = (d - 1) * 2 + i
                made.append(
                    cp(ref.at[:, head_cols(kvat(d), t)], sets.at[t, 0, i, my_rows, :],
                       a2a_s.at[t, n], a2a_r.at[t, n], {"kv": kvat(d)})
                )
        return made

    lo, hi = pl.ds(0, 128), pl.ds(128, 128)

    def moved(t, n, src, dst, dev, rows=None):
        a, b = sets.at[t, src], sets.at[t, dst]
        if rows is not None:
            a, b = a.at[:, rows], b.at[:, rows]
        return cp(a, b, gs.at[t, n], gr.at[t, n], dev)

    to_x = lambda t: moved(t, 0, 0, 3, xp)
    to_p = lambda t: moved(t, 1, 0, 1, zp)
    to_m = lambda t: moved(t, 2, 0, 2, zm)
    on_p = lambda t: moved(t, 3, 1, 4, zp, lo)
    on_m = lambda t: moved(t, 4, 2, 4, zm, hi)
    xto_p = lambda t: moved(t, 5, 3, 6, zp)
    xto_m = lambda t: moved(t, 6, 3, 5, zm)
    far = lambda t: moved(t, 7, 4, 7, xp)
    gather = [to_x, to_p, to_m, on_p, on_m, xto_p, xto_m, far]
    w_x = cp(w_own.at[0], w_in.at[0], ws.at[0], wr.at[0], xp)
    w_z = [cp(w_own.at[1], w_in.at[d], ws.at[d], wr.at[d], zat(d)) for d in (1, 2, 3)]
    w_y = [cp(w_own.at[2], w_in.at[3 + d], ws.at[3 + d], wr.at[3 + d], yat(d)) for d in (1, 2, 3)]
    def summed(t, n, src, dst, dev):
        return cp(src, dst, hs.at[t, n], hr.at[t, n], dev)

    far_sum = lambda t: summed(t, 0, out_buf.at[t, 7], far_in.at[t], xp)
    half_p = lambda t: summed(t, 1, out_buf.at[t, 4, :, :, lo], half_in.at[t, 0], zp)
    half_m = lambda t: summed(t, 2, out_buf.at[t, 4, :, :, hi], half_in.at[t, 1], zm)
    plane_p = lambda t: summed(t, 3, out_buf.at[t, 5], plane_in.at[t, 0], zp)
    plane_m = lambda t: summed(t, 4, out_buf.at[t, 6], plane_in.at[t, 1], zm)
    z_p = lambda t: summed(t, 5, out_buf.at[t, 2], z_in.at[t, 0], zp)
    z_m = lambda t: summed(t, 6, out_buf.at[t, 1], z_in.at[t, 1], zm)
    x_sum = lambda t: summed(t, 7, out_buf.at[t, 3], x_in.at[t], xp)
    sums = [far_sum, half_p, half_m, plane_p, plane_m, z_p, z_m, x_sum]

    def to_owner(t, d):
        rows = pl.ds(pl.multiple_of(kvat(d) * 64, 64), 64)
        return cp(own.at[t, :, rows, :], fin.at[t, d], ks.at[t, d], kr.at[t, d], {"kv": kvat(d)})

    for c in spread(0):
        c.start()
    w_own[0] = jnp.full((8, 128), rl_ref[0, 0].astype(F32))
    w_x.start()
    for c in local:
        c.wait()

    live = jnp.where(lax.broadcasted_iota(jnp.int32, (HD, SLOTS), 1) < rl_ref[0, 0], 1.0, 0.0).astype(BF)

    def stage_queries(i, _):
        for u in range(2):
            for v in range(2):
                h = i * 4 + u * 2 + v
                half = slice(v * HD, (v + 1) * HD)
                q_t[h] = ds_ref[i * 2 + u, 0:256, half].T
                d_t[h] = ds_ref[i * 2 + u, 256:512, half].T * live
        return 0

    lax.fori_loop(0, HEADS // 4, stage_queries, 0)
    for t in range(2):
        k_n[t, RESP_AT:, :] = r_kv[0, t]
        k_t[t, :, RESP_AT:] = r_kv[0, t].T
        v_t[t, 0:HD, RESP_AT:] = r_kv[1, t].T
        v_t[t, HD:, RESP_AT:] = jnp.ones((16, SET), BF)

    plen = pl_ref[0]

    def valid_keys(s, shape, axis):
        dx, dz = SETS[s]
        owner = (xh if dx == 0 else 1 - xh) * 4 + (z + dz) % 4
        r = lax.broadcasted_iota(jnp.int32, shape, axis)
        return jnp.where((r // 64) * 512 + r % 64 < plen - owner * 64, 1.0, 0.0).astype(BF)

    def put_set(t, s):
        by_row = valid_keys(s, (SET, HD), 0)
        by_col = valid_keys(s, (16, SET), 1)
        start = (s - 1) * SET if s else OWN_AT
        at = slice(start, start + SET)
        k = sets[t, s, 0]
        k_n[t, at, :] = k * by_row + k[0:1, :] * (1 - by_row)
        k_t[t, :, at] = k.T * by_col[0:1, :]
        v_t[t, 0:HD, at] = sets[t, s, 1].T * by_col[0:1, :]
        v_t[t, HD:, at] = by_col

    s_bufs, ds_bufs, dc_bufs = (s_a, s_b), (ds_a, ds_b), (dc_a, dc_b)

    def scores(t, j, u, rows, at, mask):
        h = t * QPG + u
        s_ref = s_bufs[u % 2]
        top = None
        for r in range(0, rows, 256):
            s = dot(k_n[t, pl.ds(at + r, 256), :], q_t[h], NN) * (SCALE * LOG2E)
            if mask is not None and r:
                s = jnp.where(mask, s, -1e30)
            s_ref[r:r + 256, :] = s
            b = jnp.max(s.reshape(32, 8, SLOTS), 0)
            top = b if top is None else jnp.maximum(top, b)
        m = jnp.max(top, 0, keepdims=True)
        mc[j, h] = m if mask is not None else jnp.maximum(mc[j - 1, h], m)

    def attend(t, j, u, rows, at, first):
        h = t * QPG + u
        s_ref = s_bufs[u % 2]
        m = mc[j, h]
        parts = []
        for r in range(0, rows, 256):
            p = jnp.exp2(s_ref[r:r + 256, :] - m).astype(BF)
            p_ref[h, pl.ds(at + r, 256), :] = p
            parts.append(p)
        new = dot(v_t[t, :, pl.ds(at, rows)], cat(parts, 0), NN)
        o_acc[h] = new if first else o_acc[h] * jnp.exp2(mc[j - 1, h] - m) + new

    def forward(t, j, rows, at, mask):
        for u in range(QPG + 1):
            if u < QPG:
                scores(t, j, u, rows, at, mask)
            if u > 0:
                attend(t, j, u - 1, rows, at, mask is not None)

    def weigh(t, j, u, rows, at, values):
        h = t * QPG + u
        corr = jnp.exp2(mc[j, h] - lse[h])
        dc = (d_t[h].astype(F32) * corr).astype(BF)
        dc_bufs[u % 2][...] = dc
        cd = corr * delta[h]
        for r in range(0, rows, 256):
            dp = dot(values(r), dc, NN) - cd
            ds = p_ref[h, pl.ds(at + r, 256), :] * dp.astype(BF)
            ds_bufs[u % 2][r:r + 256, :] = ds
            ds_ref[h, pl.ds(at + r, 256), :] = ds

    def key_sums(t, u, rows, at):
        h = t * QPG + u
        for r in range(0, rows, 256):
            dv = dot(dc_bufs[u % 2][...], p_ref[h, pl.ds(at + r, 256), :], NT)
            dk = dot(q_t[h], ds_bufs[u % 2][r:r + 256, :], NT)
            if u == 0:
                dv_acc[:, r:r + 256] = dv
                dk_acc[:, r:r + 256] = dk
            else:
                dv_acc[:, r:r + 256] += dv
                dk_acc[:, r:r + 256] += dk

    def backward(t, j, rows, at, values):
        for u in range(QPG + 1):
            if u < QPG:
                weigh(t, j, u, rows, at, values)
            if u > 0:
                key_sums(t, u - 1, rows, at)

    def query_sums(t):
        for u in range(QPG):
            h = t * QPG + u
            dq = dot(k_t[t], ds_ref[h], NN) * (w2 * SCALE)
            p_ref[t * 4 + u // 2, 0:256, (u % 2) * HD:(u % 2 + 1) * HD] = dq.astype(BF).T

    for c in spread(0):
        c.wait_recv()
    for c in (to_x, to_p, to_m):
        c(0).start()
    for c in spread(1):
        c.start()
    row_at = lax.broadcasted_iota(jnp.int32, (SET, SLOTS), 0)
    slot_at = lax.broadcasted_iota(jnp.int32, (SET, SLOTS), 1)
    causal = (row_at <= slot_at) & (row_at < rl_ref[0, 0])

    def first_chunk(t, _):
        @pl.when(t == 1)
        def _():
            for c in spread(1):
                c.wait_recv()

        put_set(t, 0)
        forward(t, 0, PC, OWN_AT, causal)
        return 0

    lax.fori_loop(0, 2, first_chunk, 0)
    w_x.wait_recv()
    w_own[1] = w_own[0] + w_in[0]
    for c in w_z:
        c.start()

    def owner_sum(t):
        z_p(t).wait_recv()
        z_m(t).wait_recv()
        x_sum(t).wait_recv()
        for i in range(2):
            total = out_buf[t, 0, i].astype(F32) + z_in[t, 0, i].astype(F32)
            total = total + (z_in[t, 1, i].astype(F32) + x_in[t, i].astype(F32))
            own[t, i] = total.astype(BF).T
        for d in (1, 2, 3):
            to_owner(t, d).start()

    def plane_sums(t):
        plane_p(t).wait_recv()
        plane_m(t).wait_recv()
        total = plane_in[t, 0].astype(F32) + plane_in[t, 1].astype(F32)
        out_buf[t, 3] = (out_buf[t, 3].astype(F32) + total).astype(BF)
        x_sum(t).start()

    def half_sums(t):
        half_p(t).wait_recv()
        out_buf[t, 2, :, :, 0:128] = (
            out_buf[t, 2, :, :, 0:128].astype(F32) + half_in[t, 0].astype(F32)
        ).astype(BF)
        z_p(t).start()
        half_m(t).wait_recv()
        out_buf[t, 1, :, :, 128:256] = (
            out_buf[t, 1, :, :, 128:256].astype(F32) + half_in[t, 1].astype(F32)
        ).astype(BF)
        z_m(t).start()

    def far_sums(t):
        far_sum(t).wait_recv()
        out_buf[t, 4] = (out_buf[t, 4].astype(F32) + far_in[t].astype(F32)).astype(BF)
        half_p(t).start()
        half_m(t).start()

    def fwd_chunk(t, c):
        first = t == 0

        @pl.when(c == 1)
        def _():
            @pl.when(first)
            def _():
                to_p(0).wait_recv()
                on_p(0).start()
                to_m(0).wait_recv()
                on_m(0).start()
                to_x(0).wait_recv()
                xto_p(0).start()
                xto_m(0).start()

            put_set(t, 1)
            put_set(t, 2)

        @pl.when(c == 2)
        def _():
            @pl.when(first)
            def _():
                on_p(0).wait_recv()
                on_m(0).wait_recv()
                far(0).start()
                for w in w_z:
                    w.wait_recv()
                w_own[2] = w_own[1] + (w_in[1] + w_in[2] + w_in[3])
                for w in w_y:
                    w.start()

            @pl.when(jnp.logical_not(first))
            def _():
                plane_sums(0)

            put_set(t, 3)
            put_set(t, 4)

        @pl.when(c == 3)
        def _():
            xto_p(t).wait_recv()
            xto_m(t).wait_recv()

            @pl.when(first)
            def _():
                for o in (to_x, to_p, to_m):
                    o(1).start()

            @pl.when(jnp.logical_not(first))
            def _():
                half_sums(0)

            put_set(t, 5)
            put_set(t, 6)

        forward(t, c, PC, pl.multiple_of((c - 1) * PC, PC), None)

    def finish_fwd(t):
        for u in range(QPG):
            h = t * QPG + u
            o = o_acc[h]
            total = o[HD:HD + 1, :]
            out = (o[0:HD, :] * (1.0 / total)).astype(BF)
            o_out[t * 4 + u // 2, :, (u % 2) * HD:(u % 2 + 1) * HD] = out.T
            delta[h] = jnp.sum(out.astype(F32) * d_t[h].astype(F32), 0, keepdims=True)
            lse[h] = mc[4, h] + jnp.log2(total)

    def put_out(t, s, i):
        cols = slice(i * SET, (i + 1) * SET)
        out_buf[t, s, 0] = dk_acc[:, cols].astype(BF)
        out_buf[t, s, 1] = dv_acc[:, cols].astype(BF)

    def bwd_chunk(t, c):
        first = t == 0

        @pl.when((c == 3) & first)
        def _():
            to_p(1).wait_recv()
            on_p(1).start()
            to_m(1).wait_recv()
            on_m(1).start()
            to_x(1).wait_recv()
            xto_p(1).start()
            xto_m(1).start()

        @pl.when((c == 1) & first)
        def _():
            on_p(1).wait_recv()
            on_m(1).wait_recv()
            far(1).start()

        backward(t, c, PC, pl.multiple_of((c - 1) * PC, PC), lambda r: sets[t, 2 * c - 1 + r // SET, 1])
        put_out(t, 2 * c - 1, 0)
        put_out(t, 2 * c, 1)

        @pl.when(c == 3)
        def _():
            plane_p(t).start()
            plane_m(t).start()

        @pl.when(c == 1)
        def _():
            far_sums(t)

    def own_chunk(t):
        backward(t, 0, PC, OWN_AT, lambda r: sets[t, 0, 1] if r == 0 else r_kv[1, t])
        put_out(t, 0, 0)
        head = slice(t * HD, (t + 1) * HD)
        drk_ref[:, head] = (dk_acc[:, SET:] * (w2 * SCALE)).T.astype(BF)
        drv_ref[:, head] = (dv_acc[:, SET:] * w2).T.astype(BF)

    def o_copy(i):
        return pltpu.make_async_copy(o_out.at[i], o_hbm.at[:, pair(i)], ls.at[i])

    def both(t, _):
        lax.fori_loop(1, 4, lambda c, _: (fwd_chunk(t, c), 0)[1], 0)
        far(t).wait_recv()
        put_set(t, 7)
        forward(t, 4, SET, LAST_AT, None)
        finish_fwd(t)
        backward(t, 4, SET, LAST_AT, lambda r: sets[t, 7, 1])
        put_out(t, 7, 0)
        far_sum(t).start()
        lax.fori_loop(0, 3, lambda i, _: (bwd_chunk(t, 3 - i), 0)[1], 0)
        return 0

    lax.fori_loop(0, 2, both, 0)
    for i in range(8):
        o_copy(i).start()
    for w in w_y:
        w.wait_recv()
    count = w_own[2] + (w_in[4] + w_in[5] + w_in[6])
    weight = (8192.0 / count)[0:1, :]
    w2 = cat([weight, weight], 1)

    own_chunk(1)
    plane_sums(1)
    half_sums(1)
    own_chunk(0)
    owner_sum(0)

    def dq_copy(i):
        return pltpu.make_async_copy(p_ref.at[i, 0:256, :], dq_hbm.at[:, pair(i)], ls.at[8 + i])

    for t in range(2):
        query_sums(t)
        for i in range(t * 4, t * 4 + 4):
            dq_copy(i).start()
    owner_sum(1)

    mine = lax.broadcasted_iota(jnp.int32, (64, HD), 0) + (kv * 8 + grp) * 64 < plen
    for t in range(2):
        for d in range(4):
            cols = head_cols(kvat(4 - d), t)
            if d == 0:
                got_k, got_v = own[t, 0, my_rows, :], own[t, 1, my_rows, :]
            else:
                to_owner(t, d).wait_recv()
                got_k, got_v = fin[t, d, 0], fin[t, d, 1]
            dpk_ref[:, cols] = jnp.where(mine, got_k.astype(F32) * (weight * SCALE), 0.0)
            dpv_ref[:, cols] = jnp.where(mine, got_v.astype(F32) * weight, 0.0)

    for t in range(2):
        for c in spread(t) + [g(t) for g in gather] + [s(t) for s in sums] + [to_owner(t, d) for d in (1, 2, 3)]:
            c.wait_send()
    for c in [w_x] + w_z + w_y:
        c.wait_send()
    for i in range(8):
        o_copy(i).wait()
        dq_copy(i).wait()


def hand_over(*refs):
    n = len(refs) // 2
    sems = refs[-1]
    copies = [pltpu.make_async_copy(refs[i], refs[n + i], sems.at[i]) for i in range(n)]
    for c in copies:
        c.start()
    for c in copies:
        c.wait()


def on_device(
    queries, resp_keys, resp_values, prompt_keys, prompt_values, grad_out, resp_len, prompt_len
):
    vm = pl.BlockSpec(memory_space=pltpu.VMEM)
    sm = pl.BlockSpec(memory_space=pltpu.SMEM)
    hbm = pl.BlockSpec(memory_space=pl.ANY)
    shape = jax.ShapeDtypeStruct
    dma = pltpu.SemaphoreType.DMA
    shapes = [
        shape((256, 2048), BF), shape((256, 2048), BF), shape((256, 256), BF), shape((256, 256), BF),
        shape((64, 1024), F32), shape((64, 1024), F32),
    ]
    outs = pl.pallas_call(
        kernel,
        out_shape=shapes,
        in_specs=[sm, sm] + [hbm] * 6,
        out_specs=[hbm, hbm] + [vm] * 4,
        scratch_shapes=[
            pltpu.VMEM((2, 8, 2, SET, HD), BF),
            pltpu.VMEM((HEADS, KEYS, SLOTS), BF),
            pltpu.VMEM((HEADS, KEYS, SLOTS), BF),
            pltpu.VMEM((HEADS, HD + 16, SLOTS), F32),
            pltpu.VMEM((8, SLOTS, 256), BF),
            pltpu.VMEM((5, HEADS, 1, SLOTS), F32),
            pltpu.VMEM((HEADS, 1, SLOTS), F32),
            pltpu.VMEM((HEADS, 1, SLOTS), F32),
            pltpu.VMEM((2, KEYS, HD), BF),
            pltpu.VMEM((2, HD, KEYS), BF),
            pltpu.VMEM((2, HD + 16, KEYS), BF),
            pltpu.VMEM((2, 2, SET, HD), BF),
            pltpu.VMEM((HEADS, HD, SLOTS), BF),
            pltpu.VMEM((HEADS, HD, SLOTS), BF),
            pltpu.VMEM((PC, SLOTS), F32),
            pltpu.VMEM((PC, SLOTS), F32),
            pltpu.VMEM((PC, SLOTS), BF),
            pltpu.VMEM((PC, SLOTS), BF),
            pltpu.VMEM((HD, SLOTS), BF),
            pltpu.VMEM((HD, SLOTS), BF),
            pltpu.VMEM((HD, PC), F32),
            pltpu.VMEM((HD, PC), F32),
            pltpu.VMEM((2, 8, 2, HD, SET), BF),
            pltpu.VMEM((2, 2, SET, HD), BF),
            pltpu.VMEM((2, 2, 2, HD, 128), BF),
            pltpu.VMEM((2, 2, 2, HD, SET), BF),
            pltpu.VMEM((2, 2, 2, HD, SET), BF),
            pltpu.VMEM((2, 2, HD, SET), BF),
            pltpu.VMEM((2, 2, HD, SET), BF),
            pltpu.VMEM((2, 4, 2, 64, HD), BF),
            pltpu.VMEM((3, 8, 128), F32),
            pltpu.VMEM((7, 8, 128), F32),
            dma((24,)), dma((2, 6)), dma((2, 6)), dma((2, 8)), dma((2, 8)), dma((2, 8)), dma((2, 8)),
            dma((2, 4)), dma((2, 4)), dma((7,)), dma((7,)),
        ],
        compiler_params=pltpu.CompilerParams(
            collective_id=0, has_side_effects=True, vmem_limit_bytes=62 * 2**20
        ),
        name="attention",
    )(
        resp_len, prompt_len, queries.reshape(256, 2048), grad_out.reshape(256, 2048),
        resp_keys.reshape(256, 256), resp_values.reshape(256, 256),
        prompt_keys.reshape(64, 1024), prompt_values.reshape(64, 1024),
    )
    attended, grad_q, grad_rk, grad_rv, grad_pk, grad_pv = pl.pallas_call(
        hand_over,
        out_shape=shapes,
        in_specs=[vm] * 6,
        out_specs=[hbm] * 6,
        scratch_shapes=[dma((6,))],
        name="hand_over",
    )(*outs)
    return (
        attended.reshape(queries.shape),
        grad_q.reshape(queries.shape),
        grad_rk.reshape(resp_keys.shape),
        grad_rv.reshape(resp_values.shape),
        grad_pk.reshape(1, 64, 1024),
        grad_pv.reshape(1, 64, 1024),
    )


def solution(mesh):
    wide = P("prompt", "grp", None, "kv")
    rows = P("prompt", ("kv", "grp"), None)
    return jax.shard_map(
        on_device,
        mesh=mesh,
        in_specs=(wide, wide, wide, rows, rows, wide, P("prompt", "grp"), P("prompt")),
        out_specs=(wide, wide, wide, wide, rows, rows),
        check_vma=False,
    )
```

```python
import jax
import jax.numpy as jnp
from jax import lax
from jax.experimental import pallas as pl
from jax.experimental.pallas import tpu as pltpu
from jax.sharding import PartitionSpec as P

F32 = jnp.float32
BF = jnp.bfloat16
MESH = pl.DeviceIdType.MESH
HD = 128
QPG = 8
SCALE = HD ** (-0.5)
LOG2E = 1.4426950408889634
NT = (((1,), (1,)), ((), ()))
NN = (((1,), (0,)), ((), ()))
SET = 256
PC = 512
HEADS = 16
SLOTS = 256
RESP_AT = 2048
KEYS = 2304
OWN_AT = 1792
LAST_AT = 1536
SETS = ((0, 0), (0, 3), (0, 1), (1, 0), (0, 2), (1, 1), (1, 3), (1, 2))


def dot(a, b, dims):
    return lax.dot_general(a, b, dims, preferred_element_type=F32)


def cat(parts, axis):
    return parts[0] if len(parts) == 1 else jnp.concatenate(parts, axis)


def kernel(
    rl_ref, pl_ref, q_hbm, do_hbm, rk_hbm, rv_hbm, pk_hbm, pv_hbm,
    o_hbm, dq_hbm, drk_ref, drv_ref, dpk_ref, dpv_ref,
    sets, p_ref, ds_ref, o_acc, o_out, mc, lse, delta, k_n, k_t, v_t, r_kv, q_t, d_t,
    s_a, s_b, ds_a, ds_b, dc_a, dc_b, dk_acc, dv_acc,
    out_buf, own, half_in, plane_in, z_in, x_in, far_in, fin, w_own, w_in,
    ls, a2a_s, a2a_r, gs, gr, hs, hr, ks, kr, ws, wr,
):
    kv = lax.axis_index("kv")
    grp = lax.axis_index("grp")
    prm = lax.axis_index("prompt")
    xh = grp // 4
    z = grp % 4
    zat = lambda d: {"grp": xh * 4 + (z + d) % 4}
    zp, zm, xp = zat(1), zat(3), {"grp": (1 - xh) * 4 + z}
    kvat = lambda d: (kv + d) % 4
    yat = lambda d: {"prompt": (prm + d) % 4}
    my_rows = pl.ds(pl.multiple_of(kv * 64, 64), 64)
    head_cols = lambda who, t: pl.ds(pl.multiple_of(who * 256 + t * HD, HD), HD)

    pair = lambda i: pl.ds(i * 256, 256)
    local = []
    for i in range(8):
        local.append(pltpu.make_async_copy(q_hbm.at[:, pair(i)], ds_ref.at[i, 0:256, :], ls.at[i]))
        local.append(pltpu.make_async_copy(do_hbm.at[:, pair(i)], ds_ref.at[i, 256:512, :], ls.at[8 + i]))
    for t in range(2):
        for i, ref in ((0, pk_hbm), (1, pv_hbm)):
            n = 16 + t * 2 + i
            local.append(pltpu.make_async_copy(ref.at[:, head_cols(kv, t)], sets.at[t, 0, i, my_rows, :], ls.at[n]))
        for i, ref in ((0, rk_hbm), (1, rv_hbm)):
            n = 20 + t * 2 + i
            local.append(pltpu.make_async_copy(ref.at[:, t * HD:(t + 1) * HD], r_kv.at[i, t], ls.at[n]))
    for c in local:
        c.start()

    peers = [{"kv": kvat(d)} for d in (1, 2, 3)] + [zat(d) for d in (1, 2, 3)]
    peers += [yat(d) for d in (1, 2, 3)] + [xp]
    barrier = pltpu.get_barrier_semaphore()
    for peer in peers:
        pl.semaphore_signal(barrier, inc=1, device_id=peer, device_id_type=MESH)
    pl.semaphore_wait(barrier, len(peers))

    def cp(src, dst, ssem, rsem, dev):
        return pltpu.make_async_remote_copy(
            src_ref=src, dst_ref=dst, send_sem=ssem, recv_sem=rsem, device_id=dev, device_id_type=MESH
        )

    def spread(t, i):
        ref = (pk_hbm, pv_hbm)[i]
        return [
            cp(ref.at[:, head_cols(kvat(d), t)], sets.at[t, 0, i, my_rows, :],
               a2a_s.at[t, i, d], a2a_r.at[t, i, d], {"kv": kvat(d)})
            for d in (1, 2, 3)
        ]

    lo, hi = pl.ds(0, 128), pl.ds(128, 128)

    def moved(t, i, n, src, dst, dev, rows=None):
        a, b = sets.at[t, src, i], sets.at[t, dst, i]
        if rows is not None:
            a, b = a.at[rows], b.at[rows]
        return cp(a, b, gs.at[t, i, n], gr.at[t, i, n], dev)

    to_x = lambda t, i: moved(t, i, 0, 0, 3, xp)
    to_p = lambda t, i: moved(t, i, 1, 0, 1, zp)
    to_m = lambda t, i: moved(t, i, 2, 0, 2, zm)
    on_p = lambda t, i: moved(t, i, 3, 1, 4, zp, lo)
    on_m = lambda t, i: moved(t, i, 4, 2, 4, zm, hi)
    xto_p = lambda t, i: moved(t, i, 5, 3, 6, zp)
    xto_m = lambda t, i: moved(t, i, 6, 3, 5, zm)
    far = lambda t, i: moved(t, i, 7, 4, 7, xp)
    gather = [to_x, to_p, to_m, on_p, on_m, xto_p, xto_m, far]
    w_x = cp(w_own.at[0], w_in.at[0], ws.at[0], wr.at[0], xp)
    w_z = [cp(w_own.at[1], w_in.at[d], ws.at[d], wr.at[d], zat(d)) for d in (1, 2, 3)]
    w_y = [cp(w_own.at[2], w_in.at[3 + d], ws.at[3 + d], wr.at[3 + d], yat(d)) for d in (1, 2, 3)]
    def summed(t, i, n, src, dst, dev):
        return cp(src, dst, hs.at[t, i, n], hr.at[t, i, n], dev)

    far_sum = lambda t, i: summed(t, i, 0, out_buf.at[t, 7, i], far_in.at[t, i], xp)
    half_p = lambda t, i: summed(t, i, 1, out_buf.at[t, 4, i, :, lo], half_in.at[t, 0, i], zp)
    half_m = lambda t, i: summed(t, i, 2, out_buf.at[t, 4, i, :, hi], half_in.at[t, 1, i], zm)
    plane_p = lambda t, i: summed(t, i, 3, out_buf.at[t, 5, i], plane_in.at[t, 0, i], zp)
    plane_m = lambda t, i: summed(t, i, 4, out_buf.at[t, 6, i], plane_in.at[t, 1, i], zm)
    z_p = lambda t, i: summed(t, i, 5, out_buf.at[t, 2, i], z_in.at[t, 0, i], zp)
    z_m = lambda t, i: summed(t, i, 6, out_buf.at[t, 1, i], z_in.at[t, 1, i], zm)
    x_sum = lambda t, i: summed(t, i, 7, out_buf.at[t, 3, i], x_in.at[t, i], xp)
    sums = [far_sum, half_p, half_m, plane_p, plane_m, z_p, z_m, x_sum]

    def to_owner(t, i, d):
        rows = pl.ds(pl.multiple_of(kvat(d) * 64, 64), 64)
        return cp(own.at[t, i, rows, :], fin.at[t, d, i], ks.at[t, i, d], kr.at[t, i, d], {"kv": kvat(d)})

    for i in range(2):
        for c in spread(0, i):
            c.start()
    w_own[0] = jnp.full((8, 128), rl_ref[0, 0].astype(F32))
    w_x.start()
    for c in local:
        c.wait()

    live = jnp.where(lax.broadcasted_iota(jnp.int32, (HD, SLOTS), 1) < rl_ref[0, 0], 1.0, 0.0).astype(BF)

    def stage_queries(i, _):
        for u in range(2):
            for v in range(2):
                h = i * 4 + u * 2 + v
                half = slice(v * HD, (v + 1) * HD)
                q_t[h] = ds_ref[i * 2 + u, 0:256, half].T
                d_t[h] = ds_ref[i * 2 + u, 256:512, half].T * live
        return 0

    lax.fori_loop(0, HEADS // 4, stage_queries, 0)
    for t in range(2):
        k_n[t, RESP_AT:, :] = r_kv[0, t]
        k_t[t, :, RESP_AT:] = r_kv[0, t].T
        v_t[t, 0:HD, RESP_AT:] = r_kv[1, t].T
        v_t[t, HD:, RESP_AT:] = jnp.ones((16, SET), BF)

    plen = pl_ref[0]

    def valid_keys(s, shape, axis):
        dx, dz = SETS[s]
        owner = (xh if dx == 0 else 1 - xh) * 4 + (z + dz) % 4
        r = lax.broadcasted_iota(jnp.int32, shape, axis)
        return jnp.where((r // 64) * 512 + r % 64 < plen - owner * 64, 1.0, 0.0).astype(BF)

    def put_set(t, s):
        by_row = valid_keys(s, (SET, HD), 0)
        by_col = valid_keys(s, (16, SET), 1)
        start = (s - 1) * SET if s else OWN_AT
        at = slice(start, start + SET)
        k = sets[t, s, 0]
        k_n[t, at, :] = k * by_row + k[0:1, :] * (1 - by_row)
        k_t[t, :, at] = k.T * by_col[0:1, :]
        v_t[t, 0:HD, at] = sets[t, s, 1].T * by_col[0:1, :]
        v_t[t, HD:, at] = by_col

    s_bufs, ds_bufs, dc_bufs = (s_a, s_b), (ds_a, ds_b), (dc_a, dc_b)

    def scores(t, j, u, rows, at, mask):
        h = t * QPG + u
        s_ref = s_bufs[u % 2]
        top = None
        for r in range(0, rows, 256):
            s = dot(k_n[t, pl.ds(at + r, 256), :], q_t[h], NN) * (SCALE * LOG2E)
            if mask is not None and r:
                s = jnp.where(mask, s, -1e30)
            s_ref[r:r + 256, :] = s
            b = jnp.max(s.reshape(32, 8, SLOTS), 0)
            top = b if top is None else jnp.maximum(top, b)
        m = jnp.max(top, 0, keepdims=True)
        mc[j, h] = m if mask is not None else jnp.maximum(mc[j - 1, h], m)

    def attend(t, j, u, rows, at, first):
        h = t * QPG + u
        s_ref = s_bufs[u % 2]
        m = mc[j, h]
        parts = []
        for r in range(0, rows, 256):
            p = jnp.exp2(s_ref[r:r + 256, :] - m).astype(BF)
            p_ref[h, pl.ds(at + r, 256), :] = p
            parts.append(p)
        new = dot(v_t[t, :, pl.ds(at, rows)], cat(parts, 0), NN)
        o_acc[h] = new if first else o_acc[h] * jnp.exp2(mc[j - 1, h] - m) + new

    def forward(t, j, rows, at, mask):
        for u in range(QPG + 1):
            if u < QPG:
                scores(t, j, u, rows, at, mask)
            if u > 0:
                attend(t, j, u - 1, rows, at, mask is not None)

    def weigh(t, j, u, rows, at, values):
        h = t * QPG + u
        corr = jnp.exp2(mc[j, h] - lse[h])
        dc = (d_t[h].astype(F32) * corr).astype(BF)
        dc_bufs[u % 2][...] = dc
        cd = corr * delta[h]
        for r in range(0, rows, 256):
            dp = dot(values(r), dc, NN) - cd
            ds = p_ref[h, pl.ds(at + r, 256), :] * dp.astype(BF)
            ds_bufs[u % 2][r:r + 256, :] = ds
            ds_ref[h, pl.ds(at + r, 256), :] = ds

    def key_sums(t, u, rows, at):
        h = t * QPG + u
        for r in range(0, rows, 256):
            dv = dot(dc_bufs[u % 2][...], p_ref[h, pl.ds(at + r, 256), :], NT)
            dk = dot(q_t[h], ds_bufs[u % 2][r:r + 256, :], NT)
            if u == 0:
                dv_acc[:, r:r + 256] = dv
                dk_acc[:, r:r + 256] = dk
            else:
                dv_acc[:, r:r + 256] += dv
                dk_acc[:, r:r + 256] += dk

    def backward(t, j, rows, at, values):
        for u in range(QPG + 1):
            if u < QPG:
                weigh(t, j, u, rows, at, values)
            if u > 0:
                key_sums(t, u - 1, rows, at)

    def query_sums(t):
        for u in range(QPG):
            h = t * QPG + u
            dq = dot(k_t[t], ds_ref[h], NN) * (w2 * SCALE)
            p_ref[t * 4 + u // 2, 0:256, (u % 2) * HD:(u % 2 + 1) * HD] = dq.astype(BF).T

    for i in range(2):
        for c in spread(0, i):
            c.wait_recv()
        for c in (to_x, to_p, to_m):
            c(0, i).start()
    row_at = lax.broadcasted_iota(jnp.int32, (SET, SLOTS), 0)
    slot_at = lax.broadcasted_iota(jnp.int32, (SET, SLOTS), 1)
    causal = (row_at <= slot_at) & (row_at < rl_ref[0, 0])

    def first_chunk(t):
        put_set(t, 0)
        forward(t, 0, PC, OWN_AT, causal)

    first_chunk(0)
    w_x.wait_recv()
    w_own[1] = w_own[0] + w_in[0]
    for c in w_z:
        c.start()

    def pass_on(t):
        for i in range(2):
            to_p(t, i).wait_recv()
            on_p(t, i).start()
            to_m(t, i).wait_recv()
            on_m(t, i).start()
            to_x(t, i).wait_recv()
            xto_p(t, i).start()
            xto_m(t, i).start()

    def pass_far(t):
        for i in range(2):
            on_p(t, i).wait_recv()
            on_m(t, i).wait_recv()
            far(t, i).start()

    def owner_sum(t):
        for i in range(2):
            z_p(t, i).wait_recv()
            z_m(t, i).wait_recv()
            x_sum(t, i).wait_recv()
            total = out_buf[t, 0, i].astype(F32) + z_in[t, 0, i].astype(F32)
            total = total + (z_in[t, 1, i].astype(F32) + x_in[t, i].astype(F32))
            own[t, i] = total.astype(BF).T
            for d in (1, 2, 3):
                to_owner(t, i, d).start()

    def plane_sums(t, i):
        plane_p(t, i).wait_recv()
        plane_m(t, i).wait_recv()
        total = plane_in[t, 0, i].astype(F32) + plane_in[t, 1, i].astype(F32)
        out_buf[t, 3, i] = (out_buf[t, 3, i].astype(F32) + total).astype(BF)
        x_sum(t, i).start()

    def half_sums(t, i):
        half_p(t, i).wait_recv()
        out_buf[t, 2, i, :, 0:128] = (
            out_buf[t, 2, i, :, 0:128].astype(F32) + half_in[t, 0, i].astype(F32)
        ).astype(BF)
        z_p(t, i).start()
        half_m(t, i).wait_recv()
        out_buf[t, 1, i, :, 128:256] = (
            out_buf[t, 1, i, :, 128:256].astype(F32) + half_in[t, 1, i].astype(F32)
        ).astype(BF)
        z_m(t, i).start()

    def far_sums(t, i):
        far_sum(t, i).wait_recv()
        out_buf[t, 4, i] = (out_buf[t, 4, i].astype(F32) + far_in[t, i].astype(F32)).astype(BF)
        half_p(t, i).start()
        half_m(t, i).start()

    def fwd_chunk(t, c):
        first = t == 0
        second = jnp.logical_not(first)

        @pl.when(c == 1)
        def _():
            @pl.when(first)
            def _():
                pass_on(0)
                for i in range(2):
                    for o in spread(1, i):
                        o.start()

            put_set(t, 1)
            put_set(t, 2)

        @pl.when(c == 2)
        def _():
            @pl.when(first)
            def _():
                for i in range(2):
                    for o in spread(1, i):
                        o.wait_recv()
                first_chunk(1)
                pass_far(0)
                for w in w_z:
                    w.wait_recv()
                w_own[2] = w_own[1] + (w_in[1] + w_in[2] + w_in[3])
                for w in w_y:
                    w.start()

            @pl.when(second)
            def _():
                plane_sums(0, 0)
                plane_sums(0, 1)

            put_set(t, 3)
            put_set(t, 4)

        @pl.when(c == 3)
        def _():
            for i in range(2):
                xto_p(t, i).wait_recv()
                xto_m(t, i).wait_recv()

            @pl.when(first)
            def _():
                for i in range(2):
                    to_p(1, i).start()
                    to_m(1, i).start()

            @pl.when(second)
            def _():
                half_sums(0, 0)
                half_sums(0, 1)

            put_set(t, 5)
            put_set(t, 6)

        forward(t, c, PC, pl.multiple_of((c - 1) * PC, PC), None)

    def last_chunk(t):
        far(t, 0).wait_recv()
        far(t, 1).wait_recv()

        @pl.when(t == 0)
        def _():
            to_x(1, 0).start()
            to_x(1, 1).start()

        put_set(t, 7)
        forward(t, 4, SET, LAST_AT, None)

    def finish_fwd(t):
        for u in range(QPG):
            h = t * QPG + u
            o = o_acc[h]
            total = o[HD:HD + 1, :]
            out = (o[0:HD, :] * (1.0 / total)).astype(BF)
            o_out[t * 4 + u // 2, :, (u % 2) * HD:(u % 2 + 1) * HD] = out.T
            delta[h] = jnp.sum(out.astype(F32) * d_t[h].astype(F32), 0, keepdims=True)
            lse[h] = mc[4, h] + jnp.log2(total)

    def put_out(t, s, i):
        cols = slice(i * SET, (i + 1) * SET)
        out_buf[t, s, 0] = dk_acc[:, cols].astype(BF)
        out_buf[t, s, 1] = dv_acc[:, cols].astype(BF)

    def bwd_chunk(t, c):
        first = t == 0

        @pl.when((c == 3) & first)
        def _():
            pass_on(1)

        @pl.when((c == 1) & first)
        def _():
            pass_far(1)

        backward(t, c, PC, pl.multiple_of((c - 1) * PC, PC), lambda r: sets[t, 2 * c - 1 + r // SET, 1])
        put_out(t, 2 * c - 1, 0)
        put_out(t, 2 * c, 1)

        @pl.when(c == 3)
        def _():
            for i in range(2):
                plane_p(t, i).start()
                plane_m(t, i).start()

        @pl.when(c == 2)
        def _():
            far_sums(t, 0)

        @pl.when(c == 1)
        def _():
            far_sums(t, 1)

    def own_chunk(t):
        backward(t, 0, PC, OWN_AT, lambda r: sets[t, 0, 1] if r == 0 else r_kv[1, t])
        put_out(t, 0, 0)
        head = slice(t * HD, (t + 1) * HD)
        drk_ref[:, head] = (dk_acc[:, SET:] * (w2 * SCALE)).T.astype(BF)
        drv_ref[:, head] = (dv_acc[:, SET:] * w2).T.astype(BF)

    def o_copy(i):
        return pltpu.make_async_copy(o_out.at[i], o_hbm.at[:, pair(i)], ls.at[i])

    def both(t, _):
        lax.fori_loop(1, 4, lambda c, _: (fwd_chunk(t, c), 0)[1], 0)
        last_chunk(t)
        finish_fwd(t)
        backward(t, 4, SET, LAST_AT, lambda r: sets[t, 7, 1])
        put_out(t, 7, 0)
        far_sum(t, 0).start()
        far_sum(t, 1).start()
        lax.fori_loop(0, 3, lambda i, _: (bwd_chunk(t, 3 - i), 0)[1], 0)
        return 0

    lax.fori_loop(0, 2, both, 0)
    for i in range(8):
        o_copy(i).start()
    for w in w_y:
        w.wait_recv()
    count = w_own[2] + (w_in[4] + w_in[5] + w_in[6])
    weight = (8192.0 / count)[0:1, :]
    w2 = cat([weight, weight], 1)

    def dq_copy(i):
        return pltpu.make_async_copy(p_ref.at[i, 0:256, :], dq_hbm.at[:, pair(i)], ls.at[8 + i])

    def finish_queries(t):
        query_sums(t)
        for i in range(t * 4, t * 4 + 4):
            dq_copy(i).start()

    plane_sums(1, 0)
    own_chunk(1)
    half_sums(1, 0)
    plane_sums(1, 1)
    finish_queries(1)
    half_sums(1, 1)
    own_chunk(0)
    owner_sum(0)
    finish_queries(0)
    owner_sum(1)

    mine = lax.broadcasted_iota(jnp.int32, (64, HD), 0) + (kv * 8 + grp) * 64 < plen
    for t in range(2):
        for d in range(4):
            cols = head_cols(kvat(4 - d), t)
            if d == 0:
                got_k, got_v = own[t, 0, my_rows, :], own[t, 1, my_rows, :]
            else:
                to_owner(t, 0, d).wait_recv()
                to_owner(t, 1, d).wait_recv()
                got_k, got_v = fin[t, d, 0], fin[t, d, 1]
            dpk_ref[:, cols] = jnp.where(mine, got_k.astype(F32) * (weight * SCALE), 0.0)
            dpv_ref[:, cols] = jnp.where(mine, got_v.astype(F32) * weight, 0.0)

    for t in range(2):
        for i in range(2):
            for c in spread(t, i) + [g(t, i) for g in gather + sums] + [to_owner(t, i, d) for d in (1, 2, 3)]:
                c.wait_send()
    for c in [w_x] + w_z + w_y:
        c.wait_send()
    for i in range(8):
        o_copy(i).wait()
        dq_copy(i).wait()


def hand_over(*refs):
    ins, outs, held, (in_sem, out_sem) = refs[0:6], refs[6:12], refs[12:18], refs[18:]
    pieces = []
    for i in range(6):
        parts = 4 if i < 2 else 1
        rows = ins[i].shape[0] // parts
        for j in range(parts):
            pieces.append((i, pl.ds(j * rows, rows)))
    into = [
        pltpu.make_async_copy(ins[i].at[r], held[i].at[r], in_sem.at[n]) for n, (i, r) in enumerate(pieces)
    ]
    out = [
        pltpu.make_async_copy(held[i].at[r], outs[i].at[r], out_sem.at[n]) for n, (i, r) in enumerate(pieces)
    ]
    for c in into:
        c.start()
    for a, b in zip(into, out):
        a.wait()
        b.start()
    for c in out:
        c.wait()


def on_device(
    queries, resp_keys, resp_values, prompt_keys, prompt_values, grad_out, resp_len, prompt_len
):
    vm = pl.BlockSpec(memory_space=pltpu.VMEM)
    sm = pl.BlockSpec(memory_space=pltpu.SMEM)
    hbm = pl.BlockSpec(memory_space=pl.ANY)
    shape = jax.ShapeDtypeStruct
    dma = pltpu.SemaphoreType.DMA
    shapes = [
        shape((256, 2048), BF), shape((256, 2048), BF), shape((256, 256), BF), shape((256, 256), BF),
        shape((64, 1024), F32), shape((64, 1024), F32),
    ]
    outs = pl.pallas_call(
        kernel,
        out_shape=shapes,
        in_specs=[sm, sm] + [hbm] * 6,
        out_specs=[hbm, hbm] + [vm] * 4,
        scratch_shapes=[
            pltpu.VMEM((2, 8, 2, SET, HD), BF),
            pltpu.VMEM((HEADS, KEYS, SLOTS), BF),
            pltpu.VMEM((HEADS, KEYS, SLOTS), BF),
            pltpu.VMEM((HEADS, HD + 16, SLOTS), F32),
            pltpu.VMEM((8, SLOTS, 256), BF),
            pltpu.VMEM((5, HEADS, 1, SLOTS), F32),
            pltpu.VMEM((HEADS, 1, SLOTS), F32),
            pltpu.VMEM((HEADS, 1, SLOTS), F32),
            pltpu.VMEM((2, KEYS, HD), BF),
            pltpu.VMEM((2, HD, KEYS), BF),
            pltpu.VMEM((2, HD + 16, KEYS), BF),
            pltpu.VMEM((2, 2, SET, HD), BF),
            pltpu.VMEM((HEADS, HD, SLOTS), BF),
            pltpu.VMEM((HEADS, HD, SLOTS), BF),
            pltpu.VMEM((PC, SLOTS), F32),
            pltpu.VMEM((PC, SLOTS), F32),
            pltpu.VMEM((PC, SLOTS), BF),
            pltpu.VMEM((PC, SLOTS), BF),
            pltpu.VMEM((HD, SLOTS), BF),
            pltpu.VMEM((HD, SLOTS), BF),
            pltpu.VMEM((HD, PC), F32),
            pltpu.VMEM((HD, PC), F32),
            pltpu.VMEM((2, 8, 2, HD, SET), BF),
            pltpu.VMEM((2, 2, SET, HD), BF),
            pltpu.VMEM((2, 2, 2, HD, 128), BF),
            pltpu.VMEM((2, 2, 2, HD, SET), BF),
            pltpu.VMEM((2, 2, 2, HD, SET), BF),
            pltpu.VMEM((2, 2, HD, SET), BF),
            pltpu.VMEM((2, 2, HD, SET), BF),
            pltpu.VMEM((2, 4, 2, 64, HD), BF),
            pltpu.VMEM((3, 8, 128), F32),
            pltpu.VMEM((7, 8, 128), F32),
            dma((24,)), dma((2, 2, 4)), dma((2, 2, 4)), dma((2, 2, 8)), dma((2, 2, 8)), dma((2, 2, 8)), dma((2, 2, 8)),
            dma((2, 2, 4)), dma((2, 2, 4)), dma((7,)), dma((7,)),
        ],
        compiler_params=pltpu.CompilerParams(
            collective_id=0, has_side_effects=True, vmem_limit_bytes=62 * 2**20
        ),
        name="attention",
    )(
        resp_len, prompt_len, queries.reshape(256, 2048), grad_out.reshape(256, 2048),
        resp_keys.reshape(256, 256), resp_values.reshape(256, 256),
        prompt_keys.reshape(64, 1024), prompt_values.reshape(64, 1024),
    )
    attended, grad_q, grad_rk, grad_rv, grad_pk, grad_pv = pl.pallas_call(
        hand_over,
        out_shape=shapes,
        in_specs=[hbm] * 6,
        out_specs=[hbm] * 6,
        scratch_shapes=[pltpu.VMEM(a.shape, a.dtype) for a in shapes] + [dma((12,)), dma((12,))],
        name="hand_over",
    )(*outs)
    return (
        attended.reshape(queries.shape),
        grad_q.reshape(queries.shape),
        grad_rk.reshape(resp_keys.shape),
        grad_rv.reshape(resp_values.shape),
        grad_pk.reshape(1, 64, 1024),
        grad_pv.reshape(1, 64, 1024),
    )


def solution(mesh):
    wide = P("prompt", "grp", None, "kv")
    rows = P("prompt", ("kv", "grp"), None)
    return jax.shard_map(
        on_device,
        mesh=mesh,
        in_specs=(wide, wide, wide, rows, rows, wide, P("prompt", "grp"), P("prompt")),
        out_specs=(wide, wide, wide, wide, rows, rows),
        check_vma=False,
    )
```

```python
import jax
import jax.numpy as jnp
from jax import lax
from jax.experimental import pallas as pl
from jax.experimental.pallas import tpu as pltpu
from jax.sharding import PartitionSpec as P

F32 = jnp.float32
BF = jnp.bfloat16
MESH = pl.DeviceIdType.MESH
HD = 128
QPG = 8
SCALE = HD ** (-0.5)
LOG2E = 1.4426950408889634
NT = (((1,), (1,)), ((), ()))
NN = (((1,), (0,)), ((), ()))
SET = 256
PC = 512
HEADS = 16
SLOTS = 256
RESP_AT = 2048
KEYS = 2304
OWN_AT = 1792
LAST_AT = 1536
SETS = ((0, 0), (0, 3), (0, 1), (1, 0), (0, 2), (1, 1), (1, 3), (1, 2))


def dot(a, b, dims):
    return lax.dot_general(a, b, dims, preferred_element_type=F32)


def cat(parts, axis):
    return parts[0] if len(parts) == 1 else jnp.concatenate(parts, axis)


def kernel(
    rl_ref, pl_ref, q_hbm, do_hbm, rk_hbm, rv_hbm, pk_hbm, pv_hbm,
    o_hbm, dq_hbm, drk_ref, drv_ref, dpk_ref, dpv_ref,
    sets, p_ref, ds_ref, o_acc, o_out, mc, lse, delta, k_n, k_t, v_t, r_kv, q_t, d_t,
    s_a, s_b, ds_a, ds_b, dc_a, dc_b, dk_acc, dv_acc,
    out_buf, own, half_in, plane_in, z_in, x_in, far_in, fin, w_own, w_in,
    ls, a2a_s, a2a_r, gs, gr, hs, hr, ks, kr, ws, wr,
):
    kv = lax.axis_index("kv")
    grp = lax.axis_index("grp")
    prm = lax.axis_index("prompt")
    xh = grp // 4
    z = grp % 4
    zat = lambda d: {"grp": xh * 4 + (z + d) % 4}
    zp, zm, xp = zat(1), zat(3), {"grp": (1 - xh) * 4 + z}
    kvat = lambda d: (kv + d) % 4
    yat = lambda d: {"prompt": (prm + d) % 4}
    my_rows = pl.ds(pl.multiple_of(kv * 64, 64), 64)
    head_cols = lambda who, t: pl.ds(pl.multiple_of(who * 256 + t * HD, HD), HD)

    pair = lambda i: pl.ds(i * 256, 256)
    local = []
    for i in range(8):
        local.append(pltpu.make_async_copy(q_hbm.at[:, pair(i)], ds_ref.at[i, 0:256, :], ls.at[i]))
        local.append(pltpu.make_async_copy(do_hbm.at[:, pair(i)], ds_ref.at[i, 256:512, :], ls.at[8 + i]))
    for t in range(2):
        for i, ref in ((0, pk_hbm), (1, pv_hbm)):
            n = 16 + t * 2 + i
            local.append(pltpu.make_async_copy(ref.at[:, head_cols(kv, t)], sets.at[t, 0, i, my_rows, :], ls.at[n]))
        for i, ref in ((0, rk_hbm), (1, rv_hbm)):
            n = 20 + t * 2 + i
            local.append(pltpu.make_async_copy(ref.at[:, t * HD:(t + 1) * HD], r_kv.at[i, t], ls.at[n]))
    for c in local:
        c.start()

    peers = [{"kv": kvat(d)} for d in (1, 2, 3)] + [zat(d) for d in (1, 2, 3)]
    peers += [yat(d) for d in (1, 2, 3)] + [xp]
    barrier = pltpu.get_barrier_semaphore()
    for peer in peers:
        pl.semaphore_signal(barrier, inc=1, device_id=peer, device_id_type=MESH)
    pl.semaphore_wait(barrier, len(peers))

    def cp(src, dst, ssem, rsem, dev):
        return pltpu.make_async_remote_copy(
            src_ref=src, dst_ref=dst, send_sem=ssem, recv_sem=rsem, device_id=dev, device_id_type=MESH
        )

    whole = slice(None)
    def spread(t, i):
        ref = (pk_hbm, pv_hbm)[i]
        return [
            cp(ref.at[:, head_cols(kvat(d), t)], sets.at[t, 0, i, my_rows, :],
               a2a_s.at[t, i, d], a2a_r.at[t, i, d], {"kv": kvat(d)})
            for d in (1, 2, 3)
        ]

    lo, hi = pl.ds(0, 128), pl.ds(128, 128)

    def moved(t, i, n, src, dst, dev, rows=None):
        if i is None:
            a, b = sets.at[t, src], sets.at[t, dst]
            if rows is not None:
                a, b = a.at[:, rows], b.at[:, rows]
            return cp(a, b, gs.at[t, 0, n], gr.at[t, 0, n], dev)
        a, b = sets.at[t, src, i], sets.at[t, dst, i]
        if rows is not None:
            a, b = a.at[rows], b.at[rows]
        return cp(a, b, gs.at[t, i, n], gr.at[t, i, n], dev)

    to_x = lambda t, i: moved(t, i, 0, 0, 3, xp)
    to_p = lambda t, i: moved(t, i, 1, 0, 1, zp)
    to_m = lambda t, i: moved(t, i, 2, 0, 2, zm)
    on_p = lambda t, i: moved(t, i, 3, 1, 4, zp, lo)
    on_m = lambda t, i: moved(t, i, 4, 2, 4, zm, hi)
    xto_p = lambda t, i: moved(t, i, 5, 3, 6, zp)
    xto_m = lambda t, i: moved(t, i, 6, 3, 5, zm)
    far = lambda t, i: moved(t, i, 7, 4, 7, xp)
    gather = [to_x, to_p, to_m, on_p, on_m, xto_p, xto_m, far]
    w_x = cp(w_own.at[0], w_in.at[0], ws.at[0], wr.at[0], xp)
    w_z = [cp(w_own.at[1], w_in.at[d], ws.at[d], wr.at[d], zat(d)) for d in (1, 2, 3)]
    w_y = [cp(w_own.at[2], w_in.at[3 + d], ws.at[3 + d], wr.at[3 + d], yat(d)) for d in (1, 2, 3)]
    def summed(t, i, n, src, dst, dev):
        if i is not None:
            src, dst = src.at[i], dst.at[i]
        i = i or 0
        return cp(src, dst, hs.at[t, i, n], hr.at[t, i, n], dev)

    far_sum = lambda t, i: summed(t, i, 0, out_buf.at[t, 7], far_in.at[t], xp)
    half_p = lambda t, i: summed(t, i, 1, out_buf.at[t, 4, :, :, lo], half_in.at[t, 0], zp)
    half_m = lambda t, i: summed(t, i, 2, out_buf.at[t, 4, :, :, hi], half_in.at[t, 1], zm)
    plane_p = lambda t, i: summed(t, i, 3, out_buf.at[t, 5], plane_in.at[t, 0], zp)
    plane_m = lambda t, i: summed(t, i, 4, out_buf.at[t, 6], plane_in.at[t, 1], zm)
    z_p = lambda t, i: summed(t, i, 5, out_buf.at[t, 2], z_in.at[t, 0], zp)
    z_m = lambda t, i: summed(t, i, 6, out_buf.at[t, 1], z_in.at[t, 1], zm)
    x_sum = lambda t, i: summed(t, i, 7, out_buf.at[t, 3], x_in.at[t], xp)
    sums = [far_sum, half_p, half_m, plane_p, plane_m, z_p, z_m, x_sum]

    def to_owner(t, i, d):
        rows = pl.ds(pl.multiple_of(kvat(d) * 64, 64), 64)
        return cp(own.at[t, i, rows, :], fin.at[t, d, i], ks.at[t, i, d], kr.at[t, i, d], {"kv": kvat(d)})

    for i in range(2):
        for c in spread(0, i):
            c.start()
    w_own[0] = jnp.full((8, 128), rl_ref[0, 0].astype(F32))
    w_x.start()
    for c in local:
        c.wait()

    live = jnp.where(lax.broadcasted_iota(jnp.int32, (HD, SLOTS), 1) < rl_ref[0, 0], 1.0, 0.0).astype(BF)

    def stage_queries(i, _):
        for u in range(2):
            for v in range(2):
                h = i * 4 + u * 2 + v
                half = slice(v * HD, (v + 1) * HD)
                q_t[h] = ds_ref[i * 2 + u, 0:256, half].T
                d_t[h] = ds_ref[i * 2 + u, 256:512, half].T * live
        return 0

    lax.fori_loop(0, HEADS // 4, stage_queries, 0)
    for t in range(2):
        k_n[t, RESP_AT:, :] = r_kv[0, t]
        k_t[t, :, RESP_AT:] = r_kv[0, t].T
        v_t[t, 0:HD, RESP_AT:] = r_kv[1, t].T
        v_t[t, HD:, RESP_AT:] = jnp.ones((16, SET), BF)

    plen = pl_ref[0]

    def valid_keys(s, shape, axis):
        dx, dz = SETS[s]
        owner = (xh if dx == 0 else 1 - xh) * 4 + (z + dz) % 4
        r = lax.broadcasted_iota(jnp.int32, shape, axis)
        return jnp.where((r // 64) * 512 + r % 64 < plen - owner * 64, 1.0, 0.0).astype(BF)

    def put_set(t, s):
        by_row = valid_keys(s, (SET, HD), 0)
        by_col = valid_keys(s, (16, SET), 1)
        start = (s - 1) * SET if s else OWN_AT
        at = slice(start, start + SET)
        k = sets[t, s, 0]
        k_n[t, at, :] = k * by_row + k[0:1, :] * (1 - by_row)
        k_t[t, :, at] = k.T * by_col[0:1, :]
        v_t[t, 0:HD, at] = sets[t, s, 1].T * by_col[0:1, :]
        v_t[t, HD:, at] = by_col

    s_bufs, ds_bufs, dc_bufs = (s_a, s_b), (ds_a, ds_b), (dc_a, dc_b)

    def scores(t, j, u, rows, at, mask):
        h = t * QPG + u
        top = None
        for r in range(0, rows, 256):
            s = dot(k_n[t, pl.ds(at + r, 256), :], q_t[h], NN) * (SCALE * LOG2E)
            if mask is not None and r:
                s = jnp.where(mask, s, -1e30)
            s_bufs[u % 2][r:r + 256, :] = s
            b = jnp.max(s.reshape(32, 8, SLOTS), 0)
            top = b if top is None else jnp.maximum(top, b)
            yield
        m = jnp.max(top, 0, keepdims=True)
        mc[j, h] = m if mask is not None else jnp.maximum(mc[j - 1, h], m)

    def weights(t, j, u, rows, at):
        h = t * QPG + u
        m = mc[j, h]
        for r in range(0, rows, 256):
            p = jnp.exp2(s_bufs[u % 2][r:r + 256, :] - m).astype(BF)
            p_ref[h, pl.ds(at + r, 256), :] = p
            ds_bufs[u % 2][r:r + 256, :] = p
            yield

    def attend(t, j, u, rows, at, first):
        h = t * QPG + u
        new = dot(v_t[t, :, pl.ds(at, rows)], ds_bufs[u % 2][0:rows, :], NN)
        yield
        o_acc[h] = new if first else o_acc[h] * jnp.exp2(mc[j - 1, h] - mc[j, h]) + new

    def forward(t, j, rows, at, mask):
        for u in range(QPG + 2):
            steps = []
            if u < QPG:
                steps.append(scores(t, j, u, rows, at, mask))
            if 0 <= u - 1 < QPG:
                steps.append(weights(t, j, u - 1, rows, at))
            if 0 <= u - 2:
                steps.append(attend(t, j, u - 2, rows, at, mask is not None))
            while steps:
                for step in list(steps):
                    try:
                        next(step)
                    except StopIteration:
                        steps.remove(step)

    def weigh(t, j, u, rows, at, values):
        h = t * QPG + u
        corr = jnp.exp2(mc[j, h] - lse[h])
        dc = (d_t[h].astype(F32) * corr).astype(BF)
        dc_bufs[u % 2][...] = dc
        cd = corr * delta[h]
        for r in range(0, rows, 256):
            dp = dot(values(r), dc, NN) - cd
            ds = p_ref[h, pl.ds(at + r, 256), :] * dp.astype(BF)
            ds_bufs[u % 2][r:r + 256, :] = ds
            ds_ref[h, pl.ds(at + r, 256), :] = ds

    def key_sums(t, u, rows, at):
        h = t * QPG + u
        for r in range(0, rows, 256):
            dv = dot(dc_bufs[u % 2][...], p_ref[h, pl.ds(at + r, 256), :], NT)
            dk = dot(q_t[h], ds_bufs[u % 2][r:r + 256, :], NT)
            if u == 0:
                dv_acc[:, r:r + 256] = dv
                dk_acc[:, r:r + 256] = dk
            else:
                dv_acc[:, r:r + 256] += dv
                dk_acc[:, r:r + 256] += dk

    def backward(t, j, rows, at, values):
        for u in range(QPG + 1):
            if u < QPG:
                weigh(t, j, u, rows, at, values)
            if u > 0:
                key_sums(t, u - 1, rows, at)

    def query_sums(t):
        for u in range(QPG):
            h = t * QPG + u
            dq = dot(k_t[t], ds_ref[h], NN) * (w2 * SCALE)
            p_ref[t * 4 + u // 2, 0:256, (u % 2) * HD:(u % 2 + 1) * HD] = dq.astype(BF).T

    for i in range(2):
        for c in spread(0, i):
            c.wait_recv()
        for c in (to_x, to_p, to_m):
            c(0, i).start()
    row_at = lax.broadcasted_iota(jnp.int32, (SET, SLOTS), 0)
    slot_at = lax.broadcasted_iota(jnp.int32, (SET, SLOTS), 1)
    causal = (row_at <= slot_at) & (row_at < rl_ref[0, 0])

    def first_chunk(t):
        put_set(t, 0)
        forward(t, 0, PC, OWN_AT, causal)

    first_chunk(0)
    w_x.wait_recv()
    w_own[1] = w_own[0] + w_in[0]
    for c in w_z:
        c.start()

    def pass_on(t, parts):
        for i in parts:
            to_p(t, i).wait_recv()
            on_p(t, i).start()
            to_m(t, i).wait_recv()
            on_m(t, i).start()
            to_x(t, i).wait_recv()
            xto_p(t, i).start()
            xto_m(t, i).start()

    def pass_far(t, parts):
        for i in parts:
            on_p(t, i).wait_recv()
            on_m(t, i).wait_recv()
            far(t, i).start()

    def owner_sum(t, i):
        z_p(t, i).wait_recv()
        z_m(t, i).wait_recv()
        x_sum(t, i).wait_recv()
        for n in (0, 1) if i is None else (i,):
            total = out_buf[t, 0, n].astype(F32) + z_in[t, 0, n].astype(F32)
            total = total + (z_in[t, 1, n].astype(F32) + x_in[t, n].astype(F32))
            own[t, n] = total.astype(BF).T
            for d in (1, 2, 3):
                to_owner(t, n, d).start()

    def add_to(ref, more):
        ref[...] = (ref[...].astype(F32) + more).astype(BF)

    def plane_sums(t, i):
        n = whole if i is None else i
        plane_p(t, i).wait_recv()
        plane_m(t, i).wait_recv()
        add_to(out_buf.at[t, 3, n], plane_in[t, 0, n].astype(F32) + plane_in[t, 1, n].astype(F32))
        x_sum(t, i).start()

    def half_sums(t, i):
        n = whole if i is None else i
        half_p(t, i).wait_recv()
        add_to(out_buf.at[t, 2, n, :, 0:128], half_in[t, 0, n].astype(F32))
        z_p(t, i).start()
        half_m(t, i).wait_recv()
        add_to(out_buf.at[t, 1, n, :, 128:256], half_in[t, 1, n].astype(F32))
        z_m(t, i).start()

    def far_sums(t, i):
        n = whole if i is None else i
        far_sum(t, i).wait_recv()
        add_to(out_buf.at[t, 4, n], far_in[t, n].astype(F32))
        half_p(t, i).start()
        half_m(t, i).start()

    def fwd_chunk(t, c):
        first = t == 0
        second = jnp.logical_not(first)

        @pl.when(c == 1)
        def _():
            @pl.when(first)
            def _():
                pass_on(0, (0, 1))
                for i in range(2):
                    for o in spread(1, i):
                        o.start()

            put_set(t, 1)
            put_set(t, 2)

        @pl.when(c == 2)
        def _():
            @pl.when(first)
            def _():
                for i in range(2):
                    for o in spread(1, i):
                        o.wait_recv()
                first_chunk(1)
                pass_far(0, (0, 1))
                for w in w_z:
                    w.wait_recv()
                w_own[2] = w_own[1] + (w_in[1] + w_in[2] + w_in[3])
                for w in w_y:
                    w.start()

            @pl.when(second)
            def _():
                plane_sums(0, None)

            put_set(t, 3)
            put_set(t, 4)

        @pl.when(c == 3)
        def _():
            @pl.when(first)
            def _():
                for i in range(2):
                    xto_p(0, i).wait_recv()
                    xto_m(0, i).wait_recv()
                to_p(1, None).start()
                to_m(1, None).start()

            @pl.when(second)
            def _():
                xto_p(1, None).wait_recv()
                xto_m(1, None).wait_recv()
                half_sums(0, None)

            put_set(t, 5)
            put_set(t, 6)

        forward(t, c, PC, pl.multiple_of((c - 1) * PC, PC), None)

    def last_chunk(t):
        @pl.when(t == 0)
        def _():
            far(0, 0).wait_recv()
            far(0, 1).wait_recv()
            to_x(1, None).start()

        @pl.when(t == 1)
        def _():
            far(1, None).wait_recv()

        put_set(t, 7)
        forward(t, 4, SET, LAST_AT, None)

    def finish_fwd(t):
        for u in range(QPG):
            h = t * QPG + u
            o = o_acc[h]
            total = o[HD:HD + 1, :]
            out = (o[0:HD, :] * (1.0 / total)).astype(BF)
            o_out[t * 4 + u // 2, :, (u % 2) * HD:(u % 2 + 1) * HD] = out.T
            delta[h] = jnp.sum(out.astype(F32) * d_t[h].astype(F32), 0, keepdims=True)
            lse[h] = mc[4, h] + jnp.log2(total)

    def put_out(t, s, i):
        cols = slice(i * SET, (i + 1) * SET)
        out_buf[t, s, 0] = dk_acc[:, cols].astype(BF)
        out_buf[t, s, 1] = dv_acc[:, cols].astype(BF)

    def bwd_chunk(t, c):
        first = t == 0
        second = jnp.logical_not(first)

        @pl.when((c == 3) & first)
        def _():
            pass_on(1, (None,))

        @pl.when((c == 1) & first)
        def _():
            pass_far(1, (None,))

        backward(t, c, PC, pl.multiple_of((c - 1) * PC, PC), lambda r: sets[t, 2 * c - 1 + r // SET, 1])
        put_out(t, 2 * c - 1, 0)
        put_out(t, 2 * c, 1)

        @pl.when((c == 3) & first)
        def _():
            plane_p(0, None).start()
            plane_m(0, None).start()

        @pl.when((c == 3) & second)
        def _():
            for i in range(2):
                plane_p(1, i).start()
                plane_m(1, i).start()

        @pl.when((c == 2) & second)
        def _():
            far_sums(1, 0)

        @pl.when((c == 1) & first)
        def _():
            far_sums(0, None)

        @pl.when((c == 1) & second)
        def _():
            far_sums(1, 1)

    def own_chunk(t):
        backward(t, 0, PC, OWN_AT, lambda r: sets[t, 0, 1] if r == 0 else r_kv[1, t])
        put_out(t, 0, 0)
        head = slice(t * HD, (t + 1) * HD)
        drk_ref[:, head] = (dk_acc[:, SET:] * (w2 * SCALE)).T.astype(BF)
        drv_ref[:, head] = (dv_acc[:, SET:] * w2).T.astype(BF)

    def o_copy(i):
        return pltpu.make_async_copy(o_out.at[i], o_hbm.at[:, pair(i)], ls.at[i])

    def both(t, _):
        lax.fori_loop(1, 4, lambda c, _: (fwd_chunk(t, c), 0)[1], 0)
        last_chunk(t)
        finish_fwd(t)
        backward(t, 4, SET, LAST_AT, lambda r: sets[t, 7, 1])
        put_out(t, 7, 0)

        @pl.when(t == 0)
        def _():
            far_sum(0, None).start()

        @pl.when(t == 1)
        def _():
            far_sum(1, 0).start()
            far_sum(1, 1).start()

        lax.fori_loop(0, 3, lambda i, _: (bwd_chunk(t, 3 - i), 0)[1], 0)
        return 0

    lax.fori_loop(0, 2, both, 0)
    for i in range(8):
        o_copy(i).start()
    for w in w_y:
        w.wait_recv()
    count = w_own[2] + (w_in[4] + w_in[5] + w_in[6])
    weight = (8192.0 / count)[0:1, :]
    w2 = cat([weight, weight], 1)

    def dq_copy(i):
        return pltpu.make_async_copy(p_ref.at[i, 0:256, :], dq_hbm.at[:, pair(i)], ls.at[8 + i])

    def finish_queries(t):
        query_sums(t)
        for i in range(t * 4, t * 4 + 4):
            dq_copy(i).start()

    mine = lax.broadcasted_iota(jnp.int32, (64, HD), 0) + (kv * 8 + grp) * 64 < plen

    def finish_keys(t):
        for d in range(4):
            cols = head_cols(kvat(4 - d), t)
            if d == 0:
                got_k, got_v = own[t, 0, my_rows, :], own[t, 1, my_rows, :]
            else:
                to_owner(t, 0, d).wait_recv()
                to_owner(t, 1, d).wait_recv()
                got_k, got_v = fin[t, d, 0], fin[t, d, 1]
            dpk_ref[:, cols] = jnp.where(mine, got_k.astype(F32) * (weight * SCALE), 0.0)
            dpv_ref[:, cols] = jnp.where(mine, got_v.astype(F32) * weight, 0.0)

    plane_sums(1, 0)
    own_chunk(1)
    half_sums(1, 0)
    plane_sums(1, 1)
    finish_queries(1)
    half_sums(1, 1)
    own_chunk(0)
    owner_sum(0, None)
    finish_queries(0)
    owner_sum(1, 0)
    finish_keys(0)
    owner_sum(1, 1)

    for c in [w_x] + w_z + w_y:
        c.wait_send()
    for t in range(2):
        for i in range(2):
            for c in spread(t, i):
                c.wait_send()
        for i in ((0, 1), (None,))[t]:
            for g in gather:
                g(t, i).wait_send()
        for i in ((None,), (0, 1))[t]:
            for g in sums:
                g(t, i).wait_send()
    for i in range(8):
        o_copy(i).wait()
        dq_copy(i).wait()
    finish_keys(1)
    for t in range(2):
        for i in range(2):
            for d in (1, 2, 3):
                to_owner(t, i, d).wait_send()


def hand_over(*refs):
    ins, outs, held, (in_sem, out_sem) = refs[0:6], refs[6:12], refs[12:18], refs[18:]
    pieces = []
    for i in range(6):
        parts = 4 if i < 2 else 1
        rows = ins[i].shape[0] // parts
        for j in range(parts):
            pieces.append((i, pl.ds(j * rows, rows)))
    into = [
        pltpu.make_async_copy(ins[i].at[r], held[i].at[r], in_sem.at[n]) for n, (i, r) in enumerate(pieces)
    ]
    out = [
        pltpu.make_async_copy(held[i].at[r], outs[i].at[r], out_sem.at[n]) for n, (i, r) in enumerate(pieces)
    ]
    for c in into:
        c.start()
    for a, b in zip(into, out):
        a.wait()
        b.start()
    for c in out:
        c.wait()


def on_device(
    queries, resp_keys, resp_values, prompt_keys, prompt_values, grad_out, resp_len, prompt_len
):
    vm = pl.BlockSpec(memory_space=pltpu.VMEM)
    sm = pl.BlockSpec(memory_space=pltpu.SMEM)
    hbm = pl.BlockSpec(memory_space=pl.ANY)
    shape = jax.ShapeDtypeStruct
    dma = pltpu.SemaphoreType.DMA
    shapes = [
        shape((256, 2048), BF), shape((256, 2048), BF), shape((256, 256), BF), shape((256, 256), BF),
        shape((64, 1024), F32), shape((64, 1024), F32),
    ]
    outs = pl.pallas_call(
        kernel,
        out_shape=shapes,
        in_specs=[sm, sm] + [hbm] * 6,
        out_specs=[hbm, hbm] + [vm] * 4,
        scratch_shapes=[
            pltpu.VMEM((2, 8, 2, SET, HD), BF),
            pltpu.VMEM((HEADS, KEYS, SLOTS), BF),
            pltpu.VMEM((HEADS, KEYS, SLOTS), BF),
            pltpu.VMEM((HEADS, HD + 16, SLOTS), F32),
            pltpu.VMEM((8, SLOTS, 256), BF),
            pltpu.VMEM((5, HEADS, 1, SLOTS), F32),
            pltpu.VMEM((HEADS, 1, SLOTS), F32),
            pltpu.VMEM((HEADS, 1, SLOTS), F32),
            pltpu.VMEM((2, KEYS, HD), BF),
            pltpu.VMEM((2, HD, KEYS), BF),
            pltpu.VMEM((2, HD + 16, KEYS), BF),
            pltpu.VMEM((2, 2, SET, HD), BF),
            pltpu.VMEM((HEADS, HD, SLOTS), BF),
            pltpu.VMEM((HEADS, HD, SLOTS), BF),
            pltpu.VMEM((PC, SLOTS), F32),
            pltpu.VMEM((PC, SLOTS), F32),
            pltpu.VMEM((PC, SLOTS), BF),
            pltpu.VMEM((PC, SLOTS), BF),
            pltpu.VMEM((HD, SLOTS), BF),
            pltpu.VMEM((HD, SLOTS), BF),
            pltpu.VMEM((HD, PC), F32),
            pltpu.VMEM((HD, PC), F32),
            pltpu.VMEM((2, 8, 2, HD, SET), BF),
            pltpu.VMEM((2, 2, SET, HD), BF),
            pltpu.VMEM((2, 2, 2, HD, 128), BF),
            pltpu.VMEM((2, 2, 2, HD, SET), BF),
            pltpu.VMEM((2, 2, 2, HD, SET), BF),
            pltpu.VMEM((2, 2, HD, SET), BF),
            pltpu.VMEM((2, 2, HD, SET), BF),
            pltpu.VMEM((2, 4, 2, 64, HD), BF),
            pltpu.VMEM((3, 8, 128), F32),
            pltpu.VMEM((7, 8, 128), F32),
            dma((24,)), dma((2, 2, 4)), dma((2, 2, 4)), dma((2, 2, 8)), dma((2, 2, 8)), dma((2, 2, 8)), dma((2, 2, 8)),
            dma((2, 2, 4)), dma((2, 2, 4)), dma((7,)), dma((7,)),
        ],
        compiler_params=pltpu.CompilerParams(
            collective_id=0, has_side_effects=True, vmem_limit_bytes=62 * 2**20
        ),
        name="attention",
    )(
        resp_len, prompt_len, queries.reshape(256, 2048), grad_out.reshape(256, 2048),
        resp_keys.reshape(256, 256), resp_values.reshape(256, 256),
        prompt_keys.reshape(64, 1024), prompt_values.reshape(64, 1024),
    )
    attended, grad_q, grad_rk, grad_rv, grad_pk, grad_pv = pl.pallas_call(
        hand_over,
        out_shape=shapes,
        in_specs=[hbm] * 6,
        out_specs=[hbm] * 6,
        scratch_shapes=[pltpu.VMEM(a.shape, a.dtype) for a in shapes] + [dma((12,)), dma((12,))],
        name="hand_over",
    )(*outs)
    return (
        attended.reshape(queries.shape),
        grad_q.reshape(queries.shape),
        grad_rk.reshape(resp_keys.shape),
        grad_rv.reshape(resp_values.shape),
        grad_pk.reshape(1, 64, 1024),
        grad_pv.reshape(1, 64, 1024),
    )


def solution(mesh):
    wide = P("prompt", "grp", None, "kv")
    rows = P("prompt", ("kv", "grp"), None)
    return jax.shard_map(
        on_device,
        mesh=mesh,
        in_specs=(wide, wide, wide, rows, rows, wide, P("prompt", "grp"), P("prompt")),
        out_specs=(wide, wide, wide, wide, rows, rows),
        check_vma=False,
    )
```

```python
import jax
import jax.numpy as jnp
from jax import lax
from jax.experimental import pallas as pl
from jax.experimental.pallas import tpu as pltpu
from jax.sharding import PartitionSpec as P

F32 = jnp.float32
BF = jnp.bfloat16
MESH = pl.DeviceIdType.MESH
HD = 128
QPG = 8
SCALE = HD ** (-0.5)
LOG2E = 1.4426950408889634
NT = (((1,), (1,)), ((), ()))
NN = (((1,), (0,)), ((), ()))
SET = 256
PC = 512
HEADS = 16
SLOTS = 256
RESP_AT = 2048
KEYS = 2304
OWN_AT = 1792
LAST_AT = 1536
SETS = ((0, 0), (0, 3), (0, 1), (1, 0), (0, 2), (1, 1), (1, 3), (1, 2))


def dot(a, b, dims):
    return lax.dot_general(a, b, dims, preferred_element_type=F32)


def cat(parts, axis):
    return parts[0] if len(parts) == 1 else jnp.concatenate(parts, axis)


def kernel(
    rl_ref, pl_ref, q_hbm, do_hbm, rk_hbm, rv_hbm, pk_hbm, pv_hbm,
    o_hbm, dq_hbm, drk_ref, drv_ref, dpk_ref, dpv_ref,
    sets, p_ref, ds_ref, o_acc, o_out, mc, lse, delta, k_n, k_t, v_t, r_kv, q_t, d_t,
    s_a, s_b, ds_a, ds_b, dc_a, dc_b, dk_acc, dv_acc,
    out_buf, own, half_in, plane_in, z_in, x_in, far_in, fin, w_own, w_in,
    ls, a2a_s, a2a_r, gs, gr, hs, hr, ks, kr, ws, wr,
):
    kv = lax.axis_index("kv")
    grp = lax.axis_index("grp")
    prm = lax.axis_index("prompt")
    xh = grp // 4
    z = grp % 4
    zat = lambda d: {"grp": xh * 4 + (z + d) % 4}
    zp, zm, xp = zat(1), zat(3), {"grp": (1 - xh) * 4 + z}
    kvat = lambda d: (kv + d) % 4
    yat = lambda d: {"prompt": (prm + d) % 4}
    my_rows = pl.ds(pl.multiple_of(kv * 64, 64), 64)
    head_cols = lambda who, t: pl.ds(pl.multiple_of(who * 256 + t * HD, HD), HD)

    pair = lambda i: pl.ds(i * 256, 256)
    local = []
    for i in range(8):
        local.append(pltpu.make_async_copy(q_hbm.at[:, pair(i)], ds_ref.at[i, 0:256, :], ls.at[i]))
        local.append(pltpu.make_async_copy(do_hbm.at[:, pair(i)], ds_ref.at[i, 256:512, :], ls.at[8 + i]))
    for t in range(2):
        for i, ref in ((0, pk_hbm), (1, pv_hbm)):
            n = 16 + t * 2 + i
            local.append(pltpu.make_async_copy(ref.at[:, head_cols(kv, t)], sets.at[t, 0, i, my_rows, :], ls.at[n]))
        for i, ref in ((0, rk_hbm), (1, rv_hbm)):
            n = 20 + t * 2 + i
            local.append(pltpu.make_async_copy(ref.at[:, t * HD:(t + 1) * HD], r_kv.at[i, t], ls.at[n]))
    for c in local:
        c.start()

    peers = [{"kv": kvat(d)} for d in (1, 2, 3)] + [zat(d) for d in (1, 2, 3)]
    peers += [yat(d) for d in (1, 2, 3)] + [xp]
    barrier = pltpu.get_barrier_semaphore()
    for peer in peers:
        pl.semaphore_signal(barrier, inc=1, device_id=peer, device_id_type=MESH)
    pl.semaphore_wait(barrier, len(peers))

    def cp(src, dst, ssem, rsem, dev):
        return pltpu.make_async_remote_copy(
            src_ref=src, dst_ref=dst, send_sem=ssem, recv_sem=rsem, device_id=dev, device_id_type=MESH
        )

    def spread(t):
        made = []
        for d in (1, 2, 3):
            for i, ref in ((0, pk_hbm), (1, pv_hbm)):
                n = (d - 1) * 2 + i
                made.append(
                    cp(ref.at[:, head_cols(kvat(d), t)], sets.at[t, 0, i, my_rows, :],
                       a2a_s.at[t, n], a2a_r.at[t, n], {"kv": kvat(d)})
                )
        return made

    lo, hi = pl.ds(0, 128), pl.ds(128, 128)

    def moved(t, n, src, dst, dev, rows=None):
        a, b = sets.at[t, src], sets.at[t, dst]
        if rows is not None:
            a, b = a.at[:, rows], b.at[:, rows]
        return cp(a, b, gs.at[t, n], gr.at[t, n], dev)

    to_x = lambda t: moved(t, 0, 0, 3, xp)
    to_p = lambda t: moved(t, 1, 0, 1, zp)
    to_m = lambda t: moved(t, 2, 0, 2, zm)
    on_p = lambda t: moved(t, 3, 1, 4, zp, lo)
    on_m = lambda t: moved(t, 4, 2, 4, zm, hi)
    xto_p = lambda t: moved(t, 5, 3, 6, zp)
    xto_m = lambda t: moved(t, 6, 3, 5, zm)
    far = lambda t: moved(t, 7, 4, 7, xp)
    gather = [to_x, to_p, to_m, on_p, on_m, xto_p, xto_m, far]
    w_x = cp(w_own.at[0], w_in.at[0], ws.at[0], wr.at[0], xp)
    w_z = [cp(w_own.at[1], w_in.at[d], ws.at[d], wr.at[d], zat(d)) for d in (1, 2, 3)]
    w_y = [cp(w_own.at[2], w_in.at[3 + d], ws.at[3 + d], wr.at[3 + d], yat(d)) for d in (1, 2, 3)]
    def summed(t, n, src, dst, dev):
        return cp(src, dst, hs.at[t, n], hr.at[t, n], dev)

    far_sum = lambda t: summed(t, 0, out_buf.at[t, 7], far_in.at[t], xp)
    half_p = lambda t: summed(t, 1, out_buf.at[t, 4, :, :, lo], half_in.at[t, 0], zp)
    half_m = lambda t: summed(t, 2, out_buf.at[t, 4, :, :, hi], half_in.at[t, 1], zm)
    plane_p = lambda t: summed(t, 3, out_buf.at[t, 5], plane_in.at[t, 0], zp)
    plane_m = lambda t: summed(t, 4, out_buf.at[t, 6], plane_in.at[t, 1], zm)
    z_p = lambda t: summed(t, 5, out_buf.at[t, 2], z_in.at[t, 0], zp)
    z_m = lambda t: summed(t, 6, out_buf.at[t, 1], z_in.at[t, 1], zm)
    x_sum = lambda t: summed(t, 7, out_buf.at[t, 3], x_in.at[t], xp)
    sums = [far_sum, half_p, half_m, plane_p, plane_m, z_p, z_m, x_sum]

    def to_owner(t, d):
        rows = pl.ds(pl.multiple_of(kvat(d) * 64, 64), 64)
        return cp(own.at[t, :, rows, :], fin.at[t, d], ks.at[t, d], kr.at[t, d], {"kv": kvat(d)})

    for c in spread(0):
        c.start()
    w_own[0] = jnp.full((8, 128), rl_ref[0, 0].astype(F32))
    w_x.start()
    for c in local:
        c.wait()

    live = jnp.where(lax.broadcasted_iota(jnp.int32, (HD, SLOTS), 1) < rl_ref[0, 0], 1.0, 0.0).astype(BF)

    def stage_queries(i, _):
        for u in range(2):
            for v in range(2):
                h = i * 4 + u * 2 + v
                half = slice(v * HD, (v + 1) * HD)
                q_t[h] = ds_ref[i * 2 + u, 0:256, half].T
                d_t[h] = ds_ref[i * 2 + u, 256:512, half].T * live
        return 0

    lax.fori_loop(0, HEADS // 4, stage_queries, 0)
    for t in range(2):
        k_n[t, RESP_AT:, :] = r_kv[0, t]
        k_t[t, :, RESP_AT:] = r_kv[0, t].T
        v_t[t, 0:HD, RESP_AT:] = r_kv[1, t].T
        v_t[t, HD:, RESP_AT:] = jnp.ones((16, SET), BF)

    plen = pl_ref[0]

    def valid_keys(s, shape, axis):
        dx, dz = SETS[s]
        owner = (xh if dx == 0 else 1 - xh) * 4 + (z + dz) % 4
        r = lax.broadcasted_iota(jnp.int32, shape, axis)
        return jnp.where((r // 64) * 512 + r % 64 < plen - owner * 64, 1.0, 0.0).astype(BF)

    def put_set(t, s):
        by_row = valid_keys(s, (SET, HD), 0)
        by_col = valid_keys(s, (16, SET), 1)
        start = (s - 1) * SET if s else OWN_AT
        at = slice(start, start + SET)
        k = sets[t, s, 0]
        k_n[t, at, :] = k * by_row + k[0:1, :] * (1 - by_row)
        k_t[t, :, at] = k.T * by_col[0:1, :]
        v_t[t, 0:HD, at] = sets[t, s, 1].T * by_col[0:1, :]
        v_t[t, HD:, at] = by_col

    s_bufs, ds_bufs, dc_bufs = (s_a, s_b), (ds_a, ds_b), (dc_a, dc_b)

    def scores(t, j, u, rows, at, mask):
        h = t * QPG + u
        s_ref = s_bufs[u % 2]
        top = None
        for r in range(0, rows, 256):
            s = dot(k_n[t, pl.ds(at + r, 256), :], q_t[h], NN) * (SCALE * LOG2E)
            if mask is not None and r:
                s = jnp.where(mask, s, -1e30)
            s_ref[r:r + 256, :] = s
            b = jnp.max(s.reshape(32, 8, SLOTS), 0)
            top = b if top is None else jnp.maximum(top, b)
        m = jnp.max(top, 0, keepdims=True)
        mc[j, h] = m if mask is not None else jnp.maximum(mc[j - 1, h], m)

    def attend(t, j, u, rows, at, first):
        h = t * QPG + u
        s_ref = s_bufs[u % 2]
        m = mc[j, h]
        parts = []
        for r in range(0, rows, 256):
            p = jnp.exp2(s_ref[r:r + 256, :] - m).astype(BF)
            p_ref[h, pl.ds(at + r, 256), :] = p
            parts.append(p)
        new = dot(v_t[t, :, pl.ds(at, rows)], cat(parts, 0), NN)
        o_acc[h] = new if first else o_acc[h] * jnp.exp2(mc[j - 1, h] - m) + new

    def forward(t, j, rows, at, mask):
        for u in range(QPG + 1):
            if u < QPG:
                scores(t, j, u, rows, at, mask)
            if u > 0:
                attend(t, j, u - 1, rows, at, mask is not None)

    def weigh(t, j, u, rows, at, values):
        h = t * QPG + u
        corr = jnp.exp2(mc[j, h] - lse[h])
        dc = (d_t[h].astype(F32) * corr).astype(BF)
        dc_bufs[u % 2][...] = dc
        cd = corr * delta[h]
        for r in range(0, rows, 256):
            dp = dot(values(r), dc, NN) - cd
            ds = p_ref[h, pl.ds(at + r, 256), :] * dp.astype(BF)
            ds_bufs[u % 2][r:r + 256, :] = ds
            ds_ref[h, pl.ds(at + r, 256), :] = ds

    def key_sums(t, u, rows, at):
        h = t * QPG + u
        for r in range(0, rows, 256):
            dv = dot(dc_bufs[u % 2][...], p_ref[h, pl.ds(at + r, 256), :], NT)
            dk = dot(q_t[h], ds_bufs[u % 2][r:r + 256, :], NT)
            if u == 0:
                dv_acc[:, r:r + 256] = dv
                dk_acc[:, r:r + 256] = dk
            else:
                dv_acc[:, r:r + 256] += dv
                dk_acc[:, r:r + 256] += dk

    def backward(t, j, rows, at, values):
        for u in range(QPG + 1):
            if u < QPG:
                weigh(t, j, u, rows, at, values)
            if u > 0:
                key_sums(t, u - 1, rows, at)

    def query_sums(t):
        for u in range(QPG):
            h = t * QPG + u
            dq = dot(k_t[t], ds_ref[h], NN) * (w2 * SCALE)
            p_ref[t * 4 + u // 2, 0:256, (u % 2) * HD:(u % 2 + 1) * HD] = dq.astype(BF).T

    for c in spread(0):
        c.wait_recv()
    for c in (to_x, to_p, to_m):
        c(0).start()
    for c in spread(1):
        c.start()
    row_at = lax.broadcasted_iota(jnp.int32, (SET, SLOTS), 0)
    slot_at = lax.broadcasted_iota(jnp.int32, (SET, SLOTS), 1)
    causal = (row_at <= slot_at) & (row_at < rl_ref[0, 0])

    def first_chunk(t, _):
        @pl.when(t == 1)
        def _():
            for c in spread(1):
                c.wait_recv()

        put_set(t, 0)
        forward(t, 0, PC, OWN_AT, causal)
        return 0

    lax.fori_loop(0, 2, first_chunk, 0)
    w_x.wait_recv()
    w_own[1] = w_own[0] + w_in[0]
    for c in w_z:
        c.start()

    def owner_sum(t):
        z_p(t).wait_recv()
        z_m(t).wait_recv()
        x_sum(t).wait_recv()
        for i in range(2):
            total = out_buf[t, 0, i].astype(F32) + z_in[t, 0, i].astype(F32)
            total = total + (z_in[t, 1, i].astype(F32) + x_in[t, i].astype(F32))
            own[t, i] = total.astype(BF).T
        for d in (1, 2, 3):
            to_owner(t, d).start()

    def plane_sums(t):
        plane_p(t).wait_recv()
        plane_m(t).wait_recv()
        total = plane_in[t, 0].astype(F32) + plane_in[t, 1].astype(F32)
        out_buf[t, 3] = (out_buf[t, 3].astype(F32) + total).astype(BF)
        x_sum(t).start()

    def half_sums(t):
        half_p(t).wait_recv()
        out_buf[t, 2, :, :, 0:128] = (
            out_buf[t, 2, :, :, 0:128].astype(F32) + half_in[t, 0].astype(F32)
        ).astype(BF)
        z_p(t).start()
        half_m(t).wait_recv()
        out_buf[t, 1, :, :, 128:256] = (
            out_buf[t, 1, :, :, 128:256].astype(F32) + half_in[t, 1].astype(F32)
        ).astype(BF)
        z_m(t).start()

    def far_sums(t):
        far_sum(t).wait_recv()
        out_buf[t, 4] = (out_buf[t, 4].astype(F32) + far_in[t].astype(F32)).astype(BF)
        half_p(t).start()
        half_m(t).start()

    def fwd_chunk(t, c):
        first = t == 0

        @pl.when(c == 1)
        def _():
            @pl.when(first)
            def _():
                to_p(0).wait_recv()
                on_p(0).start()
                to_m(0).wait_recv()
                on_m(0).start()
                to_x(0).wait_recv()
                xto_p(0).start()
                xto_m(0).start()

            put_set(t, 1)
            put_set(t, 2)

        @pl.when(c == 2)
        def _():
            @pl.when(first)
            def _():
                on_p(0).wait_recv()
                on_m(0).wait_recv()
                far(0).start()
                for w in w_z:
                    w.wait_recv()
                w_own[2] = w_own[1] + (w_in[1] + w_in[2] + w_in[3])
                for w in w_y:
                    w.start()

            @pl.when(jnp.logical_not(first))
            def _():
                on_p(1).wait_recv()
                on_m(1).wait_recv()
                far(1).start()

            put_set(t, 3)
            put_set(t, 4)

        @pl.when(c == 3)
        def _():
            xto_p(t).wait_recv()
            xto_m(t).wait_recv()

            @pl.when(first)
            def _():
                for o in (to_x, to_p, to_m):
                    o(1).start()

            put_set(t, 5)
            put_set(t, 6)

        forward(t, c, PC, pl.multiple_of((c - 1) * PC, PC), None)

    def finish_fwd(t):
        for u in range(QPG):
            h = t * QPG + u
            o = o_acc[h]
            total = o[HD:HD + 1, :]
            out = (o[0:HD, :] * (1.0 / total)).astype(BF)
            o_out[t * 4 + u // 2, :, (u % 2) * HD:(u % 2 + 1) * HD] = out.T
            delta[h] = jnp.sum(out.astype(F32) * d_t[h].astype(F32), 0, keepdims=True)
            lse[h] = mc[4, h] + jnp.log2(total)

    def put_out(t, s, i):
        cols = slice(i * SET, (i + 1) * SET)
        out_buf[t, s, 0] = dk_acc[:, cols].astype(BF)
        out_buf[t, s, 1] = dv_acc[:, cols].astype(BF)

    def bwd_step(t, n):
        s = t * (1 - n % 2)
        c = 3 - t * ((n + 1) // 2)

        @pl.when(t == 0)
        def _():
            to_p(1).wait_recv()
            on_p(1).start()
            to_m(1).wait_recv()
            on_m(1).start()
            to_x(1).wait_recv()
            xto_p(1).start()
            xto_m(1).start()

        backward(s, c, PC, pl.multiple_of((c - 1) * PC, PC), lambda r: sets[s, 2 * c - 1 + r // SET, 1])
        put_out(s, 2 * c - 1, 0)
        put_out(s, 2 * c, 1)

        @pl.when(n == 0)
        def _():
            plane_p(s).start()
            plane_m(s).start()

        @pl.when(n == 1)
        def _():
            far_sums(0)
            plane_sums(0)

        @pl.when(n == 2)
        def _():
            far_sums(1)

        @pl.when(n == 3)
        def _():
            half_sums(0)
            plane_sums(1)

        @pl.when(n == 4)
        def _():
            half_sums(1)

    def own_chunk(t):
        backward(t, 0, PC, OWN_AT, lambda r: sets[t, 0, 1] if r == 0 else r_kv[1, t])
        put_out(t, 0, 0)
        head = slice(t * HD, (t + 1) * HD)
        drk_ref[:, head] = (dk_acc[:, SET:] * (w2 * SCALE)).T.astype(BF)
        drv_ref[:, head] = (dv_acc[:, SET:] * w2).T.astype(BF)

    def o_copy(i):
        return pltpu.make_async_copy(o_out.at[i], o_hbm.at[:, pair(i)], ls.at[i])

    def both(t, _):
        lax.fori_loop(1, 4, lambda c, _: (fwd_chunk(t, c), 0)[1], 0)
        far(t).wait_recv()
        put_set(t, 7)
        forward(t, 4, SET, LAST_AT, None)
        finish_fwd(t)
        backward(t, 4, SET, LAST_AT, lambda r: sets[t, 7, 1])
        put_out(t, 7, 0)
        far_sum(t).start()
        lax.fori_loop(0, 1 + 4 * t, lambda n, _: (bwd_step(t, n), 0)[1], 0)
        return 0

    lax.fori_loop(0, 2, both, 0)
    for i in range(8):
        o_copy(i).start()
    for w in w_y:
        w.wait_recv()
    count = w_own[2] + (w_in[4] + w_in[5] + w_in[6])
    weight = (8192.0 / count)[0:1, :]
    w2 = cat([weight, weight], 1)

    def dq_copy(i):
        return pltpu.make_async_copy(p_ref.at[i, 0:256, :], dq_hbm.at[:, pair(i)], ls.at[8 + i])

    def finish_queries(t):
        query_sums(t)
        for i in range(t * 4, t * 4 + 4):
            dq_copy(i).start()

    own_chunk(1)
    own_chunk(0)
    owner_sum(0)
    finish_queries(1)
    owner_sum(1)
    finish_queries(0)

    mine = lax.broadcasted_iota(jnp.int32, (64, HD), 0) + (kv * 8 + grp) * 64 < plen
    for t in range(2):
        for d in range(4):
            cols = head_cols(kvat(4 - d), t)
            if d == 0:
                got_k, got_v = own[t, 0, my_rows, :], own[t, 1, my_rows, :]
            else:
                to_owner(t, d).wait_recv()
                got_k, got_v = fin[t, d, 0], fin[t, d, 1]
            dpk_ref[:, cols] = jnp.where(mine, got_k.astype(F32) * (weight * SCALE), 0.0)
            dpv_ref[:, cols] = jnp.where(mine, got_v.astype(F32) * weight, 0.0)

    for t in range(2):
        for c in spread(t) + [g(t) for g in gather] + [s(t) for s in sums] + [to_owner(t, d) for d in (1, 2, 3)]:
            c.wait_send()
    for c in [w_x] + w_z + w_y:
        c.wait_send()
    for i in range(8):
        o_copy(i).wait()
        dq_copy(i).wait()


def hand_over(*refs):
    ins, outs, held, (in_sem, out_sem) = refs[0:6], refs[6:12], refs[12:18], refs[18:]
    pieces = []
    for i in range(6):
        parts = 4 if i < 2 else 1
        rows = ins[i].shape[0] // parts
        for j in range(parts):
            pieces.append((i, pl.ds(j * rows, rows)))
    into = [
        pltpu.make_async_copy(ins[i].at[r], held[i].at[r], in_sem.at[n]) for n, (i, r) in enumerate(pieces)
    ]
    out = [
        pltpu.make_async_copy(held[i].at[r], outs[i].at[r], out_sem.at[n]) for n, (i, r) in enumerate(pieces)
    ]
    for c in into:
        c.start()
    for a, b in zip(into, out):
        a.wait()
        b.start()
    for c in out:
        c.wait()


def on_device(
    queries, resp_keys, resp_values, prompt_keys, prompt_values, grad_out, resp_len, prompt_len
):
    vm = pl.BlockSpec(memory_space=pltpu.VMEM)
    sm = pl.BlockSpec(memory_space=pltpu.SMEM)
    hbm = pl.BlockSpec(memory_space=pl.ANY)
    shape = jax.ShapeDtypeStruct
    dma = pltpu.SemaphoreType.DMA
    shapes = [
        shape((256, 2048), BF), shape((256, 2048), BF), shape((256, 256), BF), shape((256, 256), BF),
        shape((64, 1024), F32), shape((64, 1024), F32),
    ]
    outs = pl.pallas_call(
        kernel,
        out_shape=shapes,
        in_specs=[sm, sm] + [hbm] * 6,
        out_specs=[hbm, hbm] + [vm] * 4,
        scratch_shapes=[
            pltpu.VMEM((2, 8, 2, SET, HD), BF),
            pltpu.VMEM((HEADS, KEYS, SLOTS), BF),
            pltpu.VMEM((HEADS, KEYS, SLOTS), BF),
            pltpu.VMEM((HEADS, HD + 16, SLOTS), F32),
            pltpu.VMEM((8, SLOTS, 256), BF),
            pltpu.VMEM((5, HEADS, 1, SLOTS), F32),
            pltpu.VMEM((HEADS, 1, SLOTS), F32),
            pltpu.VMEM((HEADS, 1, SLOTS), F32),
            pltpu.VMEM((2, KEYS, HD), BF),
            pltpu.VMEM((2, HD, KEYS), BF),
            pltpu.VMEM((2, HD + 16, KEYS), BF),
            pltpu.VMEM((2, 2, SET, HD), BF),
            pltpu.VMEM((HEADS, HD, SLOTS), BF),
            pltpu.VMEM((HEADS, HD, SLOTS), BF),
            pltpu.VMEM((PC, SLOTS), F32),
            pltpu.VMEM((PC, SLOTS), F32),
            pltpu.VMEM((PC, SLOTS), BF),
            pltpu.VMEM((PC, SLOTS), BF),
            pltpu.VMEM((HD, SLOTS), BF),
            pltpu.VMEM((HD, SLOTS), BF),
            pltpu.VMEM((HD, PC), F32),
            pltpu.VMEM((HD, PC), F32),
            pltpu.VMEM((2, 8, 2, HD, SET), BF),
            pltpu.VMEM((2, 2, SET, HD), BF),
            pltpu.VMEM((2, 2, 2, HD, 128), BF),
            pltpu.VMEM((2, 2, 2, HD, SET), BF),
            pltpu.VMEM((2, 2, 2, HD, SET), BF),
            pltpu.VMEM((2, 2, HD, SET), BF),
            pltpu.VMEM((2, 2, HD, SET), BF),
            pltpu.VMEM((2, 4, 2, 64, HD), BF),
            pltpu.VMEM((3, 8, 128), F32),
            pltpu.VMEM((7, 8, 128), F32),
            dma((24,)), dma((2, 6)), dma((2, 6)), dma((2, 8)), dma((2, 8)), dma((2, 8)), dma((2, 8)),
            dma((2, 4)), dma((2, 4)), dma((7,)), dma((7,)),
        ],
        compiler_params=pltpu.CompilerParams(
            collective_id=0, has_side_effects=True, vmem_limit_bytes=62 * 2**20
        ),
        name="attention",
    )(
        resp_len, prompt_len, queries.reshape(256, 2048), grad_out.reshape(256, 2048),
        resp_keys.reshape(256, 256), resp_values.reshape(256, 256),
        prompt_keys.reshape(64, 1024), prompt_values.reshape(64, 1024),
    )
    attended, grad_q, grad_rk, grad_rv, grad_pk, grad_pv = pl.pallas_call(
        hand_over,
        out_shape=shapes,
        in_specs=[hbm] * 6,
        out_specs=[hbm] * 6,
        scratch_shapes=[pltpu.VMEM(a.shape, a.dtype) for a in shapes] + [dma((12,)), dma((12,))],
        name="hand_over",
    )(*outs)
    return (
        attended.reshape(queries.shape),
        grad_q.reshape(queries.shape),
        grad_rk.reshape(resp_keys.shape),
        grad_rv.reshape(resp_values.shape),
        grad_pk.reshape(1, 64, 1024),
        grad_pv.reshape(1, 64, 1024),
    )


def solution(mesh):
    wide = P("prompt", "grp", None, "kv")
    rows = P("prompt", ("kv", "grp"), None)
    return jax.shard_map(
        on_device,
        mesh=mesh,
        in_specs=(wide, wide, wide, rows, rows, wide, P("prompt", "grp"), P("prompt")),
        out_specs=(wide, wide, wide, wide, rows, rows),
        check_vma=False,
    )
```

```python
import jax
import jax.numpy as jnp
from jax import lax
from jax.experimental import pallas as pl
from jax.experimental.pallas import tpu as pltpu
from jax.sharding import PartitionSpec as P

F32 = jnp.float32
BF = jnp.bfloat16
MESH = pl.DeviceIdType.MESH
HD = 128
QPG = 8
SCALE = HD ** (-0.5)
LOG2E = 1.4426950408889634
NT = (((1,), (1,)), ((), ()))
NN = (((1,), (0,)), ((), ()))
SET = 256
PC = 512
HEADS = 16
SLOTS = 256
RESP_AT = 2048
KEYS = 2304
OWN_AT = 1792
LAST_AT = 1536
SETS = ((0, 0), (0, 3), (0, 1), (1, 0), (0, 2), (1, 1), (1, 3), (1, 2))


def dot(a, b, dims):
    return lax.dot_general(a, b, dims, preferred_element_type=F32)


def cat(parts, axis):
    return parts[0] if len(parts) == 1 else jnp.concatenate(parts, axis)


def kernel(
    rl_ref, pl_ref, q_hbm, do_hbm, rk_hbm, rv_hbm, pk_hbm, pv_hbm,
    o_hbm, dq_hbm, drk_ref, drv_ref, dpk_ref, dpv_ref,
    sets, p_ref, ds_ref, o_acc, o_out, mc, lse, delta, k_n, k_t, v_t, r_kv, q_t, d_t,
    s_a, s_b, ds_a, ds_b, dc_a, dc_b, dk_acc, dv_acc,
    out_buf, own, half_in, plane_in, z_in, x_in, far_in, fin, w_own, w_in,
    ls, a2a_s, a2a_r, gs, gr, hs, hr, ks, kr, ws, wr,
):
    kv = lax.axis_index("kv")
    grp = lax.axis_index("grp")
    prm = lax.axis_index("prompt")
    xh = grp // 4
    z = grp % 4
    zat = lambda d: {"grp": xh * 4 + (z + d) % 4}
    zp, zm, xp = zat(1), zat(3), {"grp": (1 - xh) * 4 + z}
    kvat = lambda d: (kv + d) % 4
    yat = lambda d: {"prompt": (prm + d) % 4}
    my_rows = pl.ds(pl.multiple_of(kv * 64, 64), 64)
    head_cols = lambda who, t: pl.ds(pl.multiple_of(who * 256 + t * HD, HD), HD)

    pair = lambda i: pl.ds(i * 256, 256)
    local = []
    for i in range(8):
        local.append(pltpu.make_async_copy(q_hbm.at[:, pair(i)], ds_ref.at[i, 0:256, :], ls.at[i]))
        local.append(pltpu.make_async_copy(do_hbm.at[:, pair(i)], ds_ref.at[i, 256:512, :], ls.at[8 + i]))
    for t in range(2):
        for i, ref in ((0, pk_hbm), (1, pv_hbm)):
            n = 16 + t * 2 + i
            local.append(pltpu.make_async_copy(ref.at[:, head_cols(kv, t)], sets.at[t, 0, i, my_rows, :], ls.at[n]))
        for i, ref in ((0, rk_hbm), (1, rv_hbm)):
            n = 20 + t * 2 + i
            local.append(pltpu.make_async_copy(ref.at[:, t * HD:(t + 1) * HD], r_kv.at[i, t], ls.at[n]))
    for c in local:
        c.start()

    peers = [{"kv": kvat(d)} for d in (1, 2, 3)] + [zat(d) for d in (1, 2, 3)]
    peers += [yat(d) for d in (1, 2, 3)] + [xp]
    barrier = pltpu.get_barrier_semaphore()
    for peer in peers:
        pl.semaphore_signal(barrier, inc=1, device_id=peer, device_id_type=MESH)
    pl.semaphore_wait(barrier, len(peers))

    def cp(src, dst, ssem, rsem, dev):
        return pltpu.make_async_remote_copy(
            src_ref=src, dst_ref=dst, send_sem=ssem, recv_sem=rsem, device_id=dev, device_id_type=MESH
        )

    def spread(t):
        made = []
        for d in (1, 2, 3):
            for i, ref in ((0, pk_hbm), (1, pv_hbm)):
                n = (d - 1) * 2 + i
                made.append(
                    cp(ref.at[:, head_cols(kvat(d), t)], sets.at[t, 0, i, my_rows, :],
                       a2a_s.at[t, n], a2a_r.at[t, n], {"kv": kvat(d)})
                )
        return made

    lo, hi = pl.ds(0, 128), pl.ds(128, 128)

    def moved(t, n, src, dst, dev, rows=None):
        a, b = sets.at[t, src], sets.at[t, dst]
        if rows is not None:
            a, b = a.at[:, rows], b.at[:, rows]
        return cp(a, b, gs.at[t, n], gr.at[t, n], dev)

    to_x = lambda t: moved(t, 0, 0, 3, xp)
    to_p = lambda t: moved(t, 1, 0, 1, zp)
    to_m = lambda t: moved(t, 2, 0, 2, zm)
    on_p = lambda t: moved(t, 3, 1, 4, zp, lo)
    on_m = lambda t: moved(t, 4, 2, 4, zm, hi)
    xto_p = lambda t: moved(t, 5, 3, 6, zp)
    xto_m = lambda t: moved(t, 6, 3, 5, zm)
    far = lambda t: moved(t, 7, 4, 7, xp)
    gather = [to_x, to_p, to_m, on_p, on_m, xto_p, xto_m, far]
    w_x = cp(w_own.at[0], w_in.at[0], ws.at[0], wr.at[0], xp)
    w_z = [cp(w_own.at[1], w_in.at[d], ws.at[d], wr.at[d], zat(d)) for d in (1, 2, 3)]
    w_y = [cp(w_own.at[2], w_in.at[3 + d], ws.at[3 + d], wr.at[3 + d], yat(d)) for d in (1, 2, 3)]
    def summed(t, n, src, dst, dev):
        return cp(src, dst, hs.at[t, n], hr.at[t, n], dev)

    far_sum = lambda t: summed(t, 0, out_buf.at[t, 7], far_in.at[t], xp)
    half_p = lambda t: summed(t, 1, out_buf.at[t, 4, :, :, lo], half_in.at[t, 0], zp)
    half_m = lambda t: summed(t, 2, out_buf.at[t, 4, :, :, hi], half_in.at[t, 1], zm)
    plane_p = lambda t: summed(t, 3, out_buf.at[t, 5], plane_in.at[t, 0], zp)
    plane_m = lambda t: summed(t, 4, out_buf.at[t, 6], plane_in.at[t, 1], zm)
    z_p = lambda t: summed(t, 5, out_buf.at[t, 2], z_in.at[t, 0], zp)
    z_m = lambda t: summed(t, 6, out_buf.at[t, 1], z_in.at[t, 1], zm)
    x_sum = lambda t: summed(t, 7, out_buf.at[t, 3], x_in.at[t], xp)
    sums = [far_sum, half_p, half_m, plane_p, plane_m, z_p, z_m, x_sum]

    def to_owner(t, d):
        rows = pl.ds(pl.multiple_of(kvat(d) * 64, 64), 64)
        return cp(own.at[t, :, rows, :], fin.at[t, d], ks.at[t, d], kr.at[t, d], {"kv": kvat(d)})

    for c in spread(0):
        c.start()
    w_own[0] = jnp.full((8, 128), rl_ref[0, 0].astype(F32))
    w_x.start()
    for c in local:
        c.wait()

    live = jnp.where(lax.broadcasted_iota(jnp.int32, (HD, SLOTS), 1) < rl_ref[0, 0], 1.0, 0.0).astype(BF)

    def stage_queries(i, _):
        for u in range(2):
            for v in range(2):
                h = i * 4 + u * 2 + v
                half = slice(v * HD, (v + 1) * HD)
                q_t[h] = ds_ref[i * 2 + u, 0:256, half].T
                d_t[h] = ds_ref[i * 2 + u, 256:512, half].T * live
        return 0

    lax.fori_loop(0, HEADS // 4, stage_queries, 0)
    for t in range(2):
        k_n[t, RESP_AT:, :] = r_kv[0, t]
        k_t[t, :, RESP_AT:] = r_kv[0, t].T
        v_t[t, 0:HD, RESP_AT:] = r_kv[1, t].T
        v_t[t, HD:, RESP_AT:] = jnp.ones((16, SET), BF)

    plen = pl_ref[0]

    def valid_keys(s, shape, axis):
        dx, dz = SETS[s]
        owner = (xh if dx == 0 else 1 - xh) * 4 + (z + dz) % 4
        r = lax.broadcasted_iota(jnp.int32, shape, axis)
        return jnp.where((r // 64) * 512 + r % 64 < plen - owner * 64, 1.0, 0.0).astype(BF)

    def put_set(t, s):
        by_row = valid_keys(s, (SET, HD), 0)
        by_col = valid_keys(s, (16, SET), 1)
        start = (s - 1) * SET if s else OWN_AT
        at = slice(start, start + SET)
        k = sets[t, s, 0]
        k_n[t, at, :] = k * by_row + k[0:1, :] * (1 - by_row)
        k_t[t, :, at] = k.T * by_col[0:1, :]
        v_t[t, 0:HD, at] = sets[t, s, 1].T * by_col[0:1, :]
        v_t[t, HD:, at] = by_col

    s_bufs, ds_bufs, dc_bufs = (s_a, s_b), (ds_a, ds_b), (dc_a, dc_b)

    def scores(t, j, u, rows, at, mask):
        h = t * QPG + u
        top = None
        for r in range(0, rows, 256):
            s = dot(k_n[t, pl.ds(at + r, 256), :], q_t[h], NN) * (SCALE * LOG2E)
            if mask is not None and r:
                s = jnp.where(mask, s, -1e30)
            s_bufs[u % 2][r:r + 256, :] = s
            b = jnp.max(s.reshape(32, 8, SLOTS), 0)
            top = b if top is None else jnp.maximum(top, b)
            yield
        m = jnp.max(top, 0, keepdims=True)
        mc[j, h] = m if mask is not None else jnp.maximum(mc[j - 1, h], m)

    def weights(t, j, u, rows, at):
        h = t * QPG + u
        m = mc[j, h]
        for r in range(0, rows, 256):
            p = jnp.exp2(s_bufs[u % 2][r:r + 256, :] - m).astype(BF)
            p_ref[h, pl.ds(at + r, 256), :] = p
            ds_bufs[u % 2][r:r + 256, :] = p
            yield

    def attend(t, j, u, rows, at, first):
        h = t * QPG + u
        new = dot(v_t[t, :, pl.ds(at, rows)], ds_bufs[u % 2][0:rows, :], NN)
        yield
        o_acc[h] = new if first else o_acc[h] * jnp.exp2(mc[j - 1, h] - mc[j, h]) + new

    def forward(t, j, rows, at, mask):
        for u in range(QPG + 2):
            steps = []
            if u < QPG:
                steps.append(scores(t, j, u, rows, at, mask))
            if 0 <= u - 1 < QPG:
                steps.append(weights(t, j, u - 1, rows, at))
            if 0 <= u - 2:
                steps.append(attend(t, j, u - 2, rows, at, mask is not None))
            while steps:
                for step in list(steps):
                    try:
                        next(step)
                    except StopIteration:
                        steps.remove(step)

    def weigh(t, j, u, rows, at, values):
        h = t * QPG + u
        corr = jnp.exp2(mc[j, h] - lse[h])
        dc = (d_t[h].astype(F32) * corr).astype(BF)
        dc_bufs[u % 2][...] = dc
        cd = corr * delta[h]
        for r in range(0, rows, 256):
            dp = dot(values(r), dc, NN) - cd
            ds = p_ref[h, pl.ds(at + r, 256), :] * dp.astype(BF)
            ds_bufs[u % 2][r:r + 256, :] = ds
            ds_ref[h, pl.ds(at + r, 256), :] = ds

    def key_sums(t, u, rows, at):
        h = t * QPG + u
        for r in range(0, rows, 256):
            dv = dot(dc_bufs[u % 2][...], p_ref[h, pl.ds(at + r, 256), :], NT)
            dk = dot(q_t[h], ds_bufs[u % 2][r:r + 256, :], NT)
            if u == 0:
                dv_acc[:, r:r + 256] = dv
                dk_acc[:, r:r + 256] = dk
            else:
                dv_acc[:, r:r + 256] += dv
                dk_acc[:, r:r + 256] += dk

    def backward(t, j, rows, at, values):
        for u in range(QPG + 1):
            if u < QPG:
                weigh(t, j, u, rows, at, values)
            if u > 0:
                key_sums(t, u - 1, rows, at)

    def query_sums(t):
        for u in range(QPG):
            h = t * QPG + u
            dq = dot(k_t[t], ds_ref[h], NN) * (w2 * SCALE)
            p_ref[t * 4 + u // 2, 0:256, (u % 2) * HD:(u % 2 + 1) * HD] = dq.astype(BF).T

    for c in spread(0):
        c.wait_recv()
    for c in (to_x, to_p, to_m):
        c(0).start()
    for c in spread(1):
        c.start()
    row_at = lax.broadcasted_iota(jnp.int32, (SET, SLOTS), 0)
    slot_at = lax.broadcasted_iota(jnp.int32, (SET, SLOTS), 1)
    causal = (row_at <= slot_at) & (row_at < rl_ref[0, 0])

    def first_chunk(t, _):
        @pl.when(t == 1)
        def _():
            for c in spread(1):
                c.wait_recv()

        put_set(t, 0)
        forward(t, 0, PC, OWN_AT, causal)
        return 0

    lax.fori_loop(0, 2, first_chunk, 0)
    w_x.wait_recv()
    w_own[1] = w_own[0] + w_in[0]
    for c in w_z:
        c.start()

    def owner_sum(t):
        z_p(t).wait_recv()
        z_m(t).wait_recv()
        x_sum(t).wait_recv()
        for i in range(2):
            total = out_buf[t, 0, i].astype(F32) + z_in[t, 0, i].astype(F32)
            total = total + (z_in[t, 1, i].astype(F32) + x_in[t, i].astype(F32))
            own[t, i] = total.astype(BF).T
        for d in (1, 2, 3):
            to_owner(t, d).start()

    def plane_sums(t):
        plane_p(t).wait_recv()
        plane_m(t).wait_recv()
        total = plane_in[t, 0].astype(F32) + plane_in[t, 1].astype(F32)
        out_buf[t, 3] = (out_buf[t, 3].astype(F32) + total).astype(BF)
        x_sum(t).start()

    def half_sums(t):
        half_p(t).wait_recv()
        out_buf[t, 2, :, :, 0:128] = (
            out_buf[t, 2, :, :, 0:128].astype(F32) + half_in[t, 0].astype(F32)
        ).astype(BF)
        z_p(t).start()
        half_m(t).wait_recv()
        out_buf[t, 1, :, :, 128:256] = (
            out_buf[t, 1, :, :, 128:256].astype(F32) + half_in[t, 1].astype(F32)
        ).astype(BF)
        z_m(t).start()

    def far_sums(t):
        far_sum(t).wait_recv()
        out_buf[t, 4] = (out_buf[t, 4].astype(F32) + far_in[t].astype(F32)).astype(BF)
        half_p(t).start()
        half_m(t).start()

    def fwd_chunk(t, c):
        first = t == 0

        @pl.when(c == 1)
        def _():
            @pl.when(first)
            def _():
                to_p(0).wait_recv()
                on_p(0).start()
                to_m(0).wait_recv()
                on_m(0).start()
                to_x(0).wait_recv()
                xto_p(0).start()
                xto_m(0).start()

            put_set(t, 1)
            put_set(t, 2)

        @pl.when(c == 2)
        def _():
            @pl.when(first)
            def _():
                on_p(0).wait_recv()
                on_m(0).wait_recv()
                far(0).start()
                for w in w_z:
                    w.wait_recv()
                w_own[2] = w_own[1] + (w_in[1] + w_in[2] + w_in[3])
                for w in w_y:
                    w.start()

            @pl.when(jnp.logical_not(first))
            def _():
                on_p(1).wait_recv()
                on_m(1).wait_recv()
                far(1).start()

            put_set(t, 3)
            put_set(t, 4)

        @pl.when(c == 3)
        def _():
            xto_p(t).wait_recv()
            xto_m(t).wait_recv()

            @pl.when(first)
            def _():
                for o in (to_x, to_p, to_m):
                    o(1).start()

            put_set(t, 5)
            put_set(t, 6)

        forward(t, c, PC, pl.multiple_of((c - 1) * PC, PC), None)

    def finish_fwd(t):
        for u in range(QPG):
            h = t * QPG + u
            o = o_acc[h]
            total = o[HD:HD + 1, :]
            out = (o[0:HD, :] * (1.0 / total)).astype(BF)
            o_out[t * 4 + u // 2, :, (u % 2) * HD:(u % 2 + 1) * HD] = out.T
            delta[h] = jnp.sum(out.astype(F32) * d_t[h].astype(F32), 0, keepdims=True)
            lse[h] = mc[4, h] + jnp.log2(total)

    def put_out(t, s, i):
        cols = slice(i * SET, (i + 1) * SET)
        out_buf[t, s, 0] = dk_acc[:, cols].astype(BF)
        out_buf[t, s, 1] = dv_acc[:, cols].astype(BF)

    def bwd_step(t, n):
        s = t * (1 - n % 2)
        c = 3 - t * ((n + 1) // 2)

        @pl.when(t == 0)
        def _():
            to_p(1).wait_recv()
            on_p(1).start()
            to_m(1).wait_recv()
            on_m(1).start()
            to_x(1).wait_recv()
            xto_p(1).start()
            xto_m(1).start()

        backward(s, c, PC, pl.multiple_of((c - 1) * PC, PC), lambda r: sets[s, 2 * c - 1 + r // SET, 1])
        put_out(s, 2 * c - 1, 0)
        put_out(s, 2 * c, 1)

        @pl.when(n == 0)
        def _():
            plane_p(s).start()
            plane_m(s).start()

        @pl.when(n == 1)
        def _():
            far_sums(0)
            plane_sums(0)

        @pl.when(n == 2)
        def _():
            far_sums(1)

        @pl.when(n == 3)
        def _():
            half_sums(0)
            plane_sums(1)

        @pl.when(n == 4)
        def _():
            half_sums(1)

    def own_chunk(t):
        backward(t, 0, PC, OWN_AT, lambda r: sets[t, 0, 1] if r == 0 else r_kv[1, t])
        put_out(t, 0, 0)
        head = slice(t * HD, (t + 1) * HD)
        drk_ref[:, head] = (dk_acc[:, SET:] * (w2 * SCALE)).T.astype(BF)
        drv_ref[:, head] = (dv_acc[:, SET:] * w2).T.astype(BF)

    def o_copy(i):
        return pltpu.make_async_copy(o_out.at[i], o_hbm.at[:, pair(i)], ls.at[i])

    def both(t, _):
        lax.fori_loop(1, 4, lambda c, _: (fwd_chunk(t, c), 0)[1], 0)
        far(t).wait_recv()
        put_set(t, 7)
        forward(t, 4, SET, LAST_AT, None)
        finish_fwd(t)
        backward(t, 4, SET, LAST_AT, lambda r: sets[t, 7, 1])
        put_out(t, 7, 0)
        far_sum(t).start()
        lax.fori_loop(0, 1 + 4 * t, lambda n, _: (bwd_step(t, n), 0)[1], 0)
        return 0

    lax.fori_loop(0, 2, both, 0)
    for i in range(8):
        o_copy(i).start()
    for w in w_y:
        w.wait_recv()
    count = w_own[2] + (w_in[4] + w_in[5] + w_in[6])
    weight = (8192.0 / count)[0:1, :]
    w2 = cat([weight, weight], 1)

    def dq_copy(i):
        return pltpu.make_async_copy(p_ref.at[i, 0:256, :], dq_hbm.at[:, pair(i)], ls.at[8 + i])

    def finish_queries(t):
        query_sums(t)
        for i in range(t * 4, t * 4 + 4):
            dq_copy(i).start()

    own_chunk(1)
    own_chunk(0)
    owner_sum(0)
    finish_queries(1)
    owner_sum(1)
    finish_queries(0)

    mine = lax.broadcasted_iota(jnp.int32, (64, HD), 0) + (kv * 8 + grp) * 64 < plen
    for t in range(2):
        for d in range(4):
            cols = head_cols(kvat(4 - d), t)
            if d == 0:
                got_k, got_v = own[t, 0, my_rows, :], own[t, 1, my_rows, :]
            else:
                to_owner(t, d).wait_recv()
                got_k, got_v = fin[t, d, 0], fin[t, d, 1]
            dpk_ref[:, cols] = jnp.where(mine, got_k.astype(F32) * (weight * SCALE), 0.0)
            dpv_ref[:, cols] = jnp.where(mine, got_v.astype(F32) * weight, 0.0)

    for t in range(2):
        for c in spread(t) + [g(t) for g in gather] + [s(t) for s in sums] + [to_owner(t, d) for d in (1, 2, 3)]:
            c.wait_send()
    for c in [w_x] + w_z + w_y:
        c.wait_send()
    for i in range(8):
        o_copy(i).wait()
        dq_copy(i).wait()


def hand_over(*refs):
    ins, outs, held, (in_sem, out_sem) = refs[0:6], refs[6:12], refs[12:18], refs[18:]
    pieces = []
    for i in range(6):
        parts = 8 if i < 2 else 1
        rows = ins[i].shape[0] // parts
        for j in range(parts):
            pieces.append((i, pl.ds(j * rows, rows)))
    into = [
        pltpu.make_async_copy(ins[i].at[r], held[i].at[r], in_sem.at[n]) for n, (i, r) in enumerate(pieces)
    ]
    out = [
        pltpu.make_async_copy(held[i].at[r], outs[i].at[r], out_sem.at[n]) for n, (i, r) in enumerate(pieces)
    ]
    for c in into:
        c.start()
    for a, b in zip(into, out):
        a.wait()
        b.start()
    for c in out:
        c.wait()


def on_device(
    queries, resp_keys, resp_values, prompt_keys, prompt_values, grad_out, resp_len, prompt_len
):
    vm = pl.BlockSpec(memory_space=pltpu.VMEM)
    sm = pl.BlockSpec(memory_space=pltpu.SMEM)
    hbm = pl.BlockSpec(memory_space=pl.ANY)
    shape = jax.ShapeDtypeStruct
    dma = pltpu.SemaphoreType.DMA
    shapes = [
        shape((256, 2048), BF), shape((256, 2048), BF), shape((256, 256), BF), shape((256, 256), BF),
        shape((64, 1024), F32), shape((64, 1024), F32),
    ]
    outs = pl.pallas_call(
        kernel,
        out_shape=shapes,
        in_specs=[sm, sm] + [hbm] * 6,
        out_specs=[hbm, hbm] + [vm] * 4,
        scratch_shapes=[
            pltpu.VMEM((2, 8, 2, SET, HD), BF),
            pltpu.VMEM((HEADS, KEYS, SLOTS), BF),
            pltpu.VMEM((HEADS, KEYS, SLOTS), BF),
            pltpu.VMEM((HEADS, HD + 16, SLOTS), F32),
            pltpu.VMEM((8, SLOTS, 256), BF),
            pltpu.VMEM((5, HEADS, 1, SLOTS), F32),
            pltpu.VMEM((HEADS, 1, SLOTS), F32),
            pltpu.VMEM((HEADS, 1, SLOTS), F32),
            pltpu.VMEM((2, KEYS, HD), BF),
            pltpu.VMEM((2, HD, KEYS), BF),
            pltpu.VMEM((2, HD + 16, KEYS), BF),
            pltpu.VMEM((2, 2, SET, HD), BF),
            pltpu.VMEM((HEADS, HD, SLOTS), BF),
            pltpu.VMEM((HEADS, HD, SLOTS), BF),
            pltpu.VMEM((PC, SLOTS), F32),
            pltpu.VMEM((PC, SLOTS), F32),
            pltpu.VMEM((PC, SLOTS), BF),
            pltpu.VMEM((PC, SLOTS), BF),
            pltpu.VMEM((HD, SLOTS), BF),
            pltpu.VMEM((HD, SLOTS), BF),
            pltpu.VMEM((HD, PC), F32),
            pltpu.VMEM((HD, PC), F32),
            pltpu.VMEM((2, 8, 2, HD, SET), BF),
            pltpu.VMEM((2, 2, SET, HD), BF),
            pltpu.VMEM((2, 2, 2, HD, 128), BF),
            pltpu.VMEM((2, 2, 2, HD, SET), BF),
            pltpu.VMEM((2, 2, 2, HD, SET), BF),
            pltpu.VMEM((2, 2, HD, SET), BF),
            pltpu.VMEM((2, 2, HD, SET), BF),
            pltpu.VMEM((2, 4, 2, 64, HD), BF),
            pltpu.VMEM((3, 8, 128), F32),
            pltpu.VMEM((7, 8, 128), F32),
            dma((24,)), dma((2, 6)), dma((2, 6)), dma((2, 8)), dma((2, 8)), dma((2, 8)), dma((2, 8)),
            dma((2, 4)), dma((2, 4)), dma((7,)), dma((7,)),
        ],
        compiler_params=pltpu.CompilerParams(
            collective_id=0, has_side_effects=True, vmem_limit_bytes=62 * 2**20
        ),
        name="attention",
    )(
        resp_len, prompt_len, queries.reshape(256, 2048), grad_out.reshape(256, 2048),
        resp_keys.reshape(256, 256), resp_values.reshape(256, 256),
        prompt_keys.reshape(64, 1024), prompt_values.reshape(64, 1024),
    )
    attended, grad_q, grad_rk, grad_rv, grad_pk, grad_pv = pl.pallas_call(
        hand_over,
        out_shape=shapes,
        in_specs=[hbm] * 6,
        out_specs=[hbm] * 6,
        scratch_shapes=[pltpu.VMEM(a.shape, a.dtype) for a in shapes] + [dma((20,)), dma((20,))],
        name="hand_over",
    )(*outs)
    return (
        attended.reshape(queries.shape),
        grad_q.reshape(queries.shape),
        grad_rk.reshape(resp_keys.shape),
        grad_rv.reshape(resp_values.shape),
        grad_pk.reshape(1, 64, 1024),
        grad_pv.reshape(1, 64, 1024),
    )


def solution(mesh):
    wide = P("prompt", "grp", None, "kv")
    rows = P("prompt", ("kv", "grp"), None)
    return jax.shard_map(
        on_device,
        mesh=mesh,
        in_specs=(wide, wide, wide, rows, rows, wide, P("prompt", "grp"), P("prompt")),
        out_specs=(wide, wide, wide, wide, rows, rows),
        check_vma=False,
    )
```

```python
import jax
import jax.numpy as jnp
from jax import lax
from jax.experimental import pallas as pl
from jax.experimental.pallas import tpu as pltpu
from jax.sharding import PartitionSpec as P

F32 = jnp.float32
BF = jnp.bfloat16
MESH = pl.DeviceIdType.MESH
HD = 128
QPG = 8
SCALE = HD ** (-0.5)
LOG2E = 1.4426950408889634
NT = (((1,), (1,)), ((), ()))
NN = (((1,), (0,)), ((), ()))
SET = 256
PC = 512
HEADS = 16
SLOTS = 256
RESP_AT = 2048
KEYS = 2304
OWN_AT = 1792
LAST_AT = 1536
SETS = ((0, 0), (0, 3), (0, 1), (1, 0), (0, 2), (1, 1), (1, 3), (1, 2))


def dot(a, b, dims):
    return lax.dot_general(a, b, dims, preferred_element_type=F32)


def cat(parts, axis):
    return parts[0] if len(parts) == 1 else jnp.concatenate(parts, axis)


def kernel(
    rl_ref, pl_ref, q_hbm, do_hbm, rk_hbm, rv_hbm, pk_hbm, pv_hbm,
    o_hbm, dq_hbm, drk_ref, drv_ref, dpk_ref, dpv_ref,
    sets, p_ref, ds_ref, o_acc, o_out, mc, lse, delta, k_n, k_t, v_t, r_kv, q_t, d_t,
    s_a, s_b, ds_a, ds_b, dc_a, dc_b, dk_acc, dv_acc,
    out_buf, own, half_in, plane_in, z_in, x_in, far_in, fin, w_own, w_in,
    ls, a2a_s, a2a_r, gs, gr, hs, hr, ks, kr, ws, wr,
):
    kv = lax.axis_index("kv")
    grp = lax.axis_index("grp")
    prm = lax.axis_index("prompt")
    xh = grp // 4
    z = grp % 4
    zat = lambda d: {"grp": xh * 4 + (z + d) % 4}
    zp, zm, xp = zat(1), zat(3), {"grp": (1 - xh) * 4 + z}
    kvat = lambda d: (kv + d) % 4
    yat = lambda d: {"prompt": (prm + d) % 4}
    my_rows = pl.ds(pl.multiple_of(kv * 64, 64), 64)
    head_cols = lambda who, t: pl.ds(pl.multiple_of(who * 256 + t * HD, HD), HD)

    pair = lambda i: pl.ds(i * 256, 256)
    local = []
    for i in range(8):
        local.append(pltpu.make_async_copy(q_hbm.at[:, pair(i)], ds_ref.at[i, 0:256, :], ls.at[i]))
        local.append(pltpu.make_async_copy(do_hbm.at[:, pair(i)], ds_ref.at[i, 256:512, :], ls.at[8 + i]))
    for t in range(2):
        for i, ref in ((0, pk_hbm), (1, pv_hbm)):
            n = 16 + t * 2 + i
            local.append(pltpu.make_async_copy(ref.at[:, head_cols(kv, t)], sets.at[t, 0, i, my_rows, :], ls.at[n]))
        for i, ref in ((0, rk_hbm), (1, rv_hbm)):
            n = 20 + t * 2 + i
            local.append(pltpu.make_async_copy(ref.at[:, t * HD:(t + 1) * HD], r_kv.at[i, t], ls.at[n]))
    for c in local:
        c.start()

    peers = [{"kv": kvat(d)} for d in (1, 2, 3)] + [zat(d) for d in (1, 2, 3)]
    peers += [yat(d) for d in (1, 2, 3)] + [xp]
    barrier = pltpu.get_barrier_semaphore()
    for peer in peers:
        pl.semaphore_signal(barrier, inc=1, device_id=peer, device_id_type=MESH)
    pl.semaphore_wait(barrier, len(peers))

    def cp(src, dst, ssem, rsem, dev):
        return pltpu.make_async_remote_copy(
            src_ref=src, dst_ref=dst, send_sem=ssem, recv_sem=rsem, device_id=dev, device_id_type=MESH
        )

    def spread(t):
        made = []
        for d in (1, 2, 3):
            for i, ref in ((0, pk_hbm), (1, pv_hbm)):
                n = (d - 1) * 2 + i
                made.append(
                    cp(ref.at[:, head_cols(kvat(d), t)], sets.at[t, 0, i, my_rows, :],
                       a2a_s.at[t, n], a2a_r.at[t, n], {"kv": kvat(d)})
                )
        return made

    lo, hi = pl.ds(0, 128), pl.ds(128, 128)

    def moved(t, n, src, dst, dev, rows=None):
        a, b = sets.at[t, src], sets.at[t, dst]
        if rows is not None:
            a, b = a.at[:, rows], b.at[:, rows]
        return cp(a, b, gs.at[t, n], gr.at[t, n], dev)

    to_x = lambda t: moved(t, 0, 0, 3, xp)
    to_p = lambda t: moved(t, 1, 0, 1, zp)
    to_m = lambda t: moved(t, 2, 0, 2, zm)
    on_p = lambda t: moved(t, 3, 1, 4, zp, lo)
    on_m = lambda t: moved(t, 4, 2, 4, zm, hi)
    xto_p = lambda t: moved(t, 5, 3, 6, zp)
    xto_m = lambda t: moved(t, 6, 3, 5, zm)
    far = lambda t: moved(t, 7, 4, 7, xp)
    gather = [to_x, to_p, to_m, on_p, on_m, xto_p, xto_m, far]
    w_x = cp(w_own.at[0], w_in.at[0], ws.at[0], wr.at[0], xp)
    w_z = [cp(w_own.at[1], w_in.at[d], ws.at[d], wr.at[d], zat(d)) for d in (1, 2, 3)]
    w_y = [cp(w_own.at[2], w_in.at[3 + d], ws.at[3 + d], wr.at[3 + d], yat(d)) for d in (1, 2, 3)]
    def summed(t, n, src, dst, dev):
        return cp(src, dst, hs.at[t, n], hr.at[t, n], dev)

    far_sum = lambda t: summed(t, 0, out_buf.at[t, 7], far_in.at[t], xp)
    half_p = lambda t: summed(t, 1, out_buf.at[t, 4, :, :, lo], half_in.at[t, 0], zp)
    half_m = lambda t: summed(t, 2, out_buf.at[t, 4, :, :, hi], half_in.at[t, 1], zm)
    plane_p = lambda t: summed(t, 3, out_buf.at[t, 5], plane_in.at[t, 0], zp)
    plane_m = lambda t: summed(t, 4, out_buf.at[t, 6], plane_in.at[t, 1], zm)
    z_p = lambda t: summed(t, 5, out_buf.at[t, 2], z_in.at[t, 0], zp)
    z_m = lambda t: summed(t, 6, out_buf.at[t, 1], z_in.at[t, 1], zm)
    x_sum = lambda t: summed(t, 7, out_buf.at[t, 3], x_in.at[t], xp)
    sums = [far_sum, half_p, half_m, plane_p, plane_m, z_p, z_m, x_sum]

    def to_owner(t, d):
        rows = pl.ds(pl.multiple_of(kvat(d) * 64, 64), 64)
        return cp(own.at[t, :, rows, :], fin.at[t, d], ks.at[t, d], kr.at[t, d], {"kv": kvat(d)})

    for c in spread(0):
        c.start()
    w_own[0] = jnp.full((8, 128), rl_ref[0, 0].astype(F32))
    w_x.start()
    for c in local:
        c.wait()

    live = jnp.where(lax.broadcasted_iota(jnp.int32, (HD, SLOTS), 1) < rl_ref[0, 0], 1.0, 0.0).astype(BF)

    def stage_queries(i, _):
        for u in range(2):
            for v in range(2):
                h = i * 4 + u * 2 + v
                half = slice(v * HD, (v + 1) * HD)
                q_t[h] = ds_ref[i * 2 + u, 0:256, half].T
                d_t[h] = ds_ref[i * 2 + u, 256:512, half].T * live
        return 0

    lax.fori_loop(0, HEADS // 4, stage_queries, 0)
    for t in range(2):
        k_n[t, RESP_AT:, :] = r_kv[0, t]
        k_t[t, :, RESP_AT:] = r_kv[0, t].T
        v_t[t, 0:HD, RESP_AT:] = r_kv[1, t].T
        v_t[t, HD:, RESP_AT:] = jnp.ones((16, SET), BF)

    plen = pl_ref[0]

    def valid_keys(s, shape, axis):
        dx, dz = SETS[s]
        owner = (xh if dx == 0 else 1 - xh) * 4 + (z + dz) % 4
        r = lax.broadcasted_iota(jnp.int32, shape, axis)
        return jnp.where((r // 64) * 512 + r % 64 < plen - owner * 64, 1.0, 0.0).astype(BF)

    def put_set(t, s):
        by_row = valid_keys(s, (SET, HD), 0)
        by_col = valid_keys(s, (16, SET), 1)
        start = (s - 1) * SET if s else OWN_AT
        at = slice(start, start + SET)
        k = sets[t, s, 0]
        k_n[t, at, :] = k * by_row + k[0:1, :] * (1 - by_row)
        k_t[t, :, at] = k.T * by_col[0:1, :]
        v_t[t, 0:HD, at] = sets[t, s, 1].T * by_col[0:1, :]
        v_t[t, HD:, at] = by_col

    s_bufs, ds_bufs, dc_bufs = (s_a, s_b), (ds_a, ds_b), (dc_a, dc_b)

    def scores(t, j, u, rows, at, mask):
        h = t * QPG + u
        top = None
        for r in range(0, rows, 256):
            s = dot(k_n[t, pl.ds(at + r, 256), :], q_t[h], NN) * (SCALE * LOG2E)
            if mask is not None and r:
                s = jnp.where(mask, s, -1e30)
            s_bufs[u % 2][r:r + 256, :] = s
            b = jnp.max(s.reshape(32, 8, SLOTS), 0)
            top = b if top is None else jnp.maximum(top, b)
            yield
        m = jnp.max(top, 0, keepdims=True)
        mc[j, h] = m if mask is not None else jnp.maximum(mc[j - 1, h], m)

    def weights(t, j, u, rows, at):
        h = t * QPG + u
        m = mc[j, h]
        for r in range(0, rows, 256):
            p = jnp.exp2(s_bufs[u % 2][r:r + 256, :] - m).astype(BF)
            p_ref[h, pl.ds(at + r, 256), :] = p
            ds_bufs[u % 2][r:r + 256, :] = p
            yield

    def attend(t, j, u, rows, at, first):
        h = t * QPG + u
        new = dot(v_t[t, :, pl.ds(at, rows)], ds_bufs[u % 2][0:rows, :], NN)
        yield
        o_acc[h] = new if first else o_acc[h] * jnp.exp2(mc[j - 1, h] - mc[j, h]) + new

    def forward(t, j, rows, at, mask):
        for u in range(QPG + 2):
            steps = []
            if u < QPG:
                steps.append(scores(t, j, u, rows, at, mask))
            if 0 <= u - 1 < QPG:
                steps.append(weights(t, j, u - 1, rows, at))
            if 0 <= u - 2:
                steps.append(attend(t, j, u - 2, rows, at, mask is not None))
            while steps:
                for step in list(steps):
                    try:
                        next(step)
                    except StopIteration:
                        steps.remove(step)

    def weigh(t, j, u, rows, at, values):
        h = t * QPG + u
        corr = jnp.exp2(mc[j, h] - lse[h])
        dc = (d_t[h].astype(F32) * corr).astype(BF)
        dc_bufs[u % 2][...] = dc
        cd = corr * delta[h]
        for r in range(0, rows, 256):
            dp = dot(values(r), dc, NN) - cd
            ds = p_ref[h, pl.ds(at + r, 256), :] * dp.astype(BF)
            ds_bufs[u % 2][r:r + 256, :] = ds
            ds_ref[h, pl.ds(at + r, 256), :] = ds

    def key_sums(t, u, rows, at):
        h = t * QPG + u
        for r in range(0, rows, 256):
            dv = dot(dc_bufs[u % 2][...], p_ref[h, pl.ds(at + r, 256), :], NT)
            dk = dot(q_t[h], ds_bufs[u % 2][r:r + 256, :], NT)
            if u == 0:
                dv_acc[:, r:r + 256] = dv
                dk_acc[:, r:r + 256] = dk
            else:
                dv_acc[:, r:r + 256] += dv
                dk_acc[:, r:r + 256] += dk

    def backward(t, j, rows, at, values):
        for u in range(QPG + 1):
            if u < QPG:
                weigh(t, j, u, rows, at, values)
            if u > 0:
                key_sums(t, u - 1, rows, at)

    def query_sums(t):
        for u in range(QPG):
            h = t * QPG + u
            dq = dot(k_t[t], ds_ref[h], NN) * (w2 * SCALE)
            p_ref[t * 4 + u // 2, 0:256, (u % 2) * HD:(u % 2 + 1) * HD] = dq.astype(BF).T

    for c in spread(0):
        c.wait_recv()
    for c in (to_x, to_p, to_m):
        c(0).start()
    for c in spread(1):
        c.start()
    row_at = lax.broadcasted_iota(jnp.int32, (SET, SLOTS), 0)
    slot_at = lax.broadcasted_iota(jnp.int32, (SET, SLOTS), 1)
    causal = (row_at <= slot_at) & (row_at < rl_ref[0, 0])

    def first_chunk(t, _):
        @pl.when(t == 1)
        def _():
            for c in spread(1):
                c.wait_recv()

        put_set(t, 0)
        forward(t, 0, PC, OWN_AT, causal)
        return 0

    lax.fori_loop(0, 2, first_chunk, 0)
    w_x.wait_recv()
    w_own[1] = w_own[0] + w_in[0]
    for c in w_z:
        c.start()

    def owner_sum(t):
        z_p(t).wait_recv()
        z_m(t).wait_recv()
        x_sum(t).wait_recv()
        for i in range(2):
            total = out_buf[t, 0, i].astype(F32) + z_in[t, 0, i].astype(F32)
            total = total + (z_in[t, 1, i].astype(F32) + x_in[t, i].astype(F32))
            own[t, i] = total.astype(BF).T
        for d in (1, 2, 3):
            to_owner(t, d).start()

    def plane_sums(t):
        plane_p(t).wait_recv()
        plane_m(t).wait_recv()
        total = plane_in[t, 0].astype(F32) + plane_in[t, 1].astype(F32)
        out_buf[t, 3] = (out_buf[t, 3].astype(F32) + total).astype(BF)
        x_sum(t).start()

    def half_sums(t):
        half_p(t).wait_recv()
        out_buf[t, 2, :, :, 0:128] = (
            out_buf[t, 2, :, :, 0:128].astype(F32) + half_in[t, 0].astype(F32)
        ).astype(BF)
        z_p(t).start()
        half_m(t).wait_recv()
        out_buf[t, 1, :, :, 128:256] = (
            out_buf[t, 1, :, :, 128:256].astype(F32) + half_in[t, 1].astype(F32)
        ).astype(BF)
        z_m(t).start()

    def far_sums(t):
        far_sum(t).wait_recv()
        out_buf[t, 4] = (out_buf[t, 4].astype(F32) + far_in[t].astype(F32)).astype(BF)
        half_p(t).start()
        half_m(t).start()

    def fwd_chunk(t, c):
        first = t == 0

        @pl.when(c == 1)
        def _():
            @pl.when(first)
            def _():
                to_p(0).wait_recv()
                on_p(0).start()
                to_m(0).wait_recv()
                on_m(0).start()
                to_x(0).wait_recv()
                xto_p(0).start()
                xto_m(0).start()

            put_set(t, 1)
            put_set(t, 2)

        @pl.when(c == 2)
        def _():
            @pl.when(first)
            def _():
                on_p(0).wait_recv()
                on_m(0).wait_recv()
                far(0).start()
                for w in w_z:
                    w.wait_recv()
                w_own[2] = w_own[1] + (w_in[1] + w_in[2] + w_in[3])
                for w in w_y:
                    w.start()

            @pl.when(jnp.logical_not(first))
            def _():
                on_p(1).wait_recv()
                on_m(1).wait_recv()
                far(1).start()

            put_set(t, 3)
            put_set(t, 4)

        @pl.when(c == 3)
        def _():
            xto_p(t).wait_recv()
            xto_m(t).wait_recv()

            @pl.when(first)
            def _():
                for o in (to_x, to_p, to_m):
                    o(1).start()

            put_set(t, 5)
            put_set(t, 6)

        forward(t, c, PC, pl.multiple_of((c - 1) * PC, PC), None)

    def finish_fwd(t):
        for u in range(QPG):
            h = t * QPG + u
            o = o_acc[h]
            total = o[HD:HD + 1, :]
            out = (o[0:HD, :] * (1.0 / total)).astype(BF)
            o_out[t * 4 + u // 2, :, (u % 2) * HD:(u % 2 + 1) * HD] = out.T
            delta[h] = jnp.sum(out.astype(F32) * d_t[h].astype(F32), 0, keepdims=True)
            lse[h] = mc[4, h] + jnp.log2(total)

    def put_out(t, s, i):
        cols = slice(i * SET, (i + 1) * SET)
        out_buf[t, s, 0] = dk_acc[:, cols].astype(BF)
        out_buf[t, s, 1] = dv_acc[:, cols].astype(BF)

    def bwd_step(t, n):
        s = t * (1 - n % 2)
        c = 3 - t * ((n + 1) // 2)

        @pl.when(t == 0)
        def _():
            to_p(1).wait_recv()
            on_p(1).start()
            to_m(1).wait_recv()
            on_m(1).start()
            to_x(1).wait_recv()
            xto_p(1).start()
            xto_m(1).start()

        backward(s, c, PC, pl.multiple_of((c - 1) * PC, PC), lambda r: sets[s, 2 * c - 1 + r // SET, 1])
        put_out(s, 2 * c - 1, 0)
        put_out(s, 2 * c, 1)

        @pl.when(n == 0)
        def _():
            plane_p(s).start()
            plane_m(s).start()

        @pl.when(n == 1)
        def _():
            far_sums(0)
            plane_sums(0)

        @pl.when(n == 2)
        def _():
            far_sums(1)

        @pl.when(n == 3)
        def _():
            half_sums(0)
            plane_sums(1)

        @pl.when(n == 4)
        def _():
            half_sums(1)

    def own_chunk(t):
        backward(t, 0, PC, OWN_AT, lambda r: sets[t, 0, 1] if r == 0 else r_kv[1, t])
        put_out(t, 0, 0)
        head = slice(t * HD, (t + 1) * HD)
        drk_ref[:, head] = (dk_acc[:, SET:] * (w2 * SCALE)).T.astype(BF)
        drv_ref[:, head] = (dv_acc[:, SET:] * w2).T.astype(BF)

    def o_copy(i):
        return pltpu.make_async_copy(o_out.at[i], o_hbm.at[:, pair(i)], ls.at[i])

    def both(t, _):
        lax.fori_loop(1, 4, lambda c, _: (fwd_chunk(t, c), 0)[1], 0)
        far(t).wait_recv()
        put_set(t, 7)
        forward(t, 4, SET, LAST_AT, None)
        finish_fwd(t)
        backward(t, 4, SET, LAST_AT, lambda r: sets[t, 7, 1])
        put_out(t, 7, 0)
        far_sum(t).start()
        lax.fori_loop(0, 1 + 4 * t, lambda n, _: (bwd_step(t, n), 0)[1], 0)
        return 0

    lax.fori_loop(0, 2, both, 0)
    for i in range(8):
        o_copy(i).start()
    for w in w_y:
        w.wait_recv()
    count = w_own[2] + (w_in[4] + w_in[5] + w_in[6])
    weight = (8192.0 / count)[0:1, :]
    w2 = cat([weight, weight], 1)

    def dq_copy(i):
        return pltpu.make_async_copy(p_ref.at[i, 0:256, :], dq_hbm.at[:, pair(i)], ls.at[8 + i])

    def finish_queries(t):
        query_sums(t)
        for i in range(t * 4, t * 4 + 4):
            dq_copy(i).start()

    own_chunk(1)
    own_chunk(0)
    owner_sum(0)
    finish_queries(1)
    owner_sum(1)
    finish_queries(0)

    mine = lax.broadcasted_iota(jnp.int32, (64, HD), 0) + (kv * 8 + grp) * 64 < plen
    for t in range(2):
        for d in range(4):
            cols = head_cols(kvat(4 - d), t)
            if d == 0:
                got_k, got_v = own[t, 0, my_rows, :], own[t, 1, my_rows, :]
            else:
                to_owner(t, d).wait_recv()
                got_k, got_v = fin[t, d, 0], fin[t, d, 1]
            dpk_ref[:, cols] = jnp.where(mine, got_k.astype(F32) * (weight * SCALE), 0.0)
            dpv_ref[:, cols] = jnp.where(mine, got_v.astype(F32) * weight, 0.0)

    for t in range(2):
        for c in spread(t) + [g(t) for g in gather] + [s(t) for s in sums] + [to_owner(t, d) for d in (1, 2, 3)]:
            c.wait_send()
    for c in [w_x] + w_z + w_y:
        c.wait_send()
    for i in range(8):
        o_copy(i).wait()
        dq_copy(i).wait()


def hand_over(*refs):
    ins, outs, held, (in_sem, out_sem) = refs[0:6], refs[6:12], refs[12:18], refs[18:]
    pieces = []
    for i in range(6):
        parts = 2 if i < 2 else 1
        rows = ins[i].shape[0] // parts
        for j in range(parts):
            pieces.append((i, pl.ds(j * rows, rows)))
    into = [
        pltpu.make_async_copy(ins[i].at[r], held[i].at[r], in_sem.at[n]) for n, (i, r) in enumerate(pieces)
    ]
    out = [
        pltpu.make_async_copy(held[i].at[r], outs[i].at[r], out_sem.at[n]) for n, (i, r) in enumerate(pieces)
    ]
    for c in into:
        c.start()
    for a, b in zip(into, out):
        a.wait()
        b.start()
    for c in out:
        c.wait()


def on_device(
    queries, resp_keys, resp_values, prompt_keys, prompt_values, grad_out, resp_len, prompt_len
):
    vm = pl.BlockSpec(memory_space=pltpu.VMEM)
    sm = pl.BlockSpec(memory_space=pltpu.SMEM)
    hbm = pl.BlockSpec(memory_space=pl.ANY)
    shape = jax.ShapeDtypeStruct
    dma = pltpu.SemaphoreType.DMA
    shapes = [
        shape((256, 2048), BF), shape((256, 2048), BF), shape((256, 256), BF), shape((256, 256), BF),
        shape((64, 1024), F32), shape((64, 1024), F32),
    ]
    outs = pl.pallas_call(
        kernel,
        out_shape=shapes,
        in_specs=[sm, sm] + [hbm] * 6,
        out_specs=[hbm, hbm] + [vm] * 4,
        scratch_shapes=[
            pltpu.VMEM((2, 8, 2, SET, HD), BF),
            pltpu.VMEM((HEADS, KEYS, SLOTS), BF),
            pltpu.VMEM((HEADS, KEYS, SLOTS), BF),
            pltpu.VMEM((HEADS, HD + 16, SLOTS), F32),
            pltpu.VMEM((8, SLOTS, 256), BF),
            pltpu.VMEM((5, HEADS, 1, SLOTS), F32),
            pltpu.VMEM((HEADS, 1, SLOTS), F32),
            pltpu.VMEM((HEADS, 1, SLOTS), F32),
            pltpu.VMEM((2, KEYS, HD), BF),
            pltpu.VMEM((2, HD, KEYS), BF),
            pltpu.VMEM((2, HD + 16, KEYS), BF),
            pltpu.VMEM((2, 2, SET, HD), BF),
            pltpu.VMEM((HEADS, HD, SLOTS), BF),
            pltpu.VMEM((HEADS, HD, SLOTS), BF),
            pltpu.VMEM((PC, SLOTS), F32),
            pltpu.VMEM((PC, SLOTS), F32),
            pltpu.VMEM((PC, SLOTS), BF),
            pltpu.VMEM((PC, SLOTS), BF),
            pltpu.VMEM((HD, SLOTS), BF),
            pltpu.VMEM((HD, SLOTS), BF),
            pltpu.VMEM((HD, PC), F32),
            pltpu.VMEM((HD, PC), F32),
            pltpu.VMEM((2, 8, 2, HD, SET), BF),
            pltpu.VMEM((2, 2, SET, HD), BF),
            pltpu.VMEM((2, 2, 2, HD, 128), BF),
            pltpu.VMEM((2, 2, 2, HD, SET), BF),
            pltpu.VMEM((2, 2, 2, HD, SET), BF),
            pltpu.VMEM((2, 2, HD, SET), BF),
            pltpu.VMEM((2, 2, HD, SET), BF),
            pltpu.VMEM((2, 4, 2, 64, HD), BF),
            pltpu.VMEM((3, 8, 128), F32),
            pltpu.VMEM((7, 8, 128), F32),
            dma((24,)), dma((2, 6)), dma((2, 6)), dma((2, 8)), dma((2, 8)), dma((2, 8)), dma((2, 8)),
            dma((2, 4)), dma((2, 4)), dma((7,)), dma((7,)),
        ],
        compiler_params=pltpu.CompilerParams(
            collective_id=0, has_side_effects=True, vmem_limit_bytes=62 * 2**20
        ),
        name="attention",
    )(
        resp_len, prompt_len, queries.reshape(256, 2048), grad_out.reshape(256, 2048),
        resp_keys.reshape(256, 256), resp_values.reshape(256, 256),
        prompt_keys.reshape(64, 1024), prompt_values.reshape(64, 1024),
    )
    attended, grad_q, grad_rk, grad_rv, grad_pk, grad_pv = pl.pallas_call(
        hand_over,
        out_shape=shapes,
        in_specs=[hbm] * 6,
        out_specs=[hbm] * 6,
        scratch_shapes=[pltpu.VMEM(a.shape, a.dtype) for a in shapes] + [dma((8,)), dma((8,))],
        name="hand_over",
    )(*outs)
    return (
        attended.reshape(queries.shape),
        grad_q.reshape(queries.shape),
        grad_rk.reshape(resp_keys.shape),
        grad_rv.reshape(resp_values.shape),
        grad_pk.reshape(1, 64, 1024),
        grad_pv.reshape(1, 64, 1024),
    )


def solution(mesh):
    wide = P("prompt", "grp", None, "kv")
    rows = P("prompt", ("kv", "grp"), None)
    return jax.shard_map(
        on_device,
        mesh=mesh,
        in_specs=(wide, wide, wide, rows, rows, wide, P("prompt", "grp"), P("prompt")),
        out_specs=(wide, wide, wide, wide, rows, rows),
        check_vma=False,
    )
```
